256 devices in a mesh: chan: 32 (over z, y), tm: 8 (over x, core).
Axes of the slice: x: 4, y: 4, z: 8, core: 2. Of those that a mesh axis runs over, the one named last changes fastest.
Arguments:
- intensity: bfloat16 [2, 16384, 4096], P(None, 'chan', 'tm'), may hold values from -6 to 6
- channel_scale: float32 [16384], P('chan'), may hold values from 0.5 to 2
- box_widths: int32 [6], replicated, may hold values from 1 to 64, as said below
Outputs:
- snr: float32 [2, 6, 2048, 4096], P(None, None, 'chan', 'tm')
The draws below stay inside these ranges and needn't reach their ends.
Inputs may be any that keep to these rules, and one draw needn't show every extreme that they name: `box_widths`: distinct and increasing; the first is 1 and the last is 2 ** 6.
All inputs are finite; a program needn't handle non-finite values.
Results may differ from the reference program's by a relative error of at most 0.0003.
Values may be sent and summed in bfloat16 or wider, within the bound.
No kernel may reach another device: no remote copies, remote signals or barrier semaphores. Data moves between devices by JAX's collectives and lax.ppermute only.
A program may use at most 64 MiB of HBM per device.

```python
import math
import jax
import jax.numpy as jnp
from jax import lax

BEAMS = 2
NCH = 16384
NDM = 2048
NBOX = 6
NT = 4096


def draw_box_widths(key, part):
    key = jax.random.fold_in(key, 7)
    places = jnp.arange(NBOX, dtype=jnp.int32)
    lowest = jnp.left_shift(jnp.ones((NBOX,), jnp.int32), places)
    picked = jax.random.randint(key, (NBOX,), lowest, 2 * lowest)
    return jnp.where(places == NBOX - 1, 2 * lowest, picked).astype(jnp.int32)


def level_of(rng, shape, cuts, smallest, high):
    factor_of = 1.0
    for dim, shards_of in cuts:
        steps = jax.random.uniform(jax.random.fold_in(jax.random.fold_in(rng, 6), dim), (shards_of,), jnp.float32, smallest / len(cuts), high / len(cuts))
        factor_of = factor_of * jnp.repeat(jnp.exp(steps), shape[dim] // shards_of).reshape((-1,) + (1,) * (len(shape) - 1 - dim))
    return factor_of


def noise(stream_key, extent, deviation, reach, pieces=(), kind=jnp.bfloat16):
    array = jax.random.normal(stream_key, extent, jnp.float32) * deviation
    if len(pieces) > 0:
        array = level_of(stream_key, extent, pieces, -0.22, 0.18) * array
    return jnp.clip(array, min=-reach, max=reach).astype(kind)


def setup_inputs(seed: int = 0) -> dict:
    key_of = jax.random.split(jax.random.key(seed), 4)
    intensity = noise(key_of[0], (BEAMS, NCH, NT), 1.0, 6.0, ((1, 32), (2, 8)))
    channel_scale = jnp.clip(jnp.exp(math.log(2.0) - 1.3862944 * jax.random.uniform(key_of[1], (NCH,), jnp.float32) ** level_of(key_of[1], (NCH,), ((0, 32),), -0.2, 0.2)), 0.5, 2.0)
    box_widths = draw_box_widths(jax.random.fold_in(key_of[3], 71), 0)
    return dict(intensity=intensity, channel_scale=channel_scale, box_widths=box_widths)


def skew_rows(plane):
    lead = plane.shape[:-2]
    rows = plane.shape[-2]
    span = plane.shape[-1]
    widths = [(0, 0)] * len(lead) + [(0, 0), (0, rows)]
    padded = jnp.pad(plane, widths)
    flat = padded.reshape(lead + (rows * (span + rows),))
    flat = flat[..., :rows * (span + rows - 1)]
    return flat.reshape(lead + (rows, span + rows - 1))[..., :span]

def delay_time(plane, amount, most):
    zeros = jnp.zeros(plane.shape[:-1] + (most,), plane.dtype)
    padded = jnp.concatenate([zeros, plane], axis=-1)
    start = most - jnp.minimum(amount, most)
    return lax.dynamic_slice_in_dim(padded, start, plane.shape[-1], axis=plane.ndim - 1)

def merge_pair(upper, lower, offset, most):
    early = delay_time(skew_rows(upper), offset, most)
    late = delay_time(early, 1, 1)
    joined = jnp.stack([lower + early, lower + late], axis=-2)
    return joined.reshape(lower.shape[:-2] + (2 * lower.shape[-2], lower.shape[-1]))

def reference(intensity, channel_scale, box_widths):
    beams, nch, ntime = intensity.shape
    scaled = intensity.astype(jnp.float32) * channel_scale[None, :, None]
    group = nch // NDM
    plane = scaled.reshape(beams, NDM, group, ntime).sum(axis=2)[:, :, None, :]
    while plane.shape[1] > 1:
        plane = merge_pair(plane[:, 0::2], plane[:, 1::2], 0, 0)
    dedispersed = plane[:, 0]
    most_width = 2 ** NBOX
    padded = jnp.pad(dedispersed, ((0, 0), (0, 0), (most_width, 0)))
    summed = jnp.cumsum(padded, axis=2)
    current = summed[:, :, most_width:]
    filtered = []
    for index in range(NBOX):
        width = box_widths[index]
        back = lax.dynamic_slice_in_dim(summed, (most_width - width).astype(jnp.int32), ntime, axis=2)
        norm = jnp.sqrt(width.astype(jnp.float32) * nch)
        filtered.append((current - back) / norm)
    return jnp.stack(filtered, axis=1)
```

```python
import jax
import jax.numpy as jnp
from jax import lax
from jax.experimental import pallas as pl
from jax.experimental.pallas import tpu as pltpu
from jax.sharding import PartitionSpec as P

BEAMS = 2
CHANS = 512
SPAN = 512
PARTS = 32
SEGMENTS = 8
ROWS = 64
WIDE = SPAN + 128
NBOX = 6
LANES = 128
REACH = 5


def split3(x):
    first = x.astype(jnp.bfloat16)
    rest = x - first.astype(jnp.float32)
    second = rest.astype(jnp.bfloat16)
    third = (rest - second.astype(jnp.float32)).astype(jnp.bfloat16)
    return first, second, third


def roll(x, shift):
    return x if isinstance(shift, int) and shift == 0 else pltpu.roll(x, shift, 1)


def merge_groups(groups):
    merged = []
    for upper, lower in zip(groups[0::2], groups[1::2]):
        trials = []
        for e in range(len(upper)):
            early = roll(upper[e], e)
            trials += [lower[e] + early, lower[e] + roll(early, 1)]
        merged.append(trials)
    return merged


def put(ref, start, stride, rows):
    for c in range(rows.shape[1] // LANES):
        ref[c, pl.ds(start, 8, stride=stride), :] = rows[:, c * LANES : (c + 1) * LANES]


def take(ref, start, count, first, last):
    chunks = [ref[c, pl.ds(start, count), :] for c in range(first, last)]
    return jnp.concatenate(chunks, axis=1)


def merge_rows(groups, one, two):
    tiles = WIDE // LANES
    while len(groups) > 1:
        groups = merge_groups(groups)
    for e in range(8):
        put(one, e, 8, groups[0][e])
    source, target = one, two
    trials = 8
    while trials < ROWS:
        for base in range(0, ROWS, 2 * trials):
            for a in range(0, trials, 8):
                upper = take(source, base + a, 8, 0, tiles)
                lower = take(source, base + trials + a, 8, 0, tiles)
                early = pltpu.roll(upper, a, 1, stride=1, stride_axis=0)
                late = pltpu.roll(early, 1, 1)
                put(target, base + 2 * a, 2, lower + early)
                put(target, base + 2 * a + 1, 2, lower + late)
        source, target = target, source
        trials *= 2
    return source


def local_kernel(q_ref, scale_ref, x_ref, o0, o1, o2, o3, o4, one, two, delayed):
    q = q_ref[0]
    row = lax.broadcasted_iota(jnp.int32, (ROWS, CHANS), 0)
    col = lax.broadcasted_iota(jnp.int32, (ROWS, CHANS), 1)
    member = (row & 7) * 8 + (row >> 3) == col >> 3
    weights = jnp.where(member, scale_ref[...], 0.0)
    x = x_ref[0]
    base = None
    for part in split3(weights):
        term = jnp.dot(part, x, preferred_element_type=jnp.float32)
        base = term if base is None else base + term
    blank = jnp.zeros((8, LANES), jnp.float32)
    groups = [
        [jnp.concatenate([base[8 * g : 8 * g + 8], blank], axis=1)] for g in range(8)
    ]
    plane = merge_rows(groups, one, two)
    delayed[...] = jnp.zeros_like(delayed)
    extent = WIDE + 2 * LANES
    pair = lax.broadcasted_iota(jnp.int32, (8, extent), 0) >> 1
    more = jnp.zeros((8, 2 * LANES), jnp.float32)
    for a in range(8):
        rows = jnp.concatenate(
            [take(plane, 8 * a, 8, 0, WIDE // LANES), more], axis=1
        )
        rows = jnp.where(pair & 1 != 0, pltpu.roll(rows, 2 * q, 1), rows)
        rows = jnp.where(pair & 2 != 0, pltpu.roll(rows, 4 * q, 1), rows)
        delay = 8 * q * a
        rows = pltpu.roll(rows, delay & (LANES - 1), 1)
        start = pl.multiple_of(delay - (delay & (LANES - 1)), LANES)
        delayed[pl.ds(8 * a, 8), pl.ds(start, extent)] = rows
    for k, out in enumerate((o0, o1, o2, o3, o4)):
        first = 16 * max(k - 1, 0)
        out[0] = delayed[pl.ds(first, ROWS - first), pl.ds(SPAN * k, SPAN)]


def local_plane(x, scale, q):
    counts = [ROWS - 16 * max(k - 1, 0) for k in range(REACH)]
    return pl.pallas_call(
        local_kernel,
        grid=(BEAMS,),
        in_specs=[
            pl.BlockSpec(memory_space=pltpu.SMEM),
            pl.BlockSpec((1, CHANS), lambda b: (0, 0)),
            pl.BlockSpec((1, CHANS, SPAN), lambda b: (b, 0, 0)),
        ],
        out_specs=[pl.BlockSpec((1, n, SPAN), lambda b: (b, 0, 0)) for n in counts],
        out_shape=[
            jax.ShapeDtypeStruct((BEAMS, n, SPAN), jnp.float32) for n in counts
        ],
        scratch_shapes=[
            pltpu.VMEM((WIDE // LANES, ROWS, LANES), jnp.float32),
            pltpu.VMEM((WIDE // LANES, ROWS, LANES), jnp.float32),
            pltpu.VMEM((ROWS, REACH * SPAN), jnp.float32),
        ],
        compiler_params=pltpu.CompilerParams(vmem_limit_bytes=24 << 20),
        name="local_plane",
    )(q, scale, x)


def gather_kernel(o0, r1, r2, r3, r4, out, held):
    for b in range(BEAMS):
        for a in range(0, ROWS, 16):
            total = o0[b, pl.ds(a, 16), :] + r1[b, pl.ds(a, 16), :]
            for k, received in ((2, r2), (3, r3), (4, r4)):
                first = 16 * (k - 1)
                if a >= first:
                    total = total + received[b, pl.ds(a - first, 16), :]
            for c in range(SPAN // LANES):
                held[c, pl.ds(a, 16), :] = total[:, c * LANES : (c + 1) * LANES]
        for c in range(SPAN // LANES):
            for i in range(2):
                out[pl.ds(b * 8 + c * 2 + i, PARTS, stride=16), :] = held[
                    c, pl.ds(i, PARTS, stride=2), :
                ]


def gather_shifted(pieces):
    return pl.pallas_call(
        gather_kernel,
        out_shape=jax.ShapeDtypeStruct((PARTS * 16, LANES), jnp.float32),
        scratch_shapes=[pltpu.VMEM((SPAN // LANES, ROWS, LANES), jnp.float32)],
        compiler_params=pltpu.CompilerParams(vmem_limit_bytes=24 << 20),
        name="gather_shifted",
    )(*pieces)


def final_kernel(x_ref, main, tail, one, two):
    blank = jnp.zeros((8, LANES), jnp.float32)
    lane = lax.broadcasted_iota(jnp.int32, (ROWS, LANES), 1)
    for b in range(BEAMS):
        groups = []
        for g in range(4):
            trials = []
            for e in range(2):
                chunks = [
                    x_ref[pl.ds(g * 16 + b * 8 + c * 2 + e, 8, stride=64), :]
                    for c in range(SPAN // LANES)
                ]
                trials.append(jnp.concatenate(chunks + [blank], axis=1))
            groups.append(trials)
        plane = merge_rows(groups, one, two)
        main[b] = take(plane, 0, ROWS, 0, SPAN // LANES)
        tail[b] = jnp.where(
            lane < LANES // 2,
            plane[SPAN // LANES],
            plane[SPAN // LANES - 1],
        )


def final_plane(x):
    return pl.pallas_call(
        final_kernel,
        out_shape=[
            jax.ShapeDtypeStruct((BEAMS, ROWS, SPAN), jnp.float32),
            jax.ShapeDtypeStruct((BEAMS, ROWS, LANES), jnp.float32),
        ],
        scratch_shapes=[
            pltpu.VMEM((WIDE // LANES, ROWS, LANES), jnp.float32),
            pltpu.VMEM((WIDE // LANES, ROWS, LANES), jnp.float32),
        ],
        compiler_params=pltpu.CompilerParams(vmem_limit_bytes=24 << 20),
        name="final_plane",
    )(x)


def boxcar_kernel(widths, main, tail, out, bands):
    @pl.when(pl.program_id(0) == 0)
    def _():
        u = lax.broadcasted_iota(jnp.int32, (2 * LANES, LANES), 0)
        t = lax.broadcasted_iota(jnp.int32, (2 * LANES, LANES), 1)
        ago = t + LANES - u
        for k in range(NBOX):
            inside = jnp.logical_and(ago >= 0, ago < widths[k])
            bands[:, pl.ds(k * LANES, LANES)] = jnp.where(inside, 1.0, 0.0).astype(
                jnp.bfloat16
            )

    lane = lax.broadcasted_iota(jnp.int32, (ROWS, LANES), 1)
    edge = tail[0]
    chunks = [jnp.where(lane >= LANES // 2, edge, 0.0)]
    for c in range(SPAN // LANES):
        chunks.append(main[0, :, pl.ds(c * LANES, LANES)])
    chunks[1] = chunks[1] + jnp.where(lane < LANES // 2, edge, 0.0)
    parts = [split3(chunk) for chunk in chunks]
    norms = [
        lax.rsqrt(
            jnp.full((ROWS, LANES), widths[k] * (CHANS * PARTS), jnp.int32).astype(
                jnp.float32
            )
        )
        for k in range(NBOX)
    ]
    for c in range(SPAN // LANES):
        total = None
        for before, here in zip(parts[c], parts[c + 1]):
            window = jnp.concatenate([before, here], axis=1)
            term = jnp.dot(window, bands[...], preferred_element_type=jnp.float32)
            total = term if total is None else total + term
        for k in range(NBOX):
            out[0, k, :, pl.ds(c * LANES, LANES)] = (
                total[:, k * LANES : (k + 1) * LANES] * norms[k]
            )


def boxcars(main, tail, widths):
    return pl.pallas_call(
        boxcar_kernel,
        grid=(BEAMS,),
        in_specs=[
            pl.BlockSpec(memory_space=pltpu.SMEM),
            pl.BlockSpec((1, ROWS, SPAN), lambda b: (b, 0, 0)),
            pl.BlockSpec((1, ROWS, LANES), lambda b: (b, 0, 0)),
        ],
        out_specs=pl.BlockSpec((1, NBOX, ROWS, SPAN), lambda b: (b, 0, 0, 0)),
        out_shape=jax.ShapeDtypeStruct((BEAMS, NBOX, ROWS, SPAN), jnp.float32),
        scratch_shapes=[pltpu.VMEM((2 * LANES, NBOX * LANES), jnp.bfloat16)],
        compiler_params=pltpu.CompilerParams(vmem_limit_bytes=24 << 20),
        name="boxcars",
    )(widths, main, tail)


def later(block, distance):
    route = [(i, i + distance) for i in range(SEGMENTS - distance)]
    return lax.ppermute(block, "tm", route)


def per_device(intensity, channel_scale, box_widths):
    q = (PARTS - 1 - lax.axis_index("chan")).astype(jnp.int32).reshape(1)
    pieces = list(local_plane(intensity, channel_scale.reshape(1, CHANS), q))
    for k in range(REACH - 1, 0, -1):
        pieces[k] = later(pieces[k], k)
    lined = gather_shifted(pieces)
    lined = lax.all_to_all(lined, "chan", 0, 0, tiled=True)
    main, tail = final_plane(lined)
    return boxcars(main, later(tail, 1), box_widths)


def solution(mesh):
    in_specs = (P(None, "chan", "tm"), P("chan"), P())
    out_specs = P(None, None, "chan", "tm")
    return jax.shard_map(
        per_device, mesh=mesh, in_specs=in_specs, out_specs=out_specs, check_vma=False
    )
```

```python
import jax
import jax.numpy as jnp
from jax import lax
from jax.experimental import pallas as pl
from jax.experimental.pallas import tpu as pltpu
from jax.sharding import PartitionSpec as P

BEAMS = 2
CHANS = 512
SPAN = 512
PARTS = 32
SEGMENTS = 8
ROWS = 64
WIDE = SPAN + 128
NBOX = 6
LANES = 128
REACH = 5


def split(x):
    first = x.astype(jnp.bfloat16)
    second = (x - first.astype(jnp.float32)).astype(jnp.bfloat16)
    return first, second


def roll(x, shift):
    return x if isinstance(shift, int) and shift == 0 else pltpu.roll(x, shift, 1)


def merge_groups(groups):
    merged = []
    for upper, lower in zip(groups[0::2], groups[1::2]):
        trials = []
        for e in range(len(upper)):
            early = roll(upper[e], e)
            trials += [lower[e] + early, lower[e] + roll(early, 1)]
        merged.append(trials)
    return merged


def put(ref, start, stride, rows):
    for c in range(rows.shape[1] // LANES):
        ref[c, pl.ds(start, 8, stride=stride), :] = rows[:, c * LANES : (c + 1) * LANES]


def take(ref, start, count, first, last):
    chunks = [ref[c, pl.ds(start, count), :] for c in range(first, last)]
    return jnp.concatenate(chunks, axis=1)


def merge_rows(groups, one, two):
    tiles = WIDE // LANES
    while len(groups) > 1:
        groups = merge_groups(groups)
    for e in range(8):
        put(one, e, 8, groups[0][e])
    source, target = one, two
    trials = 8
    while trials < ROWS:
        for base in range(0, ROWS, 2 * trials):
            for a in range(0, trials, 8):
                upper = take(source, base + a, 8, 0, tiles)
                lower = take(source, base + trials + a, 8, 0, tiles)
                early = pltpu.roll(upper, a, 1, stride=1, stride_axis=0)
                late = pltpu.roll(early, 1, 1)
                put(target, base + 2 * a, 2, lower + early)
                put(target, base + 2 * a + 1, 2, lower + late)
        source, target = target, source
        trials *= 2
    return source


def local_kernel(
    q_ref, scale_hbm, x_hbm, o0, o1, o2, o3, o4, scale, x, one, two, delayed, sems
):
    half = CHANS // 2
    fetch_scale = pltpu.make_async_copy(scale_hbm, scale, sems.at[2 * BEAMS])
    fetch_scale.start()
    fetches = []
    for b in range(BEAMS):
        for h in range(2):
            piece = pl.ds(h * half, half)
            fetches.append(
                pltpu.make_async_copy(
                    x_hbm.at[b, piece], x.at[b, piece], sems.at[2 * b + h]
                )
            )
            fetches[-1].start()
    q = q_ref[0]
    row = lax.broadcasted_iota(jnp.int32, (ROWS, CHANS), 0)
    col = lax.broadcasted_iota(jnp.int32, (ROWS, CHANS), 1)
    member = (row & 7) * 8 + (row >> 3) == col >> 3
    fetch_scale.wait()
    weights = jnp.where(member, scale[...], 0.0)
    weights = jnp.concatenate(split(weights), axis=0)
    blank = jnp.zeros((8, LANES), jnp.float32)
    extent = WIDE + 2 * LANES
    pair = lax.broadcasted_iota(jnp.int32, (8, extent), 0) >> 1
    more = jnp.zeros((8, 2 * LANES), jnp.float32)
    delayed[...] = jnp.zeros_like(delayed)
    for b in range(BEAMS):
        fetches[2 * b].wait()
        fetches[2 * b + 1].wait()
        base = jnp.dot(weights, x[b], preferred_element_type=jnp.float32)
        base = base[:ROWS] + base[ROWS:]
        groups = [
            [jnp.concatenate([base[8 * g : 8 * g + 8], blank], axis=1)]
            for g in range(8)
        ]
        plane = merge_rows(groups, one, two)
        for a in range(8):
            rows = jnp.concatenate(
                [take(plane, 8 * a, 8, 0, WIDE // LANES), more], axis=1
            )
            rows = jnp.where(pair & 1 != 0, pltpu.roll(rows, 2 * q, 1), rows)
            rows = jnp.where(pair & 2 != 0, pltpu.roll(rows, 4 * q, 1), rows)
            delay = 8 * q * a
            rows = pltpu.roll(rows, delay & (LANES - 1), 1)
            start = pl.multiple_of(delay - (delay & (LANES - 1)), LANES)
            delayed[b, pl.ds(8 * a, 8), pl.ds(start, extent)] = rows
        for k, out in enumerate((o0, o1, o2, o3, o4)):
            first = 16 * max(k - 1, 0)
            out[b] = delayed[b, pl.ds(first, ROWS - first), pl.ds(SPAN * k, SPAN)]


def local_plane(x, scale, q):
    counts = [ROWS - 16 * max(k - 1, 0) for k in range(REACH)]
    return pl.pallas_call(
        local_kernel,
        in_specs=[
            pl.BlockSpec(memory_space=pltpu.SMEM),
            pl.BlockSpec(memory_space=pltpu.HBM),
            pl.BlockSpec(memory_space=pltpu.HBM),
        ],
        out_shape=[
            jax.ShapeDtypeStruct((BEAMS, n, SPAN), jnp.float32) for n in counts
        ],
        scratch_shapes=[
            pltpu.VMEM((1, CHANS), jnp.float32),
            pltpu.VMEM((BEAMS, CHANS, SPAN), jnp.bfloat16),
            pltpu.VMEM((WIDE // LANES, ROWS, LANES), jnp.float32),
            pltpu.VMEM((WIDE // LANES, ROWS, LANES), jnp.float32),
            pltpu.VMEM((BEAMS, ROWS, REACH * SPAN), jnp.float32),
            pltpu.SemaphoreType.DMA((2 * BEAMS + 1,)),
        ],
        compiler_params=pltpu.CompilerParams(vmem_limit_bytes=24 << 20),
        name="local_plane",
    )(
        q,
        pltpu.with_memory_space_constraint(scale, pltpu.HBM),
        pltpu.with_memory_space_constraint(x, pltpu.HBM),
    )


def gather_kernel(o0, r1, r2, r3, r4, out, held):
    for b in range(BEAMS):
        for a in range(0, ROWS, 16):
            total = o0[b, pl.ds(a, 16), :] + r1[b, pl.ds(a, 16), :]
            for k, received in ((2, r2), (3, r3), (4, r4)):
                first = 16 * (k - 1)
                if a >= first:
                    total = total + received[b, pl.ds(a - first, 16), :]
            for c in range(SPAN // LANES):
                held[c, pl.ds(a, 16), :] = total[:, c * LANES : (c + 1) * LANES]
        for c in range(SPAN // LANES):
            for i in range(2):
                out[pl.ds(b * 8 + c * 2 + i, PARTS, stride=16), :] = held[
                    c, pl.ds(i, PARTS, stride=2), :
                ]


def gather_shifted(pieces):
    return pl.pallas_call(
        gather_kernel,
        out_shape=jax.ShapeDtypeStruct((PARTS * 16, LANES), jnp.float32),
        scratch_shapes=[pltpu.VMEM((SPAN // LANES, ROWS, LANES), jnp.float32)],
        compiler_params=pltpu.CompilerParams(vmem_limit_bytes=24 << 20),
        name="gather_shifted",
    )(*pieces)


def final_kernel(x_ref, main, tail, one, two):
    blank = jnp.zeros((8, LANES), jnp.float32)
    lane = lax.broadcasted_iota(jnp.int32, (ROWS, LANES), 1)
    for b in range(BEAMS):
        groups = []
        for g in range(4):
            trials = []
            for e in range(2):
                chunks = [
                    x_ref[pl.ds(g * 16 + b * 8 + c * 2 + e, 8, stride=64), :]
                    for c in range(SPAN // LANES)
                ]
                trials.append(jnp.concatenate(chunks + [blank], axis=1))
            groups.append(trials)
        plane = merge_rows(groups, one, two)
        main[b] = take(plane, 0, ROWS, 0, SPAN // LANES)
        tail[b] = jnp.where(
            lane < LANES // 2,
            plane[SPAN // LANES],
            plane[SPAN // LANES - 1],
        )


def final_plane(x):
    return pl.pallas_call(
        final_kernel,
        out_shape=[
            jax.ShapeDtypeStruct((BEAMS, ROWS, SPAN), jnp.float32),
            jax.ShapeDtypeStruct((BEAMS, ROWS, LANES), jnp.float32),
        ],
        scratch_shapes=[
            pltpu.VMEM((WIDE // LANES, ROWS, LANES), jnp.float32),
            pltpu.VMEM((WIDE // LANES, ROWS, LANES), jnp.float32),
        ],
        compiler_params=pltpu.CompilerParams(vmem_limit_bytes=24 << 20),
        name="final_plane",
    )(x)


def boxcar_bands(widths):
    u = lax.broadcasted_iota(jnp.int32, (2 * LANES, LANES), 0)
    t = lax.broadcasted_iota(jnp.int32, (2 * LANES, LANES), 1)
    ago = t + LANES - u
    bands = []
    for k in range(NBOX):
        inside = jnp.logical_and(ago >= 0, ago < widths[k])
        bands.append(jnp.where(inside, 1.0, 0.0).astype(jnp.bfloat16))
    return jnp.concatenate(bands, axis=1)


def boxcar_norms(widths):
    norms = []
    for k in range(NBOX):
        square = jnp.full((1, LANES), widths[k] * (CHANS * PARTS), jnp.int32)
        norms.append(lax.rsqrt(square.astype(jnp.float32)))
    return jnp.concatenate(norms, axis=1)


def boxcar_tile(before, here, bands, norms, held, c):
    window = jnp.concatenate([before, here], axis=1)
    sums = jnp.dot(window, bands, preferred_element_type=jnp.float32)
    rows = BEAMS * ROWS
    sums = (sums[:rows] + sums[rows:]) * norms
    for b in range(BEAMS):
        for k in range(NBOX):
            held[b, k, :, pl.ds(c * LANES, LANES)] = sums[
                b * ROWS : (b + 1) * ROWS, k * LANES : (k + 1) * LANES
            ]


def later_kernel(widths, main, out, held, sems):
    bands = boxcar_bands(widths)
    norms = boxcar_norms(widths)
    parts = []
    for c in range(SPAN // LANES):
        tile = main[:, :, pl.ds(c * LANES, LANES)].reshape(BEAMS * ROWS, LANES)
        parts.append(jnp.concatenate(split(tile), axis=0))
    copies = []
    for c in range(1, SPAN // LANES):
        boxcar_tile(parts[c - 1], parts[c], bands, norms, held, c - 1)
        copies.append(
            pltpu.make_async_copy(
                held.at[:, :, :, pl.ds((c - 1) * LANES, LANES)],
                out.at[:, :, :, pl.ds(c * LANES, LANES)],
                sems.at[c - 1],
            )
        )
        copies[-1].start()
    for copy in copies:
        copy.wait()


def first_kernel(widths, main, tail, rest, out, held, sem):
    del rest
    lane = lax.broadcasted_iota(jnp.int32, (BEAMS * ROWS, LANES), 1)
    edge = tail[...].reshape(BEAMS * ROWS, LANES)
    before = jnp.where(lane >= LANES // 2, edge, 0.0)
    here = main[:, :, pl.ds(0, LANES)].reshape(BEAMS * ROWS, LANES)
    here = here + jnp.where(lane < LANES // 2, edge, 0.0)
    before = jnp.concatenate(split(before), axis=0)
    here = jnp.concatenate(split(here), axis=0)
    boxcar_tile(before, here, boxcar_bands(widths), boxcar_norms(widths), held, 0)
    copy = pltpu.make_async_copy(held, out.at[:, :, :, pl.ds(0, LANES)], sem)
    copy.start()
    copy.wait()


OUT = jax.ShapeDtypeStruct((BEAMS, NBOX, ROWS, SPAN), jnp.float32)


def boxcars_later(main, widths):
    lanes = SPAN - LANES
    return pl.pallas_call(
        later_kernel,
        in_specs=[
            pl.BlockSpec(memory_space=pltpu.SMEM),
            pl.BlockSpec(memory_space=pltpu.VMEM),
        ],
        out_specs=pl.BlockSpec(memory_space=pltpu.HBM),
        out_shape=OUT,
        scratch_shapes=[
            pltpu.VMEM((BEAMS, NBOX, ROWS, lanes), jnp.float32),
            pltpu.SemaphoreType.DMA((lanes // LANES,)),
        ],
        compiler_params=pltpu.CompilerParams(vmem_limit_bytes=24 << 20),
        cost_estimate=pl.CostEstimate(
            flops=2 * 256 * 256 * 768 * 3, bytes_accessed=2 << 20, transcendentals=0
        ),
        name="boxcars_later",
    )(widths, main)


def boxcars_first(main, tail, rest, widths):
    return pl.pallas_call(
        first_kernel,
        in_specs=[
            pl.BlockSpec(memory_space=pltpu.SMEM),
            pl.BlockSpec(memory_space=pltpu.VMEM),
            pl.BlockSpec(memory_space=pltpu.VMEM),
            pl.BlockSpec(memory_space=pltpu.HBM),
        ],
        out_specs=pl.BlockSpec(memory_space=pltpu.HBM),
        out_shape=OUT,
        input_output_aliases={3: 0},
        scratch_shapes=[
            pltpu.VMEM((BEAMS, NBOX, ROWS, LANES), jnp.float32),
            pltpu.SemaphoreType.DMA,
        ],
        compiler_params=pltpu.CompilerParams(vmem_limit_bytes=24 << 20),
        name="boxcars_first",
    )(widths, main, tail, rest)


def later(block, distance):
    route = [(i, i + distance) for i in range(SEGMENTS - distance)]
    return lax.ppermute(block, "tm", route)


def per_device(intensity, channel_scale, box_widths):
    q = (PARTS - 1 - lax.axis_index("chan")).astype(jnp.int32).reshape(1)
    pieces = list(local_plane(intensity, channel_scale.reshape(1, CHANS), q))
    for k in range(REACH - 1, 0, -1):
        pieces[k] = later(pieces[k], k)
    lined = gather_shifted(pieces)
    lined = lax.all_to_all(lined, "chan", 0, 0, tiled=True)
    main, tail = final_plane(lined)
    tail = later(tail, 1)
    rest = boxcars_later(main, box_widths)
    return boxcars_first(main, tail, rest, box_widths)


def solution(mesh):
    in_specs = (P(None, "chan", "tm"), P("chan"), P())
    out_specs = P(None, None, "chan", "tm")
    return jax.shard_map(
        per_device, mesh=mesh, in_specs=in_specs, out_specs=out_specs, check_vma=False
    )
```

```python
import jax
import jax.numpy as jnp
from jax import lax
from jax.experimental import pallas as pl
from jax.experimental.pallas import tpu as pltpu
from jax.sharding import PartitionSpec as P

BEAMS = 2
CHANS = 512
SPAN = 512
PARTS = 32
SEGMENTS = 8
ROWS = 64
WIDE = SPAN + 128
NBOX = 6
LANES = 128
REACH = 5


def split(x):
    first = x.astype(jnp.bfloat16)
    second = (x - first.astype(jnp.float32)).astype(jnp.bfloat16)
    return first, second


def roll(x, shift):
    return x if isinstance(shift, int) and shift == 0 else pltpu.roll(x, shift, 1)


def merge_groups(groups):
    merged = []
    for upper, lower in zip(groups[0::2], groups[1::2]):
        trials = []
        for e in range(len(upper)):
            early = roll(upper[e], e)
            trials += [lower[e] + early, lower[e] + roll(early, 1)]
        merged.append(trials)
    return merged


def put(ref, start, stride, rows):
    for c in range(rows.shape[1] // LANES):
        ref[c, pl.ds(start, 8, stride=stride), :] = rows[:, c * LANES : (c + 1) * LANES]


def take(ref, start, count, first, last):
    chunks = [ref[c, pl.ds(start, count), :] for c in range(first, last)]
    return jnp.concatenate(chunks, axis=1)


def merge_rows(groups, one, two):
    tiles = WIDE // LANES
    while len(groups) > 1:
        groups = merge_groups(groups)
    for e in range(8):
        put(one, e, 8, groups[0][e])
    source, target = one, two
    trials = 8
    while trials < ROWS:
        for base in range(0, ROWS, 2 * trials):
            for a in range(0, trials, 8):
                upper = take(source, base + a, 8, 0, tiles)
                lower = take(source, base + trials + a, 8, 0, tiles)
                early = pltpu.roll(upper, a, 1, stride=1, stride_axis=0)
                late = pltpu.roll(early, 1, 1)
                put(target, base + 2 * a, 2, lower + early)
                put(target, base + 2 * a + 1, 2, lower + late)
        source, target = target, source
        trials *= 2
    return source


def local_kernel(
    q_ref, scale_hbm, x_hbm, o0, o1, o2, o3, o4, scale, x, one, two, delayed, sems
):
    half = CHANS // 2
    fetch_scale = pltpu.make_async_copy(scale_hbm, scale, sems.at[2 * BEAMS])
    fetch_scale.start()
    fetches = []
    for b in range(BEAMS):
        for h in range(2):
            piece = pl.ds(h * half, half)
            fetches.append(
                pltpu.make_async_copy(
                    x_hbm.at[b, piece], x.at[b, piece], sems.at[2 * b + h]
                )
            )
            fetches[-1].start()
    q = q_ref[0]
    row = lax.broadcasted_iota(jnp.int32, (ROWS, CHANS), 0)
    col = lax.broadcasted_iota(jnp.int32, (ROWS, CHANS), 1)
    member = (row & 7) * 8 + (row >> 3) == col >> 3
    fetch_scale.wait()
    weights = jnp.where(member, scale[...], 0.0)
    weights = jnp.concatenate(split(weights), axis=0)
    blank = jnp.zeros((8, LANES), jnp.float32)
    extent = WIDE + 2 * LANES
    pair = lax.broadcasted_iota(jnp.int32, (8, extent), 0) >> 1
    more = jnp.zeros((8, 2 * LANES), jnp.float32)
    delayed[...] = jnp.zeros_like(delayed)
    for b in range(BEAMS):
        fetches[2 * b].wait()
        fetches[2 * b + 1].wait()
        base = jnp.dot(weights, x[b], preferred_element_type=jnp.float32)
        base = base[:ROWS] + base[ROWS:]
        groups = [
            [jnp.concatenate([base[8 * g : 8 * g + 8], blank], axis=1)]
            for g in range(8)
        ]
        plane = merge_rows(groups, one, two)
        for a in range(8):
            rows = jnp.concatenate(
                [take(plane, 8 * a, 8, 0, WIDE // LANES), more], axis=1
            )
            rows = jnp.where(pair & 1 != 0, pltpu.roll(rows, 2 * q, 1), rows)
            rows = jnp.where(pair & 2 != 0, pltpu.roll(rows, 4 * q, 1), rows)
            delay = 8 * q * a
            rows = pltpu.roll(rows, delay & (LANES - 1), 1)
            start = pl.multiple_of(delay - (delay & (LANES - 1)), LANES)
            delayed[b, pl.ds(8 * a, 8), pl.ds(start, extent)] = rows
        for k, out in enumerate((o0, o1, o2, o3, o4)):
            first = 16 * max(k - 1, 0)
            out[b] = delayed[b, pl.ds(first, ROWS - first), pl.ds(SPAN * k, SPAN)]


def local_plane(x, scale, q):
    counts = [ROWS - 16 * max(k - 1, 0) for k in range(REACH)]
    return pl.pallas_call(
        local_kernel,
        in_specs=[
            pl.BlockSpec(memory_space=pltpu.SMEM),
            pl.BlockSpec(memory_space=pltpu.HBM),
            pl.BlockSpec(memory_space=pltpu.HBM),
        ],
        out_shape=[
            jax.ShapeDtypeStruct((BEAMS, n, SPAN), jnp.float32) for n in counts
        ],
        scratch_shapes=[
            pltpu.VMEM((1, CHANS), jnp.float32),
            pltpu.VMEM((BEAMS, CHANS, SPAN), jnp.bfloat16),
            pltpu.VMEM((WIDE // LANES, ROWS, LANES), jnp.float32),
            pltpu.VMEM((WIDE // LANES, ROWS, LANES), jnp.float32),
            pltpu.VMEM((BEAMS, ROWS, REACH * SPAN), jnp.float32),
            pltpu.SemaphoreType.DMA((2 * BEAMS + 1,)),
        ],
        compiler_params=pltpu.CompilerParams(vmem_limit_bytes=24 << 20),
        name="local_plane",
    )(
        q,
        pltpu.with_memory_space_constraint(scale, pltpu.HBM),
        pltpu.with_memory_space_constraint(x, pltpu.HBM),
    )


def gather_kernel(o0, r1, r2, r3, r4, out, held):
    for b in range(BEAMS):
        for a in range(0, ROWS, 16):
            total = o0[b, pl.ds(a, 16), :] + r1[b, pl.ds(a, 16), :]
            for k, received in ((2, r2), (3, r3), (4, r4)):
                first = 16 * (k - 1)
                if a >= first:
                    total = total + received[b, pl.ds(a - first, 16), :]
            for c in range(SPAN // LANES):
                held[c, pl.ds(a, 16), :] = total[:, c * LANES : (c + 1) * LANES]
        for c in range(SPAN // LANES):
            for i in range(2):
                out[pl.ds(b * 8 + c * 2 + i, PARTS, stride=16), :] = held[
                    c, pl.ds(i, PARTS, stride=2), :
                ]


def gather_shifted(pieces):
    return pl.pallas_call(
        gather_kernel,
        out_shape=jax.ShapeDtypeStruct((PARTS * 16, LANES), jnp.float32),
        scratch_shapes=[pltpu.VMEM((SPAN // LANES, ROWS, LANES), jnp.float32)],
        compiler_params=pltpu.CompilerParams(vmem_limit_bytes=24 << 20),
        name="gather_shifted",
    )(*pieces)


def final_kernel(x_ref, main, tail, one, two):
    blank = jnp.zeros((8, LANES), jnp.float32)
    lane = lax.broadcasted_iota(jnp.int32, (ROWS, LANES), 1)
    for b in range(BEAMS):
        groups = []
        for g in range(4):
            trials = []
            for e in range(2):
                chunks = [
                    x_ref[pl.ds(g * 16 + b * 8 + c * 2 + e, 8, stride=64), :]
                    for c in range(SPAN // LANES)
                ]
                trials.append(jnp.concatenate(chunks + [blank], axis=1))
            groups.append(trials)
        plane = merge_rows(groups, one, two)
        main[b] = take(plane, 0, ROWS, 0, SPAN // LANES)
        tail[b] = jnp.where(
            lane < LANES // 2,
            plane[SPAN // LANES],
            plane[SPAN // LANES - 1],
        )


def final_plane(x):
    return pl.pallas_call(
        final_kernel,
        out_shape=[
            jax.ShapeDtypeStruct((BEAMS, ROWS, SPAN), jnp.float32),
            jax.ShapeDtypeStruct((BEAMS, ROWS, LANES), jnp.float32),
        ],
        scratch_shapes=[
            pltpu.VMEM((WIDE // LANES, ROWS, LANES), jnp.float32),
            pltpu.VMEM((WIDE // LANES, ROWS, LANES), jnp.float32),
        ],
        compiler_params=pltpu.CompilerParams(vmem_limit_bytes=24 << 20),
        name="final_plane",
    )(x)


def boxcar_bands(widths):
    u = lax.broadcasted_iota(jnp.int32, (2 * LANES, LANES), 0)
    t = lax.broadcasted_iota(jnp.int32, (2 * LANES, LANES), 1)
    ago = t + LANES - u
    bands = []
    for k in range(NBOX):
        inside = jnp.logical_and(ago >= 0, ago < widths[k])
        bands.append(jnp.where(inside, 1.0, 0.0).astype(jnp.bfloat16))
    return jnp.concatenate(bands, axis=1)


def boxcar_norms(widths):
    norms = []
    for k in range(NBOX):
        square = jnp.full((1, LANES), widths[k] * (CHANS * PARTS), jnp.int32)
        norms.append(lax.rsqrt(square.astype(jnp.float32)))
    return jnp.concatenate(norms, axis=1)


def boxcar_tile(before, here, bands, norms, held, c):
    window = jnp.concatenate([before, here], axis=1)
    sums = jnp.dot(window, bands, preferred_element_type=jnp.float32)
    rows = BEAMS * ROWS
    sums = (sums[:rows] + sums[rows:]) * norms
    for b in range(BEAMS):
        for k in range(NBOX):
            held[b, k, :, pl.ds(c * LANES, LANES)] = sums[
                b * ROWS : (b + 1) * ROWS, k * LANES : (k + 1) * LANES
            ]


def later_kernel(widths, main, out, held, sems):
    bands = boxcar_bands(widths)
    norms = boxcar_norms(widths)
    parts = []
    for c in range(SPAN // LANES):
        tile = main[:, :, pl.ds(c * LANES, LANES)].reshape(BEAMS * ROWS, LANES)
        parts.append(jnp.concatenate(split(tile), axis=0))
    copies = []
    for c in range(1, SPAN // LANES):
        boxcar_tile(parts[c - 1], parts[c], bands, norms, held, c - 1)
        copies.append(
            pltpu.make_async_copy(
                held.at[:, :, :, pl.ds((c - 1) * LANES, LANES)],
                out.at[:, :, :, pl.ds(c * LANES, LANES)],
                sems.at[c - 1],
            )
        )
        copies[-1].start()
    for copy in copies:
        copy.wait()


def first_kernel(widths, main, tail, rest, out, held, sem):
    del rest
    lane = lax.broadcasted_iota(jnp.int32, (BEAMS * ROWS, LANES), 1)
    edge = tail[...].reshape(BEAMS * ROWS, LANES)
    before = jnp.where(lane >= LANES // 2, edge, 0.0)
    here = main[:, :, pl.ds(0, LANES)].reshape(BEAMS * ROWS, LANES)
    here = here + jnp.where(lane < LANES // 2, edge, 0.0)
    before = jnp.concatenate(split(before), axis=0)
    here = jnp.concatenate(split(here), axis=0)
    boxcar_tile(before, here, boxcar_bands(widths), boxcar_norms(widths), held, 0)
    copy = pltpu.make_async_copy(held, out.at[:, :, :, pl.ds(0, LANES)], sem)
    copy.start()
    copy.wait()


OUT = jax.ShapeDtypeStruct((BEAMS, NBOX, ROWS, SPAN), jnp.float32)


def boxcars_later(main, widths):
    lanes = SPAN - LANES
    return pl.pallas_call(
        later_kernel,
        in_specs=[
            pl.BlockSpec(memory_space=pltpu.SMEM),
            pl.BlockSpec(memory_space=pltpu.VMEM),
        ],
        out_specs=pl.BlockSpec(memory_space=pltpu.HBM),
        out_shape=OUT,
        scratch_shapes=[
            pltpu.VMEM((BEAMS, NBOX, ROWS, lanes), jnp.float32),
            pltpu.SemaphoreType.DMA((lanes // LANES,)),
        ],
        compiler_params=pltpu.CompilerParams(vmem_limit_bytes=24 << 20),
        cost_estimate=pl.CostEstimate(
            flops=2 * 256 * 256 * 768 * 3, bytes_accessed=2 << 20, transcendentals=0
        ),
        name="boxcars_later",
    )(widths, main)


def boxcars_first(main, tail, rest, widths):
    return pl.pallas_call(
        first_kernel,
        in_specs=[
            pl.BlockSpec(memory_space=pltpu.SMEM),
            pl.BlockSpec(memory_space=pltpu.VMEM),
            pl.BlockSpec(memory_space=pltpu.VMEM),
            pl.BlockSpec(memory_space=pltpu.HBM),
        ],
        out_specs=pl.BlockSpec(memory_space=pltpu.HBM),
        out_shape=OUT,
        input_output_aliases={3: 0},
        scratch_shapes=[
            pltpu.VMEM((BEAMS, NBOX, ROWS, LANES), jnp.float32),
            pltpu.SemaphoreType.DMA,
        ],
        compiler_params=pltpu.CompilerParams(vmem_limit_bytes=24 << 20),
        name="boxcars_first",
    )(widths, main, tail, rest)


def later(block, distance):
    route = []
    for part in range(PARTS):
        longest = (PARTS - 1 - part) * (ROWS - 2) + ROWS - 1
        if longest + SPAN > distance * SPAN:
            for i in range(SEGMENTS - distance):
                sender = part * SEGMENTS + i
                route.append((sender, sender + distance))
    return lax.ppermute(block, ("chan", "tm"), route)


def per_device(intensity, channel_scale, box_widths):
    q = (PARTS - 1 - lax.axis_index("chan")).astype(jnp.int32).reshape(1)
    pieces = list(local_plane(intensity, channel_scale.reshape(1, CHANS), q))
    for k in range(REACH - 1, 0, -1):
        pieces[k] = later(pieces[k], k)
    lined = gather_shifted(pieces)
    lined = lax.all_to_all(lined, "chan", 0, 0, tiled=True)
    main, tail = final_plane(lined)
    tail = later(tail, 1)
    rest = boxcars_later(main, box_widths)
    return boxcars_first(main, tail, rest, box_widths)


def solution(mesh):
    in_specs = (P(None, "chan", "tm"), P("chan"), P())
    out_specs = P(None, None, "chan", "tm")
    return jax.shard_map(
        per_device, mesh=mesh, in_specs=in_specs, out_specs=out_specs, check_vma=False
    )
```

```python
import jax
import jax.numpy as jnp
import numpy as np
from jax import lax
from jax.experimental import pallas as pl
from jax.experimental.pallas import tpu as pltpu
from jax.sharding import PartitionSpec as P

BEAMS = 2
CHANS = 512
SPAN = 512
PARTS = 32
SEGMENTS = 8
ROWS = 64
WIDE = SPAN + 128
NBOX = 6
LANES = 128
REACH = 5
TILES = 16
UNITS = 6
PER = SPAN // LANES


def packing():
    tail = [sum(((i >> level) + 1) // 2 for level in range(6)) for i in range(ROWS)]
    units = {}
    for q in range(PARTS):
        for a in range(TILES):
            delay = 4 * q * a
            ends = [
                delay % LANES + 2 * q * (r // 2) + SPAN + tail[4 * a + r] for r in range(4)
            ]
            units[q, a] = (delay // LANES, -(-max(ends) // LANES))
    counts = np.zeros((PARTS, REACH), np.int32)
    for (q, a), (first, number) in units.items():
        for h in range(first, first + number):
            counts[q, h // PER] += 1
    sizes = [int(n) for n in counts.max(axis=0)]
    starts = [sum(sizes[:k]) for k in range(REACH)]
    spare = sum(sizes)
    table = np.full((PARTS, 2, LANES), spare, np.int32)
    for q in range(PARTS):
        free = list(starts)
        for a in range(TILES):
            first, number = units[q, a]
            for i in range(number):
                h = first + i
                table[q, 0, a * UNITS + i] = free[h // PER]
                place = (a * PER + h % PER) * 2 + (i >= PER)
                table[q, 1, place] = free[h // PER]
                free[h // PER] += 1
    return sizes, starts, spare, table, counts


SIZES, STARTS, SPARE, TABLE, COUNTS = packing()


def split(x):
    first = x.astype(jnp.bfloat16)
    second = (x - first.astype(jnp.float32)).astype(jnp.bfloat16)
    return first, second


def roll(x, shift):
    return x if isinstance(shift, int) and shift == 0 else pltpu.roll(x, shift, 1)


def merge_groups(groups):
    merged = []
    for upper, lower in zip(groups[0::2], groups[1::2]):
        trials = []
        for e in range(len(upper)):
            early = roll(upper[e], e)
            trials += [lower[e] + early, lower[e] + roll(early, 1)]
        merged.append(trials)
    return merged


def put(ref, start, stride, rows):
    for c in range(rows.shape[1] // LANES):
        ref[c, pl.ds(start, 8, stride=stride), :] = rows[:, c * LANES : (c + 1) * LANES]


def take(ref, start, count, first, last):
    chunks = [ref[c, pl.ds(start, count), :] for c in range(first, last)]
    return jnp.concatenate(chunks, axis=1)


def merge_rows(groups, one, two):
    tiles = WIDE // LANES
    while len(groups) > 1:
        groups = merge_groups(groups)
    for e in range(8):
        put(one, e, 8, groups[0][e])
    source, target = one, two
    trials = 8
    while trials < ROWS:
        for base in range(0, ROWS, 2 * trials):
            for a in range(0, trials, 8):
                upper = take(source, base + a, 8, 0, tiles)
                lower = take(source, base + trials + a, 8, 0, tiles)
                early = pltpu.roll(upper, a, 1, stride=1, stride_axis=0)
                late = pltpu.roll(early, 1, 1)
                put(target, base + 2 * a, 2, lower + early)
                put(target, base + 2 * a + 1, 2, lower + late)
        source, target = target, source
        trials *= 2
    return source


def local_kernel(
    q_ref,
    table_hbm,
    scale_hbm,
    x_hbm,
    o0,
    o1,
    o2,
    o3,
    o4,
    slots,
    scale,
    x,
    one,
    two,
    packed,
    sems,
):
    half = CHANS // 2
    q = q_ref[0]
    fetch_scale = pltpu.make_async_copy(scale_hbm, scale, sems.at[2 * BEAMS])
    fetch_scale.start()
    fetch_slots = pltpu.make_async_copy(table_hbm.at[q], slots, sems.at[2 * BEAMS + 1])
    fetch_slots.start()
    fetches = []
    for b in range(BEAMS):
        for h in range(2):
            piece = pl.ds(h * half, half)
            fetches.append(
                pltpu.make_async_copy(
                    x_hbm.at[b, piece], x.at[b, piece], sems.at[2 * b + h]
                )
            )
            fetches[-1].start()
    row = lax.broadcasted_iota(jnp.int32, (ROWS, CHANS), 0)
    col = lax.broadcasted_iota(jnp.int32, (ROWS, CHANS), 1)
    member = (row & 7) * 8 + (row >> 3) == col >> 3
    fetch_scale.wait()
    weights = jnp.where(member, scale[...], 0.0)
    weights = jnp.concatenate(split(weights), axis=0)
    blank = jnp.zeros((8, LANES), jnp.float32)
    for b in range(BEAMS):
        fetches[2 * b].wait()
        fetches[2 * b + 1].wait()
        base = jnp.dot(weights, x[b], preferred_element_type=jnp.float32)
        base = base[:ROWS] + base[ROWS:]
        groups = [
            [jnp.concatenate([base[8 * g : 8 * g + 8], blank], axis=1)]
            for g in range(8)
        ]
        merge_rows(groups, one, two.at[b])
    fetch_slots.wait()
    odd = lax.broadcasted_iota(jnp.int32, (8, UNITS * LANES), 0) & 2 != 0
    for a in range(TILES):
        rows = [take(two.at[b], 4 * a, 4, 0, WIDE // LANES) for b in range(BEAMS)]
        rows = jnp.concatenate([jnp.concatenate(rows, axis=0), blank], axis=1)
        rows = jnp.where(odd, pltpu.roll(rows, 2 * q, 1), rows)
        rows = pltpu.roll(rows, (4 * q * a) & (LANES - 1), 1)
        for i in range(UNITS):
            packed[slots[0, a * UNITS + i]] = rows[:, i * LANES : (i + 1) * LANES]
    for k, out in enumerate((o0, o1, o2, o3, o4)):
        out[...] = packed[pl.ds(STARTS[k], SIZES[k])]


def local_plane(x, scale, q):
    return pl.pallas_call(
        local_kernel,
        in_specs=[
            pl.BlockSpec(memory_space=pltpu.SMEM),
            pl.BlockSpec(memory_space=pltpu.HBM),
            pl.BlockSpec(memory_space=pltpu.HBM),
            pl.BlockSpec(memory_space=pltpu.HBM),
        ],
        out_shape=[jax.ShapeDtypeStruct((n, 8, LANES), jnp.float32) for n in SIZES],
        scratch_shapes=[
            pltpu.SMEM((2, LANES), jnp.int32),
            pltpu.VMEM((1, CHANS), jnp.float32),
            pltpu.VMEM((BEAMS, CHANS, SPAN), jnp.bfloat16),
            pltpu.VMEM((WIDE // LANES, ROWS, LANES), jnp.float32),
            pltpu.VMEM((BEAMS, WIDE // LANES, ROWS, LANES), jnp.float32),
            pltpu.VMEM((SPARE + 1, 8, LANES), jnp.float32),
            pltpu.SemaphoreType.DMA((2 * BEAMS + 2,)),
        ],
        compiler_params=pltpu.CompilerParams(vmem_limit_bytes=24 << 20),
        name="local_plane",
    )(
        q,
        pltpu.with_memory_space_constraint(TABLE, pltpu.HBM),
        pltpu.with_memory_space_constraint(scale, pltpu.HBM),
        pltpu.with_memory_space_constraint(x, pltpu.HBM),
    )


def gather_kernel(
    q_ref, table_hbm, o0, r1, r2, r3, r4, out, slots, packed, held, sem
):
    fetch_slots = pltpu.make_async_copy(table_hbm.at[q_ref[0]], slots, sem)
    fetch_slots.start()
    for k, piece in enumerate((o0, r1, r2, r3, r4)):
        packed[pl.ds(STARTS[k], SIZES[k])] = piece[...]
    packed[SPARE] = jnp.zeros((8, LANES), jnp.float32)
    fetch_slots.wait()
    for a in range(TILES):
        for c in range(PER):
            place = (a * PER + c) * 2
            held[c, pl.ds(8 * a, 8), :] = (
                packed[slots[1, place]] + packed[slots[1, place + 1]]
            )
    for c in range(PER):
        for r in range(8):
            b, m, i = r >> 2, r >> 1 & 1, r & 1
            out[pl.ds(m * 16 + b * 8 + c * 2 + i, TILES, stride=32), :] = held[
                c, pl.ds(r, TILES, stride=8), :
            ]


def gather_shifted(pieces, q):
    vmem = pl.BlockSpec(memory_space=pltpu.VMEM)
    return pl.pallas_call(
        gather_kernel,
        in_specs=[
            pl.BlockSpec(memory_space=pltpu.SMEM),
            pl.BlockSpec(memory_space=pltpu.HBM),
        ]
        + [vmem] * REACH,
        out_shape=jax.ShapeDtypeStruct((PARTS * 16, LANES), jnp.float32),
        scratch_shapes=[
            pltpu.SMEM((2, LANES), jnp.int32),
            pltpu.VMEM((SPARE + 1, 8, LANES), jnp.float32),
            pltpu.VMEM((PER, 8 * TILES, LANES), jnp.float32),
            pltpu.SemaphoreType.DMA,
        ],
        compiler_params=pltpu.CompilerParams(vmem_limit_bytes=24 << 20),
        name="gather_shifted",
    )(q, pltpu.with_memory_space_constraint(TABLE, pltpu.HBM), *pieces)


def final_kernel(x_ref, main, tail, one, two):
    blank = jnp.zeros((8, LANES), jnp.float32)
    lane = lax.broadcasted_iota(jnp.int32, (ROWS, LANES), 1)
    for b in range(BEAMS):
        groups = []
        for g in range(4):
            trials = []
            for e in range(2):
                chunks = [
                    x_ref[pl.ds(g * 16 + b * 8 + c * 2 + e, 8, stride=64), :]
                    for c in range(SPAN // LANES)
                ]
                trials.append(jnp.concatenate(chunks + [blank], axis=1))
            groups.append(trials)
        plane = merge_rows(groups, one, two)
        main[b] = take(plane, 0, ROWS, 0, SPAN // LANES)
        tail[b] = jnp.where(
            lane < LANES // 2,
            plane[SPAN // LANES],
            plane[SPAN // LANES - 1],
        )


def final_plane(x):
    return pl.pallas_call(
        final_kernel,
        out_shape=[
            jax.ShapeDtypeStruct((BEAMS, ROWS, SPAN), jnp.float32),
            jax.ShapeDtypeStruct((BEAMS, ROWS, LANES), jnp.float32),
        ],
        scratch_shapes=[
            pltpu.VMEM((WIDE // LANES, ROWS, LANES), jnp.float32),
            pltpu.VMEM((WIDE // LANES, ROWS, LANES), jnp.float32),
        ],
        compiler_params=pltpu.CompilerParams(vmem_limit_bytes=24 << 20),
        name="final_plane",
    )(x)


def boxcar_bands(widths):
    u = lax.broadcasted_iota(jnp.int32, (2 * LANES, LANES), 0)
    t = lax.broadcasted_iota(jnp.int32, (2 * LANES, LANES), 1)
    ago = t + LANES - u
    bands = []
    for k in range(NBOX):
        inside = jnp.logical_and(ago >= 0, ago < widths[k])
        bands.append(jnp.where(inside, 1.0, 0.0).astype(jnp.bfloat16))
    return jnp.concatenate(bands, axis=1)


def boxcar_norms(widths):
    norms = []
    for k in range(NBOX):
        square = jnp.full((1, LANES), widths[k] * (CHANS * PARTS), jnp.int32)
        norms.append(lax.rsqrt(square.astype(jnp.float32)))
    return jnp.concatenate(norms, axis=1)


def boxcar_tile(before, here, bands, norms, held, c):
    window = jnp.concatenate([before, here], axis=1)
    sums = jnp.dot(window, bands, preferred_element_type=jnp.float32)
    rows = BEAMS * ROWS
    sums = (sums[:rows] + sums[rows:]) * norms
    for b in range(BEAMS):
        for k in range(NBOX):
            held[b, k, :, pl.ds(c * LANES, LANES)] = sums[
                b * ROWS : (b + 1) * ROWS, k * LANES : (k + 1) * LANES
            ]


def later_kernel(widths, main, out, held, sems):
    bands = boxcar_bands(widths)
    norms = boxcar_norms(widths)
    parts = []
    for c in range(SPAN // LANES):
        tile = main[:, :, pl.ds(c * LANES, LANES)].reshape(BEAMS * ROWS, LANES)
        parts.append(jnp.concatenate(split(tile), axis=0))
    copies = []
    for c in range(1, SPAN // LANES):
        boxcar_tile(parts[c - 1], parts[c], bands, norms, held, c - 1)
        copies.append(
            pltpu.make_async_copy(
                held.at[:, :, :, pl.ds((c - 1) * LANES, LANES)],
                out.at[:, :, :, pl.ds(c * LANES, LANES)],
                sems.at[c - 1],
            )
        )
        copies[-1].start()
    for copy in copies:
        copy.wait()


def first_kernel(widths, main, tail, rest, out, held, sem):
    del rest
    lane = lax.broadcasted_iota(jnp.int32, (BEAMS * ROWS, LANES), 1)
    edge = tail[...].reshape(BEAMS * ROWS, LANES)
    before = jnp.where(lane >= LANES // 2, edge, 0.0)
    here = main[:, :, pl.ds(0, LANES)].reshape(BEAMS * ROWS, LANES)
    here = here + jnp.where(lane < LANES // 2, edge, 0.0)
    before = jnp.concatenate(split(before), axis=0)
    here = jnp.concatenate(split(here), axis=0)
    boxcar_tile(before, here, boxcar_bands(widths), boxcar_norms(widths), held, 0)
    copy = pltpu.make_async_copy(held, out.at[:, :, :, pl.ds(0, LANES)], sem)
    copy.start()
    copy.wait()


OUT = jax.ShapeDtypeStruct((BEAMS, NBOX, ROWS, SPAN), jnp.float32)


def boxcars_later(main, widths):
    lanes = SPAN - LANES
    return pl.pallas_call(
        later_kernel,
        in_specs=[
            pl.BlockSpec(memory_space=pltpu.SMEM),
            pl.BlockSpec(memory_space=pltpu.VMEM),
        ],
        out_specs=pl.BlockSpec(memory_space=pltpu.HBM),
        out_shape=OUT,
        scratch_shapes=[
            pltpu.VMEM((BEAMS, NBOX, ROWS, lanes), jnp.float32),
            pltpu.SemaphoreType.DMA((lanes // LANES,)),
        ],
        compiler_params=pltpu.CompilerParams(vmem_limit_bytes=24 << 20),
        cost_estimate=pl.CostEstimate(
            flops=2 * 256 * 256 * 768 * 3, bytes_accessed=2 << 20, transcendentals=0
        ),
        name="boxcars_later",
    )(widths, main)


def boxcars_first(main, tail, rest, widths):
    return pl.pallas_call(
        first_kernel,
        in_specs=[
            pl.BlockSpec(memory_space=pltpu.SMEM),
            pl.BlockSpec(memory_space=pltpu.VMEM),
            pl.BlockSpec(memory_space=pltpu.VMEM),
            pl.BlockSpec(memory_space=pltpu.HBM),
        ],
        out_specs=pl.BlockSpec(memory_space=pltpu.HBM),
        out_shape=OUT,
        input_output_aliases={3: 0},
        scratch_shapes=[
            pltpu.VMEM((BEAMS, NBOX, ROWS, LANES), jnp.float32),
            pltpu.SemaphoreType.DMA,
        ],
        compiler_params=pltpu.CompilerParams(vmem_limit_bytes=24 << 20),
        name="boxcars_first",
    )(widths, main, tail, rest)


def later(block, distance):
    route = []
    for part in range(PARTS):
        if COUNTS[PARTS - 1 - part, distance]:
            for i in range(SEGMENTS - distance):
                sender = part * SEGMENTS + i
                route.append((sender, sender + distance))
    return lax.ppermute(block, ("chan", "tm"), route)


def per_device(intensity, channel_scale, box_widths):
    q = (PARTS - 1 - lax.axis_index("chan")).astype(jnp.int32).reshape(1)
    pieces = list(local_plane(intensity, channel_scale.reshape(1, CHANS), q))
    for k in range(REACH - 1, 0, -1):
        pieces[k] = later(pieces[k], k)
    lined = gather_shifted(pieces, q)
    lined = lax.all_to_all(lined, "chan", 0, 0, tiled=True)
    main, tail = final_plane(lined)
    tail = later(tail, 1)
    rest = boxcars_later(main, box_widths)
    return boxcars_first(main, tail, rest, box_widths)


def solution(mesh):
    in_specs = (P(None, "chan", "tm"), P("chan"), P())
    out_specs = P(None, None, "chan", "tm")
    return jax.shard_map(
        per_device, mesh=mesh, in_specs=in_specs, out_specs=out_specs, check_vma=False
    )
```

```python
import jax
import jax.numpy as jnp
import numpy as np
from jax import lax
from jax.experimental import pallas as pl
from jax.experimental.pallas import tpu as pltpu
from jax.sharding import PartitionSpec as P

BEAMS = 2
CHANS = 512
SPAN = 512
PARTS = 32
SEGMENTS = 8
ROWS = 64
WIDE = SPAN + 128
NBOX = 6
LANES = 128
REACH = 5
TILES = 16
UNITS = 6
PER = SPAN // LANES


def packing():
    tail = [sum(((i >> level) + 1) // 2 for level in range(6)) for i in range(ROWS)]
    units = {}
    for q in range(PARTS):
        for a in range(TILES):
            delay = 4 * q * a
            ends = [
                delay % LANES + 2 * q * (r // 2) + SPAN + tail[4 * a + r] for r in range(4)
            ]
            units[q, a] = (delay // LANES, -(-max(ends) // LANES))
    counts = np.zeros((PARTS, REACH), np.int32)
    for (q, a), (first, number) in units.items():
        for h in range(first, first + number):
            counts[q, h // PER] += 1
    buffers = np.tile(np.arange(REACH), (PARTS, 1))
    last = REACH - 1
    few = (counts[:, last] == 0) & (counts[:, last - 1] <= counts[:, last].max())
    buffers[few, last - 1] = last
    sizes = [0] * REACH
    distances = np.zeros((PARTS, REACH), np.int32)
    for q in range(PARTS):
        for k in range(REACH):
            if counts[q, k]:
                sizes[buffers[q, k]] = max(sizes[buffers[q, k]], int(counts[q, k]))
                distances[q, buffers[q, k]] = k
    starts = [sum(sizes[:k]) for k in range(REACH)]
    spare = sum(sizes)
    table = np.full((PARTS, 2, LANES), spare, np.int32)
    for q in range(PARTS):
        free = list(starts)
        for a in range(TILES):
            first, number = units[q, a]
            for i in range(number):
                h = first + i
                k = buffers[q, h // PER]
                table[q, 0, a * UNITS + i] = free[k]
                place = (a * PER + h % PER) * 2 + (i >= PER)
                table[q, 1, place] = free[k]
                free[k] += 1
    return sizes, starts, spare, table, distances


SIZES, STARTS, SPARE, TABLE, DISTANCES = packing()


def split(x):
    first = x.astype(jnp.bfloat16)
    second = (x - first.astype(jnp.float32)).astype(jnp.bfloat16)
    return first, second


def roll(x, shift):
    return x if isinstance(shift, int) and shift == 0 else pltpu.roll(x, shift, 1)


def merge_groups(groups):
    merged = []
    for upper, lower in zip(groups[0::2], groups[1::2]):
        trials = []
        for e in range(len(upper)):
            trials += [lower[e] + roll(upper[e], e), lower[e] + roll(upper[e], e + 1)]
        merged.append(trials)
    return merged


def put(ref, start, stride, rows):
    for c in range(rows.shape[1] // LANES):
        ref[c, pl.ds(start, 8, stride=stride), :] = rows[:, c * LANES : (c + 1) * LANES]


def take(ref, start, count, first, last):
    chunks = [ref[c, pl.ds(start, count), :] for c in range(first, last)]
    return jnp.concatenate(chunks, axis=1)


def merge_rows(groups, one, two):
    tiles = WIDE // LANES
    while len(groups) > 1:
        groups = merge_groups(groups)
    for e in range(8):
        put(one, e, 8, groups[0][e])
    source, target = one, two
    trials = 8
    while trials < ROWS:
        for base in range(0, ROWS, 2 * trials):
            for a in range(0, trials, 8):
                upper = take(source, base + a, 8, 0, tiles)
                lower = take(source, base + trials + a, 8, 0, tiles)
                early = pltpu.roll(upper, a, 1, stride=1, stride_axis=0)
                late = pltpu.roll(upper, a + 1, 1, stride=1, stride_axis=0)
                put(target, base + 2 * a, 2, lower + early)
                put(target, base + 2 * a + 1, 2, lower + late)
        source, target = target, source
        trials *= 2
    return source


def local_kernel(
    q_ref,
    table_hbm,
    scale_hbm,
    x_hbm,
    o0,
    o1,
    o2,
    o3,
    o4,
    slots,
    scale,
    x,
    one,
    two,
    packed,
    sems,
):
    half = CHANS // 2
    q = q_ref[0]
    fetch_scale = pltpu.make_async_copy(scale_hbm, scale, sems.at[2 * BEAMS])
    fetch_scale.start()
    fetch_slots = pltpu.make_async_copy(table_hbm.at[q], slots, sems.at[2 * BEAMS + 1])
    fetch_slots.start()
    fetches = []
    for b in range(BEAMS):
        for h in range(2):
            piece = pl.ds(h * half, half)
            fetches.append(
                pltpu.make_async_copy(
                    x_hbm.at[b, piece], x.at[b, piece], sems.at[2 * b + h]
                )
            )
            fetches[-1].start()
    row = lax.broadcasted_iota(jnp.int32, (ROWS, CHANS), 0)
    col = lax.broadcasted_iota(jnp.int32, (ROWS, CHANS), 1)
    member = (row & 7) * 8 + (row >> 3) == col >> 3
    fetch_scale.wait()
    weights = jnp.where(member, scale[...], 0.0)
    weights = jnp.concatenate(split(weights), axis=0)
    blank = jnp.zeros((8, LANES), jnp.float32)
    for b in range(BEAMS):
        fetches[2 * b].wait()
        fetches[2 * b + 1].wait()
        base = jnp.dot(weights, x[b], preferred_element_type=jnp.float32)
        base = base[:ROWS] + base[ROWS:]
        groups = [
            [jnp.concatenate([base[8 * g : 8 * g + 8], blank], axis=1)]
            for g in range(8)
        ]
        merge_rows(groups, one.at[b], two.at[b])
    fetch_slots.wait()
    odd = lax.broadcasted_iota(jnp.int32, (8, UNITS * LANES), 0) & 2 != 0
    for a in range(TILES):
        rows = [take(two.at[b], 4 * a, 4, 0, WIDE // LANES) for b in range(BEAMS)]
        rows = jnp.concatenate([jnp.concatenate(rows, axis=0), blank], axis=1)
        rows = jnp.where(odd, pltpu.roll(rows, 2 * q, 1), rows)
        rows = pltpu.roll(rows, (4 * q * a) & (LANES - 1), 1)
        for i in range(UNITS):
            packed[slots[0, a * UNITS + i]] = rows[:, i * LANES : (i + 1) * LANES]
    for k, out in enumerate((o0, o1, o2, o3, o4)):
        out[...] = packed[pl.ds(STARTS[k], SIZES[k])]


def local_plane(x, scale, q):
    return pl.pallas_call(
        local_kernel,
        in_specs=[
            pl.BlockSpec(memory_space=pltpu.SMEM),
            pl.BlockSpec(memory_space=pltpu.HBM),
            pl.BlockSpec(memory_space=pltpu.HBM),
            pl.BlockSpec(memory_space=pltpu.HBM),
        ],
        out_shape=[jax.ShapeDtypeStruct((n, 8, LANES), jnp.float32) for n in SIZES],
        scratch_shapes=[
            pltpu.SMEM((2, LANES), jnp.int32),
            pltpu.VMEM((1, CHANS), jnp.float32),
            pltpu.VMEM((BEAMS, CHANS, SPAN), jnp.bfloat16),
            pltpu.VMEM((BEAMS, WIDE // LANES, ROWS, LANES), jnp.float32),
            pltpu.VMEM((BEAMS, WIDE // LANES, ROWS, LANES), jnp.float32),
            pltpu.VMEM((SPARE + 1, 8, LANES), jnp.float32),
            pltpu.SemaphoreType.DMA((2 * BEAMS + 2,)),
        ],
        compiler_params=pltpu.CompilerParams(vmem_limit_bytes=24 << 20),
        name="local_plane",
    )(
        q,
        pltpu.with_memory_space_constraint(TABLE, pltpu.HBM),
        pltpu.with_memory_space_constraint(scale, pltpu.HBM),
        pltpu.with_memory_space_constraint(x, pltpu.HBM),
    )


def gather_kernel(q_ref, table, o0, r1, r2, r3, r4, out, slots, packed, held, sem):
    fetch_slots = pltpu.make_async_copy(table.at[q_ref[0]], slots, sem)
    fetch_slots.start()
    for k, piece in enumerate((o0, r1, r2, r3, r4)):
        packed[pl.ds(STARTS[k], SIZES[k])] = piece[...]
    packed[SPARE] = jnp.zeros((8, LANES), jnp.float32)
    fetch_slots.wait()
    for a in range(TILES):
        for c in range(PER):
            place = (a * PER + c) * 2
            held[c, pl.ds(8 * a, 8), :] = (
                packed[slots[1, place]] + packed[slots[1, place + 1]]
            )
    for c in range(PER):
        for r in range(8):
            b, m, i = r >> 2, r >> 1 & 1, r & 1
            out[pl.ds(m * 16 + b * 8 + c * 2 + i, TILES, stride=32), :] = held[
                c, pl.ds(r, TILES, stride=8), :
            ]


def gather_shifted(pieces, q):
    vmem = pl.BlockSpec(memory_space=pltpu.VMEM)
    return pl.pallas_call(
        gather_kernel,
        in_specs=[
            pl.BlockSpec(memory_space=pltpu.SMEM),
        ]
        + [vmem] * (1 + REACH),
        out_shape=jax.ShapeDtypeStruct((PARTS * 16, LANES), jnp.float32),
        scratch_shapes=[
            pltpu.SMEM((2, LANES), jnp.int32),
            pltpu.VMEM((SPARE + 1, 8, LANES), jnp.float32),
            pltpu.VMEM((PER, 8 * TILES, LANES), jnp.float32),
            pltpu.SemaphoreType.DMA,
        ],
        compiler_params=pltpu.CompilerParams(vmem_limit_bytes=24 << 20),
        name="gather_shifted",
    )(q, TABLE, *pieces)


def final_kernel(x_ref, main, tail, one, two):
    blank = jnp.zeros((8, LANES), jnp.float32)
    lane = lax.broadcasted_iota(jnp.int32, (ROWS, LANES), 1)
    for b in range(BEAMS):
        groups = []
        for g in range(4):
            trials = []
            for e in range(2):
                chunks = [
                    x_ref[pl.ds(g * 16 + b * 8 + c * 2 + e, 8, stride=64), :]
                    for c in range(SPAN // LANES)
                ]
                trials.append(jnp.concatenate(chunks + [blank], axis=1))
            groups.append(trials)
        plane = merge_rows(groups, one.at[b], two.at[b])
        main[b] = take(plane, 0, ROWS, 0, SPAN // LANES)
        tail[b] = jnp.where(
            lane < LANES // 2,
            plane[SPAN // LANES],
            plane[SPAN // LANES - 1],
        )


def final_plane(x):
    return pl.pallas_call(
        final_kernel,
        out_shape=[
            jax.ShapeDtypeStruct((BEAMS, ROWS, SPAN), jnp.float32),
            jax.ShapeDtypeStruct((BEAMS, ROWS, LANES), jnp.float32),
        ],
        scratch_shapes=[
            pltpu.VMEM((BEAMS, WIDE // LANES, ROWS, LANES), jnp.float32),
            pltpu.VMEM((BEAMS, WIDE // LANES, ROWS, LANES), jnp.float32),
        ],
        compiler_params=pltpu.CompilerParams(vmem_limit_bytes=24 << 20),
        name="final_plane",
    )(x)


def boxcar_bands(widths):
    u = lax.broadcasted_iota(jnp.int32, (2 * LANES, LANES), 0)
    t = lax.broadcasted_iota(jnp.int32, (2 * LANES, LANES), 1)
    ago = t + LANES - u
    bands = []
    for k in range(NBOX):
        inside = jnp.logical_and(ago >= 0, ago < widths[k])
        bands.append(jnp.where(inside, 1.0, 0.0).astype(jnp.bfloat16))
    return jnp.concatenate(bands, axis=1)


def boxcar_norms(widths):
    norms = []
    for k in range(NBOX):
        square = jnp.full((1, LANES), widths[k] * (CHANS * PARTS), jnp.int32)
        norms.append(lax.rsqrt(square.astype(jnp.float32)))
    return jnp.concatenate(norms, axis=1)


def boxcar_tile(before, here, bands, norms, held, c):
    window = jnp.concatenate([before, here], axis=1)
    sums = jnp.dot(window, bands, preferred_element_type=jnp.float32)
    rows = BEAMS * ROWS
    sums = (sums[:rows] + sums[rows:]) * norms
    for b in range(BEAMS):
        for k in range(NBOX):
            held[b, k, :, pl.ds(c * LANES, LANES)] = sums[
                b * ROWS : (b + 1) * ROWS, k * LANES : (k + 1) * LANES
            ]


def later_kernel(widths, main, out, bands_out, norms_out, held, sems):
    bands = boxcar_bands(widths)
    norms = boxcar_norms(widths)
    bands_out[...] = bands
    norms_out[...] = norms
    parts = []
    for c in range(SPAN // LANES):
        tile = main[:, :, pl.ds(c * LANES, LANES)].reshape(BEAMS * ROWS, LANES)
        parts.append(jnp.concatenate(split(tile), axis=0))
    copies = []
    for c in range(1, SPAN // LANES):
        boxcar_tile(parts[c - 1], parts[c], bands, norms, held, c - 1)
        copies.append(
            pltpu.make_async_copy(
                held.at[:, :, :, pl.ds((c - 1) * LANES, LANES)],
                out.at[:, :, :, pl.ds(c * LANES, LANES)],
                sems.at[c - 1],
            )
        )
        copies[-1].start()
    for copy in copies:
        copy.wait()


def first_kernel(main, tail, bands, norms, rest, out, held, sem):
    del rest
    lane = lax.broadcasted_iota(jnp.int32, (BEAMS * ROWS, LANES), 1)
    edge = tail[...].reshape(BEAMS * ROWS, LANES)
    before = jnp.where(lane >= LANES // 2, edge, 0.0)
    here = main[:, :, pl.ds(0, LANES)].reshape(BEAMS * ROWS, LANES)
    here = here + jnp.where(lane < LANES // 2, edge, 0.0)
    before = jnp.concatenate(split(before), axis=0)
    here = jnp.concatenate(split(here), axis=0)
    boxcar_tile(before, here, bands[...], norms[...], held, 0)
    copy = pltpu.make_async_copy(held, out.at[:, :, :, pl.ds(0, LANES)], sem)
    copy.start()
    copy.wait()


OUT = jax.ShapeDtypeStruct((BEAMS, NBOX, ROWS, SPAN), jnp.float32)


def boxcars_later(main, widths):
    lanes = SPAN - LANES
    return pl.pallas_call(
        later_kernel,
        in_specs=[
            pl.BlockSpec(memory_space=pltpu.SMEM),
            pl.BlockSpec(memory_space=pltpu.VMEM),
        ],
        out_specs=[
            pl.BlockSpec(memory_space=pltpu.HBM),
            pl.BlockSpec(memory_space=pltpu.VMEM),
            pl.BlockSpec(memory_space=pltpu.VMEM),
        ],
        out_shape=[
            OUT,
            jax.ShapeDtypeStruct((2 * LANES, NBOX * LANES), jnp.bfloat16),
            jax.ShapeDtypeStruct((1, NBOX * LANES), jnp.float32),
        ],
        scratch_shapes=[
            pltpu.VMEM((BEAMS, NBOX, ROWS, lanes), jnp.float32),
            pltpu.SemaphoreType.DMA((lanes // LANES,)),
        ],
        compiler_params=pltpu.CompilerParams(vmem_limit_bytes=24 << 20),
        cost_estimate=pl.CostEstimate(
            flops=2 * 256 * 256 * 768 * 3, bytes_accessed=2 << 20, transcendentals=0
        ),
        name="boxcars_later",
    )(widths, main)


def boxcars_first(main, tail, bands, norms, rest):
    return pl.pallas_call(
        first_kernel,
        in_specs=[pl.BlockSpec(memory_space=pltpu.VMEM)] * 4
        + [pl.BlockSpec(memory_space=pltpu.HBM)],
        out_specs=pl.BlockSpec(memory_space=pltpu.HBM),
        out_shape=OUT,
        input_output_aliases={4: 0},
        scratch_shapes=[
            pltpu.VMEM((BEAMS, NBOX, ROWS, LANES), jnp.float32),
            pltpu.SemaphoreType.DMA,
        ],
        compiler_params=pltpu.CompilerParams(vmem_limit_bytes=24 << 20),
        name="boxcars_first",
    )(main, tail, bands, norms, rest)


def later(block, buffer):
    route = []
    for part in range(PARTS):
        distance = int(DISTANCES[PARTS - 1 - part, buffer])
        if distance:
            for i in range(SEGMENTS - distance):
                sender = part * SEGMENTS + i
                route.append((sender, sender + distance))
    return lax.ppermute(block, ("chan", "tm"), route)


def per_device(intensity, channel_scale, box_widths):
    q = (PARTS - 1 - lax.axis_index("chan")).astype(jnp.int32).reshape(1)
    pieces = list(local_plane(intensity, channel_scale.reshape(1, CHANS), q))
    for k in range(REACH - 1, 0, -1):
        pieces[k] = later(pieces[k], k)
    lined = gather_shifted(pieces, q)
    lined = lax.all_to_all(lined, "chan", 0, 0, tiled=True)
    main, tail = final_plane(lined)
    tail = later(tail, 1)
    rest, bands, norms = boxcars_later(main, box_widths)
    return boxcars_first(main, tail, bands, norms, rest)


def solution(mesh):
    in_specs = (P(None, "chan", "tm"), P("chan"), P())
    out_specs = P(None, None, "chan", "tm")
    return jax.shard_map(
        per_device, mesh=mesh, in_specs=in_specs, out_specs=out_specs, check_vma=False
    )
```

```python
import jax
import jax.numpy as jnp
import numpy as np
from jax import lax
from jax.experimental import pallas as pl
from jax.experimental.pallas import tpu as pltpu
from jax.sharding import PartitionSpec as P

BEAMS = 2
CHANS = 512
SPAN = 512
PARTS = 32
SEGMENTS = 8
ROWS = 64
WIDE = SPAN + 128
NBOX = 6
LANES = 128
REACH = 5
TILES = 16
UNITS = 6
PER = SPAN // LANES


def tails(a):
    reach = [sum((i >> level) + 1 >> 1 for level in range(6)) for i in range(4 * a, 4 * a + 4)]
    return max(reach[:2]), max(reach[2:])


def tile_span(q, a):
    delay = 4 * q * a
    first, second = tails(a)
    end = (delay & (LANES - 1)) + SPAN
    if isinstance(q, int):
        end += max(first, 2 * q + second)
    else:
        end += jnp.maximum(first, 2 * q + second)
    return delay >> 7, (end + LANES - 1) >> 7


def packing():
    counts = np.zeros((PARTS, REACH), np.int32)
    for q in range(PARTS):
        for a in range(TILES):
            first, number = tile_span(q, a)
            for h in range(first, first + number):
                counts[q, h // PER] += 1
    sizes = [64, 48, 30, 23, 10]
    buffers = np.zeros((PARTS, REACH), np.int32)
    distances = np.zeros((PARTS, REACH), np.int32)
    for q in range(PARTS):
        taken = {0}
        for k in range(REACH - 1, 0, -1):
            if counts[q, k]:
                fits = [i for i in range(1, REACH) if i not in taken and sizes[i] >= counts[q, k]]
                buffers[q, k] = fits[-1]
                distances[q, fits[-1]] = k
                taken.add(fits[-1])
    starts = [sum(sizes[:k]) for k in range(REACH)]
    return sizes, starts, sum(sizes), buffers, distances


SIZES, STARTS, SPARE, BUFFERS, DISTANCES = packing()


def first_slots(q, free):
    for k in range(REACH):
        slot = STARTS[BUFFERS[0, k]]
        for band in range(1, PARTS):
            if BUFFERS[band, k] != BUFFERS[band - 1, k]:
                slot = jnp.where(q >= band, STARTS[BUFFERS[band, k]], slot)
        free[k] = slot
    free[REACH] = SPARE


def unit_slots(q, a, free):
    first, number = tile_span(q, a)
    at, k = first & (PER - 1), first >> 2
    here = jnp.minimum(PER - at, number)
    rest = number - here
    then = jnp.minimum(rest, PER)
    p0, p1, p2 = free[k], free[k + 1], free[k + 2]
    free[k] = p0 + here
    free[k + 1] = p1 + then
    free[k + 2] = p2 + rest - then
    slots = [p0]
    for i in range(1, PER):
        slots.append(jnp.where(i < here, p0 + i, p1 + i - here))
    slots.append(p1 + PER - here)
    last = jnp.where(here > 1, p1 + PER + 1 - here, p2)
    slots.append(jnp.where(number > PER + 1, last, SPARE))
    return slots, at


def split(x):
    first = x.astype(jnp.bfloat16)
    second = (x - first.astype(jnp.float32)).astype(jnp.bfloat16)
    return first, second


def roll(x, shift):
    return x if isinstance(shift, int) and shift == 0 else pltpu.roll(x, shift, 1)


def merge_groups(groups):
    merged = []
    for upper, lower in zip(groups[0::2], groups[1::2]):
        trials = []
        for e in range(len(upper)):
            trials += [lower[e] + roll(upper[e], e), lower[e] + roll(upper[e], e + 1)]
        merged.append(trials)
    return merged


def put(ref, start, stride, rows):
    for c in range(rows.shape[1] // LANES):
        ref[c, pl.ds(start, 8, stride=stride), :] = rows[:, c * LANES : (c + 1) * LANES]


def take(ref, start, count, first, last):
    chunks = [ref[c, pl.ds(start, count), :] for c in range(first, last)]
    return jnp.concatenate(chunks, axis=1)


def merge_rows(groups, one, two):
    tiles = WIDE // LANES
    while len(groups) > 1:
        groups = merge_groups(groups)
    for e in range(8):
        put(one, e, 8, groups[0][e])
    source, target = one, two
    trials = 8
    while trials < ROWS:
        for base in range(0, ROWS, 2 * trials):
            for a in range(0, trials, 8):
                upper = take(source, base + a, 8, 0, tiles)
                lower = take(source, base + trials + a, 8, 0, tiles)
                early = pltpu.roll(upper, a, 1, stride=1, stride_axis=0)
                late = pltpu.roll(upper, a + 1, 1, stride=1, stride_axis=0)
                put(target, base + 2 * a, 2, lower + early)
                put(target, base + 2 * a + 1, 2, lower + late)
        source, target = target, source
        trials *= 2
    return source


def local_kernel(
    q_ref,
    scale_hbm,
    x_hbm,
    o0,
    o1,
    o2,
    o3,
    o4,
    free,
    scale,
    x,
    one,
    two,
    packed,
    sems,
):
    half = CHANS // 2
    q = q_ref[0]
    fetch_scale = pltpu.make_async_copy(scale_hbm, scale, sems.at[2 * BEAMS])
    fetch_scale.start()
    fetches = []
    for b in range(BEAMS):
        for h in range(2):
            piece = pl.ds(h * half, half)
            fetches.append(
                pltpu.make_async_copy(
                    x_hbm.at[b, piece], x.at[b, piece], sems.at[2 * b + h]
                )
            )
            fetches[-1].start()
    row = lax.broadcasted_iota(jnp.int32, (ROWS, CHANS), 0)
    col = lax.broadcasted_iota(jnp.int32, (ROWS, CHANS), 1)
    member = (row & 7) * 8 + (row >> 3) == col >> 3
    fetch_scale.wait()
    weights = jnp.where(member, scale[...], 0.0)
    weights = jnp.concatenate(split(weights), axis=0)
    blank = jnp.zeros((8, LANES), jnp.float32)
    for b in range(BEAMS):
        fetches[2 * b].wait()
        fetches[2 * b + 1].wait()
        base = jnp.dot(weights, x[b], preferred_element_type=jnp.float32)
        base = base[:ROWS] + base[ROWS:]
        groups = [
            [jnp.concatenate([base[8 * g : 8 * g + 8], blank], axis=1)]
            for g in range(8)
        ]
        merge_rows(groups, one.at[b], two.at[b])
    first_slots(q, free)
    odd = lax.broadcasted_iota(jnp.int32, (8, UNITS * LANES), 0) & 2 != 0
    for a in range(TILES):
        rows = [take(two.at[b], 4 * a, 4, 0, WIDE // LANES) for b in range(BEAMS)]
        rows = jnp.concatenate([jnp.concatenate(rows, axis=0), blank], axis=1)
        rows = jnp.where(odd, pltpu.roll(rows, 2 * q, 1), rows)
        rows = pltpu.roll(rows, (4 * q * a) & (LANES - 1), 1)
        slots, _ = unit_slots(q, a, free)
        for i, slot in enumerate(slots):
            packed[slot] = rows[:, i * LANES : (i + 1) * LANES]
    for k, out in enumerate((o0, o1, o2, o3, o4)):
        out[...] = packed[pl.ds(STARTS[k], SIZES[k])]


def local_plane(x, scale, q):
    return pl.pallas_call(
        local_kernel,
        in_specs=[
            pl.BlockSpec(memory_space=pltpu.SMEM),
            pl.BlockSpec(memory_space=pltpu.HBM),
            pl.BlockSpec(memory_space=pltpu.HBM),
        ],
        out_shape=[jax.ShapeDtypeStruct((n, 8, LANES), jnp.float32) for n in SIZES],
        scratch_shapes=[
            pltpu.SMEM((REACH + 3,), jnp.int32),
            pltpu.VMEM((1, CHANS), jnp.float32),
            pltpu.VMEM((BEAMS, CHANS, SPAN), jnp.bfloat16),
            pltpu.VMEM((BEAMS, WIDE // LANES, ROWS, LANES), jnp.float32),
            pltpu.VMEM((BEAMS, WIDE // LANES, ROWS, LANES), jnp.float32),
            pltpu.VMEM((SPARE + 1, 8, LANES), jnp.float32),
            pltpu.SemaphoreType.DMA((2 * BEAMS + 1,)),
        ],
        compiler_params=pltpu.CompilerParams(vmem_limit_bytes=24 << 20),
        name="local_plane",
    )(
        q,
        pltpu.with_memory_space_constraint(scale, pltpu.HBM),
        pltpu.with_memory_space_constraint(x, pltpu.HBM),
    )


def gather_kernel(q_ref, o0, r1, r2, r3, r4, out, free, packed, held):
    q = q_ref[0]
    first_slots(q, free)
    for k, piece in enumerate((o0, r1, r2, r3, r4)):
        packed[pl.ds(STARTS[k], SIZES[k])] = piece[...]
    packed[SPARE] = jnp.zeros((8, LANES), jnp.float32)
    for a in range(TILES):
        slots, at = unit_slots(q, a, free)
        rows = pl.ds(8 * a, 8)
        tiles = [(at + i) & (PER - 1) for i in range(PER)]
        held[tiles[0], rows, :] = packed[slots[0]] + packed[slots[PER]]
        held[tiles[1], rows, :] = packed[slots[1]] + packed[slots[PER + 1]]
        held[tiles[2], rows, :] = packed[slots[2]]
        held[tiles[3], rows, :] = packed[slots[3]]
    for c in range(PER):
        for r in range(8):
            b, m, i = r >> 2, r >> 1 & 1, r & 1
            out[pl.ds(m * 16 + b * 8 + c * 2 + i, TILES, stride=32), :] = held[
                c, pl.ds(r, TILES, stride=8), :
            ]


def gather_shifted(pieces, q):
    vmem = pl.BlockSpec(memory_space=pltpu.VMEM)
    return pl.pallas_call(
        gather_kernel,
        in_specs=[pl.BlockSpec(memory_space=pltpu.SMEM)] + [vmem] * REACH,
        out_shape=jax.ShapeDtypeStruct((PARTS * 16, LANES), jnp.float32),
        scratch_shapes=[
            pltpu.SMEM((REACH + 3,), jnp.int32),
            pltpu.VMEM((SPARE + 1, 8, LANES), jnp.float32),
            pltpu.VMEM((PER, 8 * TILES, LANES), jnp.float32),
        ],
        compiler_params=pltpu.CompilerParams(vmem_limit_bytes=24 << 20),
        name="gather_shifted",
    )(q, *pieces)


def final_kernel(x_ref, main, tail, one, two):
    blank = jnp.zeros((8, LANES), jnp.float32)
    lane = lax.broadcasted_iota(jnp.int32, (ROWS, LANES), 1)
    for b in range(BEAMS):
        groups = []
        for g in range(4):
            trials = []
            for e in range(2):
                chunks = [
                    x_ref[pl.ds(g * 16 + b * 8 + c * 2 + e, 8, stride=64), :]
                    for c in range(SPAN // LANES)
                ]
                trials.append(jnp.concatenate(chunks + [blank], axis=1))
            groups.append(trials)
        plane = merge_rows(groups, one.at[b], two.at[b])
        main[b] = take(plane, 0, ROWS, 0, SPAN // LANES)
        tail[b] = jnp.where(
            lane < LANES // 2,
            plane[SPAN // LANES],
            plane[SPAN // LANES - 1],
        )


def final_plane(x):
    return pl.pallas_call(
        final_kernel,
        out_shape=[
            jax.ShapeDtypeStruct((BEAMS, ROWS, SPAN), jnp.float32),
            jax.ShapeDtypeStruct((BEAMS, ROWS, LANES), jnp.float32),
        ],
        scratch_shapes=[
            pltpu.VMEM((BEAMS, WIDE // LANES, ROWS, LANES), jnp.float32),
            pltpu.VMEM((BEAMS, WIDE // LANES, ROWS, LANES), jnp.float32),
        ],
        compiler_params=pltpu.CompilerParams(vmem_limit_bytes=24 << 20),
        name="final_plane",
    )(x)


def boxcar_bands(widths):
    u = lax.broadcasted_iota(jnp.int32, (2 * LANES, LANES), 0)
    t = lax.broadcasted_iota(jnp.int32, (2 * LANES, LANES), 1)
    ago = t + LANES - u
    bands = []
    for k in range(NBOX):
        inside = jnp.logical_and(ago >= 0, ago < widths[k])
        bands.append(jnp.where(inside, 1.0, 0.0).astype(jnp.bfloat16))
    return jnp.concatenate(bands, axis=1)


def boxcar_norms(widths):
    norms = []
    for k in range(NBOX):
        square = jnp.full((1, LANES), widths[k] * (CHANS * PARTS), jnp.int32)
        norms.append(lax.rsqrt(square.astype(jnp.float32)))
    return jnp.concatenate(norms, axis=1)


def boxcar_tile(before, here, bands, norms, held, c):
    window = jnp.concatenate([before, here], axis=1)
    sums = jnp.dot(window, bands, preferred_element_type=jnp.float32)
    rows = BEAMS * ROWS
    sums = (sums[:rows] + sums[rows:]) * norms
    for b in range(BEAMS):
        for k in range(NBOX):
            held[b, k, :, pl.ds(c * LANES, LANES)] = sums[
                b * ROWS : (b + 1) * ROWS, k * LANES : (k + 1) * LANES
            ]


def later_kernel(widths, main, out, bands_out, norms_out, held, sems):
    bands = boxcar_bands(widths)
    norms = boxcar_norms(widths)
    bands_out[...] = bands
    norms_out[...] = norms
    parts = []
    for c in range(SPAN // LANES):
        tile = main[:, :, pl.ds(c * LANES, LANES)].reshape(BEAMS * ROWS, LANES)
        parts.append(jnp.concatenate(split(tile), axis=0))
    copies = []
    for c in range(1, SPAN // LANES):
        boxcar_tile(parts[c - 1], parts[c], bands, norms, held, c - 1)
        copies.append(
            pltpu.make_async_copy(
                held.at[:, :, :, pl.ds((c - 1) * LANES, LANES)],
                out.at[:, :, :, pl.ds(c * LANES, LANES)],
                sems.at[c - 1],
            )
        )
        copies[-1].start()
    for copy in copies:
        copy.wait()


def first_kernel(main, tail, bands, norms, rest, out, held, sem):
    del rest
    lane = lax.broadcasted_iota(jnp.int32, (BEAMS * ROWS, LANES), 1)
    edge = tail[...].reshape(BEAMS * ROWS, LANES)
    before = jnp.where(lane >= LANES // 2, edge, 0.0)
    here = main[:, :, pl.ds(0, LANES)].reshape(BEAMS * ROWS, LANES)
    here = here + jnp.where(lane < LANES // 2, edge, 0.0)
    before = jnp.concatenate(split(before), axis=0)
    here = jnp.concatenate(split(here), axis=0)
    boxcar_tile(before, here, bands[...], norms[...], held, 0)
    copy = pltpu.make_async_copy(held, out.at[:, :, :, pl.ds(0, LANES)], sem)
    copy.start()
    copy.wait()


OUT = jax.ShapeDtypeStruct((BEAMS, NBOX, ROWS, SPAN), jnp.float32)


def boxcars_later(main, widths):
    lanes = SPAN - LANES
    return pl.pallas_call(
        later_kernel,
        in_specs=[
            pl.BlockSpec(memory_space=pltpu.SMEM),
            pl.BlockSpec(memory_space=pltpu.VMEM),
        ],
        out_specs=[
            pl.BlockSpec(memory_space=pltpu.HBM),
            pl.BlockSpec(memory_space=pltpu.VMEM),
            pl.BlockSpec(memory_space=pltpu.VMEM),
        ],
        out_shape=[
            OUT,
            jax.ShapeDtypeStruct((2 * LANES, NBOX * LANES), jnp.bfloat16),
            jax.ShapeDtypeStruct((1, NBOX * LANES), jnp.float32),
        ],
        scratch_shapes=[
            pltpu.VMEM((BEAMS, NBOX, ROWS, lanes), jnp.float32),
            pltpu.SemaphoreType.DMA((lanes // LANES,)),
        ],
        compiler_params=pltpu.CompilerParams(vmem_limit_bytes=24 << 20),
        cost_estimate=pl.CostEstimate(
            flops=2 * 256 * 256 * 768 * 3, bytes_accessed=2 << 20, transcendentals=0
        ),
        name="boxcars_later",
    )(widths, main)


def boxcars_first(main, tail, bands, norms, rest):
    return pl.pallas_call(
        first_kernel,
        in_specs=[pl.BlockSpec(memory_space=pltpu.VMEM)] * 4
        + [pl.BlockSpec(memory_space=pltpu.HBM)],
        out_specs=pl.BlockSpec(memory_space=pltpu.HBM),
        out_shape=OUT,
        input_output_aliases={4: 0},
        scratch_shapes=[
            pltpu.VMEM((BEAMS, NBOX, ROWS, LANES), jnp.float32),
            pltpu.SemaphoreType.DMA,
        ],
        compiler_params=pltpu.CompilerParams(vmem_limit_bytes=24 << 20),
        name="boxcars_first",
    )(main, tail, bands, norms, rest)


def later(block, distances):
    route = []
    for part, distance in enumerate(distances):
        if distance:
            for i in range(SEGMENTS - distance):
                sender = part * SEGMENTS + i
                route.append((sender, sender + distance))
    return lax.ppermute(block, ("chan", "tm"), route)


def per_device(intensity, channel_scale, box_widths):
    q = (PARTS - 1 - lax.axis_index("chan")).astype(jnp.int32).reshape(1)
    pieces = list(local_plane(intensity, channel_scale.reshape(1, CHANS), q))
    for k in range(REACH - 1, 0, -1):
        pieces[k] = later(pieces[k], DISTANCES[::-1, k].tolist())
    lined = gather_shifted(pieces, q)
    lined = lax.all_to_all(lined, "chan", 0, 0, tiled=True)
    main, tail = final_plane(lined)
    tail = later(tail, [1] * PARTS)
    rest, bands, norms = boxcars_later(main, box_widths)
    return boxcars_first(main, tail, bands, norms, rest)


def solution(mesh):
    in_specs = (P(None, "chan", "tm"), P("chan"), P())
    out_specs = P(None, None, "chan", "tm")
    return jax.shard_map(
        per_device, mesh=mesh, in_specs=in_specs, out_specs=out_specs, check_vma=False
    )
```

```python
import jax
import jax.numpy as jnp
import numpy as np
from jax import lax
from jax.experimental import pallas as pl
from jax.experimental.pallas import tpu as pltpu
from jax.sharding import PartitionSpec as P

BEAMS = 2
CHANS = 512
SPAN = 512
PARTS = 32
SEGMENTS = 8
ROWS = 64
WIDE = SPAN + 128
NBOX = 6
LANES = 128
REACH = 5
TILES = 16
UNITS = 6
PER = SPAN // LANES


def tails(a):
    reach = [sum((i >> level) + 1 >> 1 for level in range(6)) for i in range(4 * a, 4 * a + 4)]
    return max(reach[:2]), max(reach[2:])


def tile_span(q, a):
    delay = 4 * q * a
    first, second = tails(a)
    end = (delay & (LANES - 1)) + SPAN
    if isinstance(q, int):
        end += max(first, 2 * q + second)
    else:
        end += jnp.maximum(first, 2 * q + second)
    return delay >> 7, (end + LANES - 1) >> 7


def packing():
    counts = np.zeros((PARTS, REACH), np.int32)
    for q in range(PARTS):
        for a in range(TILES):
            first, number = tile_span(q, a)
            for h in range(first, first + number):
                counts[q, h // PER] += 1
    sizes = [64, 48, 30, 10, 23]
    buffers = np.zeros((PARTS, REACH), np.int32)
    distances = np.zeros((PARTS, REACH), np.int32)
    for q in range(PARTS):
        taken = {0}
        for k in range(REACH - 1, 0, -1):
            if counts[q, k]:
                fits = [i for i in (3, 4, 2, 1) if i not in taken and sizes[i] >= counts[q, k]]
                if q < 22 and 2 in fits:
                    fits = [i for i in fits if i != 4]
                buffers[q, k] = fits[0]
                distances[q, fits[0]] = k
                taken.add(fits[0])
    starts = [sum(sizes[:k]) for k in range(REACH)]
    return sizes, starts, sum(sizes), buffers, distances


SIZES, STARTS, SPARE, BUFFERS, DISTANCES = packing()


def first_slots(q, free):
    for k in range(REACH):
        slot = STARTS[BUFFERS[0, k]]
        for band in range(1, PARTS):
            if BUFFERS[band, k] != BUFFERS[band - 1, k]:
                slot = jnp.where(q >= band, STARTS[BUFFERS[band, k]], slot)
        free[k] = slot
    free[REACH] = SPARE


def unit_slots(q, a, free):
    first, number = tile_span(q, a)
    at, k = first & (PER - 1), first >> 2
    here = jnp.minimum(PER - at, number)
    rest = number - here
    then = jnp.minimum(rest, PER)
    p0, p1, p2 = free[k], free[k + 1], free[k + 2]
    free[k] = p0 + here
    free[k + 1] = p1 + then
    free[k + 2] = p2 + rest - then
    slots = [p0]
    for i in range(1, PER):
        slots.append(jnp.where(i < here, p0 + i, p1 + i - here))
    slots.append(p1 + PER - here)
    last = jnp.where(here > 1, p1 + PER + 1 - here, p2)
    slots.append(jnp.where(number > PER + 1, last, SPARE))
    return slots, at


def split(x):
    first = x.astype(jnp.bfloat16)
    second = (x - first.astype(jnp.float32)).astype(jnp.bfloat16)
    return first, second


def roll(x, shift):
    return x if isinstance(shift, int) and shift == 0 else pltpu.roll(x, shift, 1)


def merge_groups(groups):
    merged = []
    for upper, lower in zip(groups[0::2], groups[1::2]):
        trials = []
        for e in range(len(upper)):
            trials += [lower[e] + roll(upper[e], e), lower[e] + roll(upper[e], e + 1)]
        merged.append(trials)
    return merged


def put(ref, start, stride, rows):
    for c in range(rows.shape[1] // LANES):
        ref[c, pl.ds(start, 8, stride=stride), :] = rows[:, c * LANES : (c + 1) * LANES]


def take(ref, start, count, first, last):
    chunks = [ref[c, pl.ds(start, count), :] for c in range(first, last)]
    return jnp.concatenate(chunks, axis=1)


def merge_rows(groups, one, two, tiles):
    while len(groups[0]) > 1:
        groups = [merge_groups(beam) for beam in groups]
    for e in range(8):
        for b, beam in enumerate(groups):
            put(one.at[b], e, 8, beam[0][e])
    source, target = one, two
    trials = 8
    while trials < ROWS:
        for base in range(0, ROWS, 2 * trials):
            for a in range(0, trials, 8):
                for b in range(BEAMS):
                    upper = take(source.at[b], base + a, 8, 0, tiles)
                    lower = take(source.at[b], base + trials + a, 8, 0, tiles)
                    early = pltpu.roll(upper, a, 1, stride=1, stride_axis=0)
                    late = pltpu.roll(upper, a + 1, 1, stride=1, stride_axis=0)
                    put(target.at[b], base + 2 * a, 2, lower + early)
                    put(target.at[b], base + 2 * a + 1, 2, lower + late)
        source, target = target, source
        trials *= 2


def local_kernel(
    q_ref,
    scale_hbm,
    x_hbm,
    o0,
    o1,
    o2,
    o3,
    o4,
    free,
    scale,
    x,
    one,
    two,
    packed,
    sems,
):
    half = CHANS // 2
    q = q_ref[0]
    fetch_scale = pltpu.make_async_copy(scale_hbm, scale, sems.at[2 * BEAMS])
    fetch_scale.start()
    fetches = []
    for b in range(BEAMS):
        for h in range(2):
            piece = pl.ds(h * half, half)
            fetches.append(
                pltpu.make_async_copy(
                    x_hbm.at[b, piece], x.at[b, piece], sems.at[2 * b + h]
                )
            )
            fetches[-1].start()
    row = lax.broadcasted_iota(jnp.int32, (ROWS, CHANS), 0)
    col = lax.broadcasted_iota(jnp.int32, (ROWS, CHANS), 1)
    member = (row & 7) * 8 + (row >> 3) == col >> 3
    fetch_scale.wait()
    weights = jnp.where(member, scale[...], 0.0)
    weights = jnp.concatenate(split(weights), axis=0)
    blank = jnp.zeros((8, LANES), jnp.float32)
    for fetch in fetches:
        fetch.wait()
    groups = []
    for b in range(BEAMS):
        base = jnp.dot(weights, x[b], preferred_element_type=jnp.float32)
        base = base[:ROWS] + base[ROWS:]
        groups.append(
            [
                [jnp.concatenate([base[8 * g : 8 * g + 8], blank], axis=1)]
                for g in range(8)
            ]
        )
    merge_rows(groups, one, two, WIDE // LANES)
    first_slots(q, free)
    odd = lax.broadcasted_iota(jnp.int32, (8, UNITS * LANES), 0) & 2 != 0
    for a in range(TILES):
        rows = [take(two.at[b], 4 * a, 4, 0, WIDE // LANES) for b in range(BEAMS)]
        rows = jnp.concatenate([jnp.concatenate(rows, axis=0), blank], axis=1)
        rows = jnp.where(odd, pltpu.roll(rows, 2 * q, 1), rows)
        rows = pltpu.roll(rows, (4 * q * a) & (LANES - 1), 1)
        slots, _ = unit_slots(q, a, free)
        for i, slot in enumerate(slots):
            packed[slot] = rows[:, i * LANES : (i + 1) * LANES]
    for k, out in enumerate((o0, o1, o2, o3, o4)):
        out[...] = packed[pl.ds(STARTS[k], SIZES[k])]


def local_plane(x, scale, q):
    return pl.pallas_call(
        local_kernel,
        in_specs=[
            pl.BlockSpec(memory_space=pltpu.SMEM),
            pl.BlockSpec(memory_space=pltpu.HBM),
            pl.BlockSpec(memory_space=pltpu.HBM),
        ],
        out_shape=[jax.ShapeDtypeStruct((n, 8, LANES), jnp.float32) for n in SIZES],
        scratch_shapes=[
            pltpu.SMEM((REACH + 3,), jnp.int32),
            pltpu.VMEM((1, CHANS), jnp.float32),
            pltpu.VMEM((BEAMS, CHANS, SPAN), jnp.bfloat16),
            pltpu.VMEM((BEAMS, WIDE // LANES, ROWS, LANES), jnp.float32),
            pltpu.VMEM((BEAMS, WIDE // LANES, ROWS, LANES), jnp.float32),
            pltpu.VMEM((SPARE + 1, 8, LANES), jnp.float32),
            pltpu.SemaphoreType.DMA((2 * BEAMS + 1,)),
        ],
        compiler_params=pltpu.CompilerParams(vmem_limit_bytes=24 << 20),
        name="local_plane",
    )(
        q,
        pltpu.with_memory_space_constraint(scale, pltpu.HBM),
        pltpu.with_memory_space_constraint(x, pltpu.HBM),
    )


def gather_kernel(q_ref, o0, r1, r2, r3, r4, out, free, packed, held):
    q = q_ref[0]
    first_slots(q, free)
    for k, piece in enumerate((o0, r1, r2, r3, r4)):
        packed[pl.ds(STARTS[k], SIZES[k])] = piece[...]
    packed[SPARE] = jnp.zeros((8, LANES), jnp.float32)
    for a in range(TILES):
        slots, at = unit_slots(q, a, free)
        rows = pl.ds(8 * a, 8)
        tiles = [(at + i) & (PER - 1) for i in range(PER)]
        held[tiles[0], rows, :] = packed[slots[0]] + packed[slots[PER]]
        held[tiles[1], rows, :] = packed[slots[1]] + packed[slots[PER + 1]]
        held[tiles[2], rows, :] = packed[slots[2]]
        held[tiles[3], rows, :] = packed[slots[3]]
    for c in range(PER):
        for r in range(8):
            b, m, i = r >> 2, r >> 1 & 1, r & 1
            out[pl.ds(m * 16 + b * 8 + c * 2 + i, TILES, stride=32), :] = held[
                c, pl.ds(r, TILES, stride=8), :
            ]


def gather_shifted(pieces, q):
    vmem = pl.BlockSpec(memory_space=pltpu.VMEM)
    return pl.pallas_call(
        gather_kernel,
        in_specs=[pl.BlockSpec(memory_space=pltpu.SMEM)] + [vmem] * REACH,
        out_shape=jax.ShapeDtypeStruct((PARTS * 16, LANES), jnp.float32),
        scratch_shapes=[
            pltpu.SMEM((REACH + 3,), jnp.int32),
            pltpu.VMEM((SPARE + 1, 8, LANES), jnp.float32),
            pltpu.VMEM((PER, 8 * TILES, LANES), jnp.float32),
        ],
        compiler_params=pltpu.CompilerParams(vmem_limit_bytes=24 << 20),
        name="gather_shifted",
    )(q, *pieces)


def final_groups(x_ref, first, last):
    blank = jnp.zeros((8, LANES), jnp.float32)
    beams = []
    for b in range(BEAMS):
        groups = []
        for g in range(4):
            trials = []
            for e in range(2):
                chunks = [
                    x_ref[pl.ds(g * 16 + b * 8 + c * 2 + e, 8, stride=64), :]
                    for c in range(first, last)
                ]
                trials.append(jnp.concatenate(chunks + [blank], axis=1))
            groups.append(trials)
        beams.append(groups)
    return beams


def tail_kernel(x_ref, tail, one, two):
    merge_rows(final_groups(x_ref, PER - 1, PER), one, two, 2)
    lane = lax.broadcasted_iota(jnp.int32, (ROWS, LANES), 1)
    for b in range(BEAMS):
        tail[b] = jnp.where(lane < LANES // 2, two[b, 1], two[b, 0])


def final_tail(x):
    return pl.pallas_call(
        tail_kernel,
        out_shape=jax.ShapeDtypeStruct((BEAMS, ROWS, LANES), jnp.float32),
        scratch_shapes=[
            pltpu.VMEM((BEAMS, 2, ROWS, LANES), jnp.float32),
            pltpu.VMEM((BEAMS, 2, ROWS, LANES), jnp.float32),
        ],
        compiler_params=pltpu.CompilerParams(vmem_limit_bytes=24 << 20),
        name="final_tail",
    )(x)


def boxcar_bands(widths):
    u = lax.broadcasted_iota(jnp.int32, (2 * LANES, LANES), 0)
    t = lax.broadcasted_iota(jnp.int32, (2 * LANES, LANES), 1)
    ago = t + LANES - u
    bands = []
    for k in range(NBOX):
        inside = jnp.logical_and(ago >= 0, ago < widths[k])
        bands.append(jnp.where(inside, 1.0, 0.0).astype(jnp.bfloat16))
    return jnp.concatenate(bands, axis=1)


def boxcar_norms(widths):
    norms = []
    for k in range(NBOX):
        square = jnp.full((1, LANES), widths[k] * (CHANS * PARTS), jnp.int32)
        norms.append(lax.rsqrt(square.astype(jnp.float32)))
    return jnp.concatenate(norms, axis=1)


def boxcar_tile(before, here, bands, norms, held, c):
    window = jnp.concatenate([before, here], axis=1)
    sums = jnp.dot(window, bands, preferred_element_type=jnp.float32)
    rows = BEAMS * ROWS
    sums = (sums[:rows] + sums[rows:]) * norms
    for b in range(BEAMS):
        for k in range(NBOX):
            held[b, k, :, pl.ds(c * LANES, LANES)] = sums[
                b * ROWS : (b + 1) * ROWS, k * LANES : (k + 1) * LANES
            ]


def later_kernel(
    widths, x_ref, out, start, bands_out, norms_out, one, two, held, sems
):
    merge_rows(final_groups(x_ref, 0, PER), one, two, WIDE // LANES)
    bands = boxcar_bands(widths)
    norms = boxcar_norms(widths)
    bands_out[...] = bands
    norms_out[...] = norms
    parts = []
    for c in range(PER):
        tile = jnp.concatenate([two[b, c] for b in range(BEAMS)], axis=0)
        if c == 0:
            start[...] = tile
        parts.append(jnp.concatenate(split(tile), axis=0))
    copies = []
    for c in range(1, PER):
        boxcar_tile(parts[c - 1], parts[c], bands, norms, held, c - 1)
        copies.append(
            pltpu.make_async_copy(
                held.at[:, :, :, pl.ds((c - 1) * LANES, LANES)],
                out.at[:, :, :, pl.ds(c * LANES, LANES)],
                sems.at[c - 1],
            )
        )
        copies[-1].start()
    for copy in copies:
        copy.wait()


def first_kernel(start, tail, bands, norms, rest, out, held, sem):
    del rest
    lane = lax.broadcasted_iota(jnp.int32, (BEAMS * ROWS, LANES), 1)
    edge = tail[...].reshape(BEAMS * ROWS, LANES)
    before = jnp.where(lane >= LANES // 2, edge, 0.0)
    here = start[...] + jnp.where(lane < LANES // 2, edge, 0.0)
    before = jnp.concatenate(split(before), axis=0)
    here = jnp.concatenate(split(here), axis=0)
    boxcar_tile(before, here, bands[...], norms[...], held, 0)
    copy = pltpu.make_async_copy(held, out.at[:, :, :, pl.ds(0, LANES)], sem)
    copy.start()
    copy.wait()


OUT = jax.ShapeDtypeStruct((BEAMS, NBOX, ROWS, SPAN), jnp.float32)


def boxcars_later(x, widths):
    lanes = SPAN - LANES
    vmem = pl.BlockSpec(memory_space=pltpu.VMEM)
    return pl.pallas_call(
        later_kernel,
        in_specs=[pl.BlockSpec(memory_space=pltpu.SMEM), vmem],
        out_specs=[pl.BlockSpec(memory_space=pltpu.HBM), vmem, vmem, vmem],
        out_shape=[
            OUT,
            jax.ShapeDtypeStruct((BEAMS * ROWS, LANES), jnp.float32),
            jax.ShapeDtypeStruct((2 * LANES, NBOX * LANES), jnp.bfloat16),
            jax.ShapeDtypeStruct((1, NBOX * LANES), jnp.float32),
        ],
        scratch_shapes=[
            pltpu.VMEM((BEAMS, WIDE // LANES, ROWS, LANES), jnp.float32),
            pltpu.VMEM((BEAMS, WIDE // LANES, ROWS, LANES), jnp.float32),
            pltpu.VMEM((BEAMS, NBOX, ROWS, lanes), jnp.float32),
            pltpu.SemaphoreType.DMA((lanes // LANES,)),
        ],
        compiler_params=pltpu.CompilerParams(vmem_limit_bytes=24 << 20),
        cost_estimate=pl.CostEstimate(
            flops=2 * 256 * 256 * 768 * 3, bytes_accessed=2 << 20, transcendentals=0
        ),
        name="boxcars_later",
    )(widths, x)


def boxcars_first(start, tail, bands, norms, rest):
    return pl.pallas_call(
        first_kernel,
        in_specs=[pl.BlockSpec(memory_space=pltpu.VMEM)] * 4
        + [pl.BlockSpec(memory_space=pltpu.HBM)],
        out_specs=pl.BlockSpec(memory_space=pltpu.HBM),
        out_shape=OUT,
        input_output_aliases={4: 0},
        scratch_shapes=[
            pltpu.VMEM((BEAMS, NBOX, ROWS, LANES), jnp.float32),
            pltpu.SemaphoreType.DMA,
        ],
        compiler_params=pltpu.CompilerParams(vmem_limit_bytes=24 << 20),
        name="boxcars_first",
    )(start, tail, bands, norms, rest)


def later(block, distances):
    route = []
    for part, distance in enumerate(distances):
        if distance:
            for i in range(SEGMENTS - distance):
                sender = part * SEGMENTS + i
                route.append((sender, sender + distance))
    return lax.ppermute(block, ("chan", "tm"), route)


def per_device(intensity, channel_scale, box_widths):
    q = (PARTS - 1 - lax.axis_index("chan")).astype(jnp.int32).reshape(1)
    pieces = list(local_plane(intensity, channel_scale.reshape(1, CHANS), q))
    for k in range(REACH - 1, 0, -1):
        pieces[k] = later(pieces[k], DISTANCES[::-1, k].tolist())
    lined = gather_shifted(pieces, q)
    lined = lax.all_to_all(lined, "chan", 0, 0, tiled=True)
    tail = later(final_tail(lined), [1] * PARTS)
    rest, start, bands, norms = boxcars_later(lined, box_widths)
    return boxcars_first(start, tail, bands, norms, rest)


def solution(mesh):
    in_specs = (P(None, "chan", "tm"), P("chan"), P())
    out_specs = P(None, None, "chan", "tm")
    return jax.shard_map(
        per_device, mesh=mesh, in_specs=in_specs, out_specs=out_specs, check_vma=False
    )
```

```python
import jax
import jax.numpy as jnp
import numpy as np
from jax import lax
from jax.experimental import pallas as pl
from jax.experimental.pallas import tpu as pltpu
from jax.sharding import PartitionSpec as P

BEAMS = 2
CHANS = 512
SPAN = 512
PARTS = 32
SEGMENTS = 8
ROWS = 64
WIDE = SPAN + 128
NBOX = 6
LANES = 128
REACH = 6
TILES = 16
UNITS = 6
PER = SPAN // LANES
BLOCK = 24


def tails(a):
    reach = [sum((i >> level) + 1 >> 1 for level in range(6)) for i in range(4 * a, 4 * a + 4)]
    return max(reach[:2]), max(reach[2:])


def tile_span(q, a):
    delay = 4 * q * a
    first, second = tails(a)
    within = delay & (LANES - 1)
    end = within + SPAN + (max if isinstance(q, int) else jnp.maximum)(first, 2 * q + second)
    tile = delay >> 7
    far = (tile & (PER - 1)) * LANES + end > 2 * SPAN - (2 * q + 63)
    return tile, (end + LANES - 1) >> 7, far


def group_shares(q, a, least=min):
    tile, number, far = tile_span(q, a)
    at = tile & (PER - 1)
    here = PER - at
    then = least(number - here, PER)
    over = number - here - then
    return tile >> 2, at, number, far, (here, 1 + then, over + far)


def packing():
    counts = np.zeros((PARTS, REACH), np.int32)
    for q in range(PARTS):
        for a in range(TILES):
            k, _, _, _, shares = group_shares(q, a)
            for i, share in enumerate(shares):
                if share:
                    counts[q, k + i] += share
    sizes = [64, 60, 38, 29, 15, 1]
    buffers = np.zeros((PARTS, REACH), np.int32)
    distances = np.zeros((PARTS, REACH), np.int32)
    for q in range(PARTS):
        taken = {0}
        for k in range(REACH - 1, 0, -1):
            if counts[q, k]:
                allowed = (k,) if q >= 22 else (4, 2, 1)
                fits = [i for i in allowed if i not in taken and sizes[i] >= counts[q, k]]
                buffers[q, k] = fits[0]
                distances[q, fits[0]] = k
                taken.add(fits[0])
    starts = [sum(sizes[:k]) for k in range(REACH)]
    return sizes, starts, sum(sizes), buffers, distances


SIZES, STARTS, SPARE, BUFFERS, DISTANCES = packing()


def first_slots(q, free):
    for k in range(REACH):
        slot = STARTS[BUFFERS[0, k]]
        for band in range(1, PARTS):
            if BUFFERS[band, k] != BUFFERS[band - 1, k]:
                slot = jnp.where(q >= band, STARTS[BUFFERS[band, k]], slot)
        free[k] = slot


def unit_slots(q, a, free):
    k, at, number, far, shares = group_shares(q, a, jnp.minimum)
    here = shares[0]
    p0, p1, p2 = free[k], free[k + 1], free[k + 2]
    free[k] = p0 + here
    free[k + 1] = p1 + shares[1]
    free[k + 2] = p2 + shares[2]
    slots = [p0]
    for i in range(1, PER):
        slots.append(jnp.where(i < here, p0 + i, p1 + 1 + i - here))
    slots.append(p1 + 1 + PER - here)
    last = jnp.where(here > 1, p1 + PER + 2 - here, p2 + 1)
    slots.append(jnp.where(number > PER + 1, last, SPARE))
    again = (p1, p0 + here - 1), (jnp.where(far, p2, SPARE), jnp.where(far, p1 + PER, SPARE))
    return slots, at, again


def split(x):
    first = x.astype(jnp.bfloat16)
    second = (x - first.astype(jnp.float32)).astype(jnp.bfloat16)
    return first, second


def roll(x, shift):
    return x if isinstance(shift, int) and shift == 0 else pltpu.roll(x, shift, 1)


def merge_groups(groups):
    merged = []
    for upper, lower in zip(groups[0::2], groups[1::2]):
        trials = []
        for e in range(len(upper)):
            trials += [lower[e] + roll(upper[e], e), lower[e] + roll(upper[e], e + 1)]
        merged.append(trials)
    return merged


def put(ref, start, stride, rows):
    for c in range(rows.shape[1] // LANES):
        ref[c, pl.ds(start, 8, stride=stride), :] = rows[:, c * LANES : (c + 1) * LANES]


def take(ref, start, count, first, last):
    chunks = [ref[c, pl.ds(start, count), :] for c in range(first, last)]
    return jnp.concatenate(chunks, axis=1)


def merge_rows(groups, one, two, tiles):
    while len(groups[0]) > 1:
        groups = [merge_groups(beam) for beam in groups]
    for e in range(8):
        for b, beam in enumerate(groups):
            put(one.at[b], e, 8, beam[0][e])
    source, target = one, two
    trials = 8
    while trials < ROWS:
        for base in range(0, ROWS, 2 * trials):
            for a in range(0, trials, 8):
                for b in range(BEAMS):
                    upper = take(source.at[b], base + a, 8, 0, tiles)
                    lower = take(source.at[b], base + trials + a, 8, 0, tiles)
                    early = pltpu.roll(upper, a, 1, stride=1, stride_axis=0)
                    late = pltpu.roll(upper, a + 1, 1, stride=1, stride_axis=0)
                    put(target.at[b], base + 2 * a, 2, lower + early)
                    put(target.at[b], base + 2 * a + 1, 2, lower + late)
        source, target = target, source
        trials *= 2


def local_kernel(
    q_ref,
    scale_hbm,
    x_hbm,
    o0,
    o1,
    o2,
    o3,
    o4,
    o5,
    free,
    scale,
    x,
    one,
    two,
    packed,
    sems,
):
    half = CHANS // 2
    q = q_ref[0]
    fetch_scale = pltpu.make_async_copy(scale_hbm, scale, sems.at[2 * BEAMS])
    fetch_scale.start()
    fetches = []
    for b in range(BEAMS):
        for h in range(2):
            piece = pl.ds(h * half, half)
            fetches.append(
                pltpu.make_async_copy(
                    x_hbm.at[b, piece], x.at[b, piece], sems.at[2 * b + h]
                )
            )
            fetches[-1].start()
    row = lax.broadcasted_iota(jnp.int32, (ROWS, CHANS), 0)
    col = lax.broadcasted_iota(jnp.int32, (ROWS, CHANS), 1)
    member = (row & 7) * 8 + (row >> 3) == col >> 3
    fetch_scale.wait()
    weights = jnp.where(member, scale[...], 0.0)
    weights = jnp.concatenate(split(weights), axis=0)
    blank = jnp.zeros((8, LANES), jnp.float32)
    for fetch in fetches:
        fetch.wait()
    groups = []
    for b in range(BEAMS):
        base = jnp.dot(weights, x[b], preferred_element_type=jnp.float32)
        base = base[:ROWS] + base[ROWS:]
        groups.append(
            [
                [jnp.concatenate([base[8 * g : 8 * g + 8], blank], axis=1)]
                for g in range(8)
            ]
        )
    merge_rows(groups, one, two, WIDE // LANES)
    first_slots(q, free)
    odd = lax.broadcasted_iota(jnp.int32, (8, UNITS * LANES), 0) & 2 != 0
    for a in range(TILES):
        rows = [take(two.at[b], 4 * a, 4, 0, WIDE // LANES) for b in range(BEAMS)]
        rows = jnp.concatenate([jnp.concatenate(rows, axis=0), blank], axis=1)
        rows = jnp.where(odd, pltpu.roll(rows, 2 * q, 1), rows)
        rows = pltpu.roll(rows, (4 * q * a) & (LANES - 1), 1)
        slots, _, again = unit_slots(q, a, free)
        for i, slot in enumerate(slots):
            packed[slot] = rows[:, i * LANES : (i + 1) * LANES]
        for slot, origin in again:
            packed[slot] = packed[origin]
    for k, out in enumerate((o0, o1, o2, o3, o4, o5)):
        out[...] = packed[pl.ds(STARTS[k], SIZES[k])]


def local_plane(x, scale, q):
    return pl.pallas_call(
        local_kernel,
        in_specs=[
            pl.BlockSpec(memory_space=pltpu.SMEM),
            pl.BlockSpec(memory_space=pltpu.HBM),
            pl.BlockSpec(memory_space=pltpu.HBM),
        ],
        out_shape=[jax.ShapeDtypeStruct((n, 8, LANES), jnp.float32) for n in SIZES],
        scratch_shapes=[
            pltpu.SMEM((REACH + 2,), jnp.int32),
            pltpu.VMEM((1, CHANS), jnp.float32),
            pltpu.VMEM((BEAMS, CHANS, SPAN), jnp.bfloat16),
            pltpu.VMEM((BEAMS, WIDE // LANES, ROWS, LANES), jnp.float32),
            pltpu.VMEM((BEAMS, WIDE // LANES, ROWS, LANES), jnp.float32),
            pltpu.VMEM((SPARE + 1, 8, LANES), jnp.float32),
            pltpu.SemaphoreType.DMA((2 * BEAMS + 1,)),
        ],
        compiler_params=pltpu.CompilerParams(vmem_limit_bytes=24 << 20),
        name="local_plane",
    )(
        q,
        pltpu.with_memory_space_constraint(scale, pltpu.HBM),
        pltpu.with_memory_space_constraint(x, pltpu.HBM),
    )


def gather_kernel(q_ref, o0, r1, r2, r3, r4, r5, out, free, packed, held):
    q = q_ref[0]
    first_slots(q, free)
    for k, piece in enumerate((o0, r1, r2, r3, r4, r5)):
        packed[pl.ds(STARTS[k], SIZES[k])] = piece[...]
    packed[SPARE] = jnp.zeros((8, LANES), jnp.float32)
    for a in range(TILES):
        slots, at, again = unit_slots(q, a, free)
        rows = pl.ds(8 * a, 8)
        tiles = [1 + ((at + i) & (PER - 1)) for i in range(PER)]
        held[0, rows, :] = packed[again[0][0]] + packed[again[1][0]]
        held[tiles[0], rows, :] = packed[slots[0]] + packed[slots[PER]]
        held[tiles[1], rows, :] = packed[slots[1]] + packed[slots[PER + 1]]
        held[tiles[2], rows, :] = packed[slots[2]]
        held[tiles[3], rows, :] = packed[slots[3]]
    for c in range(WIDE // LANES):
        for r in range(8):
            b, m, i = r >> 2, r >> 1 & 1, r & 1
            out[pl.ds(m * BLOCK + c * 4 + b * 2 + i, TILES, stride=2 * BLOCK), :] = held[
                c, pl.ds(r, TILES, stride=8), :
            ]


def gather_shifted(pieces, q):
    vmem = pl.BlockSpec(memory_space=pltpu.VMEM)
    return pl.pallas_call(
        gather_kernel,
        in_specs=[pl.BlockSpec(memory_space=pltpu.SMEM)] + [vmem] * REACH,
        out_shape=jax.ShapeDtypeStruct((PARTS * BLOCK, LANES), jnp.float32),
        scratch_shapes=[
            pltpu.SMEM((REACH + 2,), jnp.int32),
            pltpu.VMEM((SPARE + 1, 8, LANES), jnp.float32),
            pltpu.VMEM((WIDE // LANES, 8 * TILES, LANES), jnp.float32),
        ],
        compiler_params=pltpu.CompilerParams(vmem_limit_bytes=24 << 20),
        name="gather_shifted",
    )(q, *pieces)


def final_groups(x_ref):
    beams = []
    for b in range(BEAMS):
        groups = []
        for g in range(4):
            trials = []
            for e in range(2):
                chunks = [
                    x_ref[pl.ds(g * BLOCK + c * 4 + b * 2 + e, 8, stride=4 * BLOCK), :]
                    for c in range(WIDE // LANES)
                ]
                trials.append(jnp.concatenate(chunks, axis=1))
            groups.append(trials)
        beams.append(groups)
    return beams


def boxcar_bands(widths):
    u = lax.broadcasted_iota(jnp.int32, (2 * LANES, LANES), 0)
    t = lax.broadcasted_iota(jnp.int32, (2 * LANES, LANES), 1)
    ago = t + LANES - u
    bands = []
    for k in range(NBOX):
        inside = jnp.logical_and(ago >= 0, ago < widths[k])
        bands.append(jnp.where(inside, 1.0, 0.0).astype(jnp.bfloat16))
    return jnp.concatenate(bands, axis=1)


def boxcar_norms(widths):
    norms = []
    for k in range(NBOX):
        square = jnp.full((1, LANES), widths[k] * (CHANS * PARTS), jnp.int32)
        norms.append(lax.rsqrt(square.astype(jnp.float32)))
    return jnp.concatenate(norms, axis=1)


def boxcar_tile(before, here, bands, norms, held, c):
    window = jnp.concatenate([before, here], axis=1)
    sums = jnp.dot(window, bands, preferred_element_type=jnp.float32)
    rows = BEAMS * ROWS
    sums = (sums[:rows] + sums[rows:]) * norms
    for b in range(BEAMS):
        for k in range(NBOX):
            held[b, k, :, pl.ds(c * LANES, LANES)] = sums[
                b * ROWS : (b + 1) * ROWS, k * LANES : (k + 1) * LANES
            ]


def final_kernel(widths, x_ref, out, one, two, held, sems):
    merge_rows(final_groups(x_ref), one, two, WIDE // LANES)
    bands = boxcar_bands(widths)
    norms = boxcar_norms(widths)
    parts = []
    for c in range(WIDE // LANES):
        tile = jnp.concatenate([two[b, c] for b in range(BEAMS)], axis=0)
        parts.append(jnp.concatenate(split(tile), axis=0))
    copies = []
    for c in range(PER):
        boxcar_tile(parts[c], parts[c + 1], bands, norms, held, c)
        lanes = pl.ds(c * LANES, LANES)
        copies.append(
            pltpu.make_async_copy(
                held.at[:, :, :, lanes], out.at[:, :, :, lanes], sems.at[c]
            )
        )
        copies[-1].start()
    for copy in copies:
        copy.wait()


def final_boxcars(x, widths):
    return pl.pallas_call(
        final_kernel,
        in_specs=[
            pl.BlockSpec(memory_space=pltpu.SMEM),
            pl.BlockSpec(memory_space=pltpu.VMEM),
        ],
        out_specs=pl.BlockSpec(memory_space=pltpu.HBM),
        out_shape=jax.ShapeDtypeStruct((BEAMS, NBOX, ROWS, SPAN), jnp.float32),
        scratch_shapes=[
            pltpu.VMEM((BEAMS, WIDE // LANES, ROWS, LANES), jnp.float32),
            pltpu.VMEM((BEAMS, WIDE // LANES, ROWS, LANES), jnp.float32),
            pltpu.VMEM((BEAMS, NBOX, ROWS, SPAN), jnp.float32),
            pltpu.SemaphoreType.DMA((PER,)),
        ],
        compiler_params=pltpu.CompilerParams(vmem_limit_bytes=24 << 20),
        name="final_boxcars",
    )(widths, x)


def later(block, distances):
    route = []
    for part, distance in enumerate(distances):
        if distance:
            for i in range(SEGMENTS - distance):
                sender = part * SEGMENTS + i
                route.append((sender, sender + distance))
    return lax.ppermute(block, ("chan", "tm"), route)


def per_device(intensity, channel_scale, box_widths):
    q = (PARTS - 1 - lax.axis_index("chan")).astype(jnp.int32).reshape(1)
    pieces = list(local_plane(intensity, channel_scale.reshape(1, CHANS), q))
    for k in range(REACH - 1, 0, -1):
        pieces[k] = later(pieces[k], DISTANCES[::-1, k].tolist())
    lined = gather_shifted(pieces, q)
    lined = lax.all_to_all(lined, "chan", 0, 0, tiled=True)
    return final_boxcars(lined, box_widths)


def solution(mesh):
    in_specs = (P(None, "chan", "tm"), P("chan"), P())
    out_specs = P(None, None, "chan", "tm")
    return jax.shard_map(
        per_device, mesh=mesh, in_specs=in_specs, out_specs=out_specs, check_vma=False
    )
```

```python
import jax
import jax.numpy as jnp
import numpy as np
from jax import lax
from jax.experimental import pallas as pl
from jax.experimental.pallas import tpu as pltpu
from jax.sharding import PartitionSpec as P

BEAMS = 2
CHANS = 512
SPAN = 512
PARTS = 32
SEGMENTS = 8
ROWS = 64
WIDE = SPAN + 128
NBOX = 6
LANES = 128
REACH = 6
TILES = 16
UNITS = 6
PER = SPAN // LANES
BLOCK = 20


def tails(a):
    reach = [sum((i >> level) + 1 >> 1 for level in range(6)) for i in range(4 * a, 4 * a + 4)]
    return max(reach[:2]), max(reach[2:])


def tile_span(q, a):
    delay = 4 * q * a
    first, second = tails(a)
    within = delay & (LANES - 1)
    end = within + SPAN + (max if isinstance(q, int) else jnp.maximum)(first, 2 * q + second)
    tile = delay >> 7
    far = (tile & (PER - 1)) * LANES + end > 2 * SPAN - (2 * q + 63)
    return tile, (end + LANES - 1) >> 7, far


def group_shares(q, a, least=min):
    tile, number, far = tile_span(q, a)
    at = tile & (PER - 1)
    here = PER - at
    then = least(number - here, PER)
    over = number - here - then
    return tile >> 2, at, number, far, (here, 1 + then, over + far)


def packing():
    counts = np.zeros((PARTS, REACH), np.int32)
    for q in range(PARTS):
        for a in range(TILES):
            k, _, _, _, shares = group_shares(q, a)
            for i, share in enumerate(shares):
                if share:
                    counts[q, k + i] += share
    sizes = [64, 60, 38, 29, 15, 1]
    buffers = np.zeros((PARTS, REACH), np.int32)
    distances = np.zeros((PARTS, REACH), np.int32)
    for q in range(PARTS):
        taken = {0}
        for k in range(REACH - 1, 0, -1):
            if counts[q, k]:
                allowed = (k,) if q >= 22 else (4, 2, 1)
                fits = [i for i in allowed if i not in taken and sizes[i] >= counts[q, k]]
                buffers[q, k] = fits[0]
                distances[q, fits[0]] = k
                taken.add(fits[0])
    starts = [sum(sizes[:k]) for k in range(REACH)]
    return sizes, starts, sum(sizes), buffers, distances


SIZES, STARTS, SPARE, BUFFERS, DISTANCES = packing()


def first_slots(q, free):
    for k in range(REACH):
        slot = STARTS[BUFFERS[0, k]]
        for band in range(1, PARTS):
            if BUFFERS[band, k] != BUFFERS[band - 1, k]:
                slot = jnp.where(q >= band, STARTS[BUFFERS[band, k]], slot)
        free[k] = slot


def unit_slots(q, a, free):
    k, at, number, far, shares = group_shares(q, a, jnp.minimum)
    here = shares[0]
    p0, p1, p2 = free[k], free[k + 1], free[k + 2]
    free[k] = p0 + here
    free[k + 1] = p1 + shares[1]
    free[k + 2] = p2 + shares[2]
    slots = [p0]
    for i in range(1, PER):
        slots.append(jnp.where(i < here, p0 + i, p1 + 1 + i - here))
    slots.append(p1 + 1 + PER - here)
    last = jnp.where(here > 1, p1 + PER + 2 - here, p2 + 1)
    slots.append(jnp.where(number > PER + 1, last, SPARE))
    again = (p1, p0 + here - 1), (jnp.where(far, p2, SPARE), jnp.where(far, p1 + PER, SPARE))
    return slots, at, again


def split(x):
    first = x.astype(jnp.bfloat16)
    second = (x - first.astype(jnp.float32)).astype(jnp.bfloat16)
    return first, second


def roll(x, shift):
    return x if isinstance(shift, int) and shift == 0 else pltpu.roll(x, shift, 1)


def merge_groups(groups):
    merged = []
    for upper, lower in zip(groups[0::2], groups[1::2]):
        trials = []
        for e in range(len(upper)):
            trials += [lower[e] + roll(upper[e], e), lower[e] + roll(upper[e], e + 1)]
        merged.append(trials)
    return merged


def put(ref, start, stride, rows):
    for c in range(rows.shape[1] // LANES):
        ref[c, pl.ds(start, 8, stride=stride), :] = rows[:, c * LANES : (c + 1) * LANES]


def take(ref, start, count, first, last):
    chunks = [ref[c, pl.ds(start, count), :] for c in range(first, last)]
    return jnp.concatenate(chunks, axis=1)


def merge_rows(groups, one, two, tiles):
    while len(groups[0]) > 1:
        groups = [merge_groups(beam) for beam in groups]
    for e in range(8):
        for b, beam in enumerate(groups):
            put(one.at[b], e, 8, beam[0][e])
    source, target = one, two
    trials = 8
    while trials < ROWS:
        for base in range(0, ROWS, 2 * trials):
            for a in range(0, trials, 8):
                for b in range(BEAMS):
                    upper = take(source.at[b], base + a, 8, 0, tiles)
                    lower = take(source.at[b], base + trials + a, 8, 0, tiles)
                    early = pltpu.roll(upper, a, 1, stride=1, stride_axis=0)
                    late = pltpu.roll(upper, a + 1, 1, stride=1, stride_axis=0)
                    put(target.at[b], base + 2 * a, 2, lower + early)
                    put(target.at[b], base + 2 * a + 1, 2, lower + late)
        source, target = target, source
        trials *= 2


def local_kernel(
    q_ref,
    scale_hbm,
    x_hbm,
    o0,
    o1,
    o2,
    o3,
    o4,
    o5,
    free,
    scale,
    x,
    one,
    two,
    packed,
    sems,
):
    half = CHANS // 2
    q = q_ref[0]
    fetch_scale = pltpu.make_async_copy(scale_hbm, scale, sems.at[2 * BEAMS])
    fetch_scale.start()
    fetches = []
    for b in range(BEAMS):
        for h in range(2):
            piece = pl.ds(h * half, half)
            fetches.append(
                pltpu.make_async_copy(
                    x_hbm.at[b, piece], x.at[b, piece], sems.at[2 * b + h]
                )
            )
            fetches[-1].start()
    row = lax.broadcasted_iota(jnp.int32, (ROWS, CHANS), 0)
    col = lax.broadcasted_iota(jnp.int32, (ROWS, CHANS), 1)
    member = (row & 7) * 8 + (row >> 3) == col >> 3
    fetch_scale.wait()
    weights = jnp.where(member, scale[...], 0.0)
    weights = jnp.concatenate(split(weights), axis=0)
    blank = jnp.zeros((8, LANES), jnp.float32)
    for fetch in fetches:
        fetch.wait()
    groups = []
    for b in range(BEAMS):
        base = jnp.dot(weights, x[b], preferred_element_type=jnp.float32)
        base = base[:ROWS] + base[ROWS:]
        groups.append(
            [
                [jnp.concatenate([base[8 * g : 8 * g + 8], blank], axis=1)]
                for g in range(8)
            ]
        )
    merge_rows(groups, one, two, WIDE // LANES)
    first_slots(q, free)
    odd = lax.broadcasted_iota(jnp.int32, (8, UNITS * LANES), 0) & 2 != 0
    for a in range(TILES):
        rows = [take(two.at[b], 4 * a, 4, 0, WIDE // LANES) for b in range(BEAMS)]
        rows = jnp.concatenate([jnp.concatenate(rows, axis=0), blank], axis=1)
        rows = jnp.where(odd, pltpu.roll(rows, 2 * q, 1), rows)
        rows = pltpu.roll(rows, (4 * q * a) & (LANES - 1), 1)
        slots, _, again = unit_slots(q, a, free)
        for i, slot in enumerate(slots):
            packed[slot] = rows[:, i * LANES : (i + 1) * LANES]
        for slot, origin in again:
            packed[slot] = packed[origin]
    for k, out in enumerate((o0, o1, o2, o3, o4, o5)):
        out[...] = packed[pl.ds(STARTS[k], SIZES[k])]


def local_plane(x, scale, q):
    return pl.pallas_call(
        local_kernel,
        in_specs=[
            pl.BlockSpec(memory_space=pltpu.SMEM),
            pl.BlockSpec(memory_space=pltpu.HBM),
            pl.BlockSpec(memory_space=pltpu.HBM),
        ],
        out_shape=[jax.ShapeDtypeStruct((n, 8, LANES), jnp.float32) for n in SIZES],
        scratch_shapes=[
            pltpu.SMEM((REACH + 2,), jnp.int32),
            pltpu.VMEM((1, CHANS), jnp.float32),
            pltpu.VMEM((BEAMS, CHANS, SPAN), jnp.bfloat16),
            pltpu.VMEM((BEAMS, WIDE // LANES, ROWS, LANES), jnp.float32),
            pltpu.VMEM((BEAMS, WIDE // LANES, ROWS, LANES), jnp.float32),
            pltpu.VMEM((SPARE + 1, 8, LANES), jnp.float32),
            pltpu.SemaphoreType.DMA((2 * BEAMS + 1,)),
        ],
        compiler_params=pltpu.CompilerParams(vmem_limit_bytes=24 << 20),
        name="local_plane",
    )(
        q,
        pltpu.with_memory_space_constraint(scale, pltpu.HBM),
        pltpu.with_memory_space_constraint(x, pltpu.HBM),
    )


def gather_kernel(q_ref, o0, r1, r2, r3, r4, r5, out, free, packed, held):
    q = q_ref[0]
    first_slots(q, free)
    for k, piece in enumerate((o0, r1, r2, r3, r4, r5)):
        packed[pl.ds(STARTS[k], SIZES[k])] = piece[...]
    packed[SPARE] = jnp.zeros((8, LANES), jnp.float32)
    for a in range(TILES):
        slots, at, again = unit_slots(q, a, free)
        rows = pl.ds(8 * a, 8)
        tiles = [1 + ((at + i) & (PER - 1)) for i in range(PER)]
        held[0, rows, :] = packed[again[0][0]] + packed[again[1][0]]
        held[tiles[0], rows, :] = packed[slots[0]] + packed[slots[PER]]
        held[tiles[1], rows, :] = packed[slots[1]] + packed[slots[PER + 1]]
        held[tiles[2], rows, :] = packed[slots[2]]
        held[tiles[3], rows, :] = packed[slots[3]]
    for c in range(WIDE // LANES):
        for r in range(8):
            b, m, i = r >> 2, r >> 1 & 1, r & 1
            out[pl.ds(m * BLOCK + c * 4 + b * 2 + i, TILES, stride=2 * BLOCK), :] = held[
                c, pl.ds(r, TILES, stride=8), :
            ]


def gather_shifted(pieces, q):
    vmem = pl.BlockSpec(memory_space=pltpu.VMEM)
    return pl.pallas_call(
        gather_kernel,
        in_specs=[pl.BlockSpec(memory_space=pltpu.SMEM)] + [vmem] * REACH,
        out_shape=jax.ShapeDtypeStruct((PARTS * BLOCK, LANES), jnp.float32),
        scratch_shapes=[
            pltpu.SMEM((REACH + 2,), jnp.int32),
            pltpu.VMEM((SPARE + 1, 8, LANES), jnp.float32),
            pltpu.VMEM((WIDE // LANES, 8 * TILES, LANES), jnp.float32),
        ],
        compiler_params=pltpu.CompilerParams(vmem_limit_bytes=24 << 20),
        name="gather_shifted",
    )(q, *pieces)


def final_groups(x_ref):
    beams = []
    for b in range(BEAMS):
        groups = []
        for g in range(4):
            trials = []
            for e in range(2):
                chunks = [
                    x_ref[pl.ds(g * BLOCK + c * 4 + b * 2 + e, 8, stride=4 * BLOCK), :]
                    for c in range(WIDE // LANES)
                ]
                trials.append(jnp.concatenate(chunks, axis=1))
            groups.append(trials)
        beams.append(groups)
    return beams


def boxcar_bands(widths):
    u = lax.broadcasted_iota(jnp.int32, (2 * LANES, LANES), 0)
    t = lax.broadcasted_iota(jnp.int32, (2 * LANES, LANES), 1)
    ago = t + LANES - u
    bands = []
    for k in range(NBOX):
        inside = jnp.logical_and(ago >= 0, ago < widths[k])
        bands.append(jnp.where(inside, 1.0, 0.0).astype(jnp.bfloat16))
    return jnp.concatenate(bands, axis=1)


def boxcar_norms(widths):
    norms = []
    for k in range(NBOX):
        square = jnp.full((1, LANES), widths[k] * (CHANS * PARTS), jnp.int32)
        norms.append(lax.rsqrt(square.astype(jnp.float32)))
    return jnp.concatenate(norms, axis=1)


def boxcar_tile(before, here, bands, norms, held, c):
    window = jnp.concatenate([before, here], axis=1)
    sums = jnp.dot(window, bands, preferred_element_type=jnp.float32)
    rows = BEAMS * ROWS
    sums = (sums[:rows] + sums[rows:]) * norms
    for b in range(BEAMS):
        for k in range(NBOX):
            held[b, k, :, pl.ds(c * LANES, LANES)] = sums[
                b * ROWS : (b + 1) * ROWS, k * LANES : (k + 1) * LANES
            ]


def final_kernel(widths, x_ref, out, one, two, held, sems):
    merge_rows(final_groups(x_ref), one, two, WIDE // LANES)
    bands = boxcar_bands(widths)
    norms = boxcar_norms(widths)
    parts = []
    for c in range(WIDE // LANES):
        tile = jnp.concatenate([two[b, c] for b in range(BEAMS)], axis=0)
        parts.append(jnp.concatenate(split(tile), axis=0))
    copies = []
    for c in range(PER):
        boxcar_tile(parts[c], parts[c + 1], bands, norms, held, c)
        lanes = pl.ds(c * LANES, LANES)
        copies.append(
            pltpu.make_async_copy(
                held.at[:, :, :, lanes], out.at[:, :, :, lanes], sems.at[c]
            )
        )
        copies[-1].start()
    for copy in copies:
        copy.wait()


def final_boxcars(x, widths):
    return pl.pallas_call(
        final_kernel,
        in_specs=[
            pl.BlockSpec(memory_space=pltpu.SMEM),
            pl.BlockSpec(memory_space=pltpu.VMEM),
        ],
        out_specs=pl.BlockSpec(memory_space=pltpu.HBM),
        out_shape=jax.ShapeDtypeStruct((BEAMS, NBOX, ROWS, SPAN), jnp.float32),
        scratch_shapes=[
            pltpu.VMEM((BEAMS, WIDE // LANES, ROWS, LANES), jnp.float32),
            pltpu.VMEM((BEAMS, WIDE // LANES, ROWS, LANES), jnp.float32),
            pltpu.VMEM((BEAMS, NBOX, ROWS, SPAN), jnp.float32),
            pltpu.SemaphoreType.DMA((PER,)),
        ],
        compiler_params=pltpu.CompilerParams(vmem_limit_bytes=24 << 20),
        name="final_boxcars",
    )(widths, x)


def later(block, distances):
    route = []
    for part, distance in enumerate(distances):
        if distance:
            for i in range(SEGMENTS - distance):
                sender = part * SEGMENTS + i
                route.append((sender, sender + distance))
    return lax.ppermute(block, ("chan", "tm"), route)


def per_device(intensity, channel_scale, box_widths):
    q = (PARTS - 1 - lax.axis_index("chan")).astype(jnp.int32).reshape(1)
    pieces = list(local_plane(intensity, channel_scale.reshape(1, CHANS), q))
    for k in range(REACH - 1, 0, -1):
        pieces[k] = later(pieces[k], DISTANCES[::-1, k].tolist())
    lined = gather_shifted(pieces, q)
    lined = lined.reshape(PARTS, 1, BLOCK * LANES)
    lined = lax.all_to_all(lined, "chan", 0, 0, tiled=True)
    lined = lined.reshape(PARTS * BLOCK, LANES)
    return final_boxcars(lined, box_widths)


def solution(mesh):
    in_specs = (P(None, "chan", "tm"), P("chan"), P())
    out_specs = P(None, None, "chan", "tm")
    return jax.shard_map(
        per_device, mesh=mesh, in_specs=in_specs, out_specs=out_specs, check_vma=False
    )
```

```python
import jax
import jax.numpy as jnp
import numpy as np
from jax import lax
from jax.experimental import pallas as pl
from jax.experimental.pallas import tpu as pltpu
from jax.sharding import PartitionSpec as P

BEAMS = 2
CHANS = 512
SPAN = 512
PARTS = 32
SEGMENTS = 8
ROWS = 64
WIDE = SPAN + 128
NBOX = 6
LANES = 128
REACH = 6
TILES = 16
UNITS = 6
PER = SPAN // LANES
BLOCK = 10
TOP = 32000.0


def tails(a):
    reach = [sum((i >> level) + 1 >> 1 for level in range(6)) for i in range(4 * a, 4 * a + 4)]
    return max(reach[:2]), max(reach[2:])


def tile_span(q, a):
    delay = 4 * q * a
    first, second = tails(a)
    within = delay & (LANES - 1)
    end = within + SPAN + (max if isinstance(q, int) else jnp.maximum)(first, 2 * q + second)
    tile = delay >> 7
    far = (tile & (PER - 1)) * LANES + end > 2 * SPAN - (2 * q + 63)
    return tile, (end + LANES - 1) >> 7, far


def group_shares(q, a, least=min):
    tile, number, far = tile_span(q, a)
    at = tile & (PER - 1)
    here = PER - at
    then = least(number - here, PER)
    over = number - here - then
    return tile >> 2, at, number, far, (here, 1 + then, over + far)


def packing():
    counts = np.zeros((PARTS, REACH), np.int32)
    for q in range(PARTS):
        for a in range(TILES):
            k, _, _, _, shares = group_shares(q, a)
            for i, share in enumerate(shares):
                if share:
                    counts[q, k + i] += share
    sizes = [64, 60, 38, 29, 15, 1]
    buffers = np.zeros((PARTS, REACH), np.int32)
    distances = np.zeros((PARTS, REACH), np.int32)
    for q in range(PARTS):
        taken = {0}
        for k in range(REACH - 1, 0, -1):
            if counts[q, k]:
                allowed = (k,) if q >= 22 else (4, 2, 1)
                fits = [i for i in allowed if i not in taken and sizes[i] >= counts[q, k]]
                buffers[q, k] = fits[0]
                distances[q, fits[0]] = k
                taken.add(fits[0])
    starts = [sum(sizes[:k]) for k in range(REACH)]
    return sizes, starts, sum(sizes), buffers, distances


SIZES, STARTS, SPARE, BUFFERS, DISTANCES = packing()


def first_slots(q, free):
    for k in range(REACH):
        slot = STARTS[BUFFERS[0, k]]
        for band in range(1, PARTS):
            if BUFFERS[band, k] != BUFFERS[band - 1, k]:
                slot = jnp.where(q >= band, STARTS[BUFFERS[band, k]], slot)
        free[k] = slot


def unit_slots(q, a, free):
    k, at, number, far, shares = group_shares(q, a, jnp.minimum)
    here = shares[0]
    p0, p1, p2 = free[k], free[k + 1], free[k + 2]
    free[k] = p0 + here
    free[k + 1] = p1 + shares[1]
    free[k + 2] = p2 + shares[2]
    slots = [p0]
    for i in range(1, PER):
        slots.append(jnp.where(i < here, p0 + i, p1 + 1 + i - here))
    slots.append(p1 + 1 + PER - here)
    last = jnp.where(here > 1, p1 + PER + 2 - here, p2 + 1)
    slots.append(jnp.where(number > PER + 1, last, SPARE))
    again = (p1, p0 + here - 1), (jnp.where(far, p2, SPARE), jnp.where(far, p1 + PER, SPARE))
    return slots, at, again


def split(x):
    first = x.astype(jnp.bfloat16)
    second = (x - first.astype(jnp.float32)).astype(jnp.bfloat16)
    return first, second


def exponent_of(largest):
    return jnp.floor(64.0 * jnp.log2(jnp.maximum(largest, 1e-36))).astype(jnp.int32) + 2


def largest_of(tiles):
    top = jnp.abs(tiles[0])
    for tile in tiles[1:]:
        top = jnp.maximum(top, jnp.abs(tile))
    top = jnp.max(jnp.max(top, axis=1, keepdims=True), axis=0, keepdims=True)
    return jnp.broadcast_to(top, (8, LANES))


def span_of(exponent):
    return jnp.exp2(exponent.astype(jnp.float32) * (1.0 / 64.0))


def code(x, inverse):
    return jnp.round(x * inverse * TOP).astype(jnp.int32)


def pair(high, low):
    return (high << 16) | (low & 0xFFFF)


def unpair(word, step):
    high = (word >> 16).astype(jnp.float32) * step
    low = ((word << 16) >> 16).astype(jnp.float32) * step
    return high, low


def roll(x, shift):
    return x if isinstance(shift, int) and shift == 0 else pltpu.roll(x, shift, 1)


def merge_groups(groups):
    merged = []
    for upper, lower in zip(groups[0::2], groups[1::2]):
        trials = []
        for e in range(len(upper)):
            trials += [lower[e] + roll(upper[e], e), lower[e] + roll(upper[e], e + 1)]
        merged.append(trials)
    return merged


def put(ref, start, stride, rows):
    for c in range(rows.shape[1] // LANES):
        ref[c, pl.ds(start, 8, stride=stride), :] = rows[:, c * LANES : (c + 1) * LANES]


def take(ref, start, count, first, last):
    chunks = [ref[c, pl.ds(start, count), :] for c in range(first, last)]
    return jnp.concatenate(chunks, axis=1)


def merge_rows(groups, one, two, tiles):
    while len(groups[0]) > 1:
        groups = [merge_groups(beam) for beam in groups]
    for e in range(8):
        for b, beam in enumerate(groups):
            put(one.at[b], e, 8, beam[0][e])
    source, target = one, two
    trials = 8
    while trials < ROWS:
        for base in range(0, ROWS, 2 * trials):
            for a in range(0, trials, 8):
                for b in range(BEAMS):
                    upper = take(source.at[b], base + a, 8, 0, tiles)
                    lower = take(source.at[b], base + trials + a, 8, 0, tiles)
                    early = pltpu.roll(upper, a, 1, stride=1, stride_axis=0)
                    late = pltpu.roll(upper, a + 1, 1, stride=1, stride_axis=0)
                    put(target.at[b], base + 2 * a, 2, lower + early)
                    put(target.at[b], base + 2 * a + 1, 2, lower + late)
        source, target = target, source
        trials *= 2


def local_kernel(
    q_ref,
    scale_hbm,
    x_hbm,
    o0,
    o1,
    o2,
    o3,
    o4,
    o5,
    free,
    scale,
    x,
    one,
    two,
    packed,
    sems,
):
    half = CHANS // 2
    q = q_ref[0]
    fetch_scale = pltpu.make_async_copy(scale_hbm, scale, sems.at[2 * BEAMS])
    fetch_scale.start()
    fetches = []
    for b in range(BEAMS):
        for h in range(2):
            piece = pl.ds(h * half, half)
            fetches.append(
                pltpu.make_async_copy(
                    x_hbm.at[b, piece], x.at[b, piece], sems.at[2 * b + h]
                )
            )
            fetches[-1].start()
    row = lax.broadcasted_iota(jnp.int32, (ROWS, CHANS), 0)
    col = lax.broadcasted_iota(jnp.int32, (ROWS, CHANS), 1)
    member = (row & 7) * 8 + (row >> 3) == col >> 3
    fetch_scale.wait()
    weights = jnp.where(member, scale[...], 0.0)
    weights = jnp.concatenate(split(weights), axis=0)
    blank = jnp.zeros((8, LANES), jnp.float32)
    for fetch in fetches:
        fetch.wait()
    groups = []
    for b in range(BEAMS):
        base = jnp.dot(weights, x[b], preferred_element_type=jnp.float32)
        base = base[:ROWS] + base[ROWS:]
        groups.append(
            [
                [jnp.concatenate([base[8 * g : 8 * g + 8], blank], axis=1)]
                for g in range(8)
            ]
        )
    merge_rows(groups, one, two, WIDE // LANES)
    first_slots(q, free)
    odd = lax.broadcasted_iota(jnp.int32, (8, UNITS * LANES), 0) & 2 != 0
    for a in range(TILES):
        rows = [take(two.at[b], 4 * a, 4, 0, WIDE // LANES) for b in range(BEAMS)]
        rows = jnp.concatenate([jnp.concatenate(rows, axis=0), blank], axis=1)
        rows = jnp.where(odd, pltpu.roll(rows, 2 * q, 1), rows)
        rows = pltpu.roll(rows, (4 * q * a) & (LANES - 1), 1)
        slots, _, again = unit_slots(q, a, free)
        for i, slot in enumerate(slots):
            packed[slot] = rows[:, i * LANES : (i + 1) * LANES]
        for slot, origin in again:
            packed[slot] = packed[origin]
    for k, out in enumerate((o0, o1, o2, o3, o4, o5)):
        out[...] = packed[pl.ds(STARTS[k], SIZES[k])]


def local_plane(x, scale, q):
    return pl.pallas_call(
        local_kernel,
        in_specs=[
            pl.BlockSpec(memory_space=pltpu.SMEM),
            pl.BlockSpec(memory_space=pltpu.HBM),
            pl.BlockSpec(memory_space=pltpu.HBM),
        ],
        out_shape=[jax.ShapeDtypeStruct((n, 8, LANES), jnp.float32) for n in SIZES],
        scratch_shapes=[
            pltpu.SMEM((REACH + 2,), jnp.int32),
            pltpu.VMEM((1, CHANS), jnp.float32),
            pltpu.VMEM((BEAMS, CHANS, SPAN), jnp.bfloat16),
            pltpu.VMEM((BEAMS, WIDE // LANES, ROWS, LANES), jnp.float32),
            pltpu.VMEM((BEAMS, WIDE // LANES, ROWS, LANES), jnp.float32),
            pltpu.VMEM((SPARE + 1, 8, LANES), jnp.float32),
            pltpu.SemaphoreType.DMA((2 * BEAMS + 1,)),
        ],
        compiler_params=pltpu.CompilerParams(vmem_limit_bytes=24 << 20),
        name="local_plane",
    )(
        q,
        pltpu.with_memory_space_constraint(scale, pltpu.HBM),
        pltpu.with_memory_space_constraint(x, pltpu.HBM),
    )


def gather_kernel(q_ref, o0, r1, r2, r3, r4, r5, out, free, packed, held):
    q = q_ref[0]
    first_slots(q, free)
    for k, piece in enumerate((o0, r1, r2, r3, r4, r5)):
        packed[pl.ds(STARTS[k], SIZES[k])] = piece[...]
    packed[SPARE] = jnp.zeros((8, LANES), jnp.float32)
    for a in range(TILES):
        slots, at, again = unit_slots(q, a, free)
        rows = pl.ds(8 * a, 8)
        tiles = [1 + ((at + i) & (PER - 1)) for i in range(PER)]
        held[0, rows, :] = packed[again[0][0]] + packed[again[1][0]]
        held[tiles[0], rows, :] = packed[slots[0]] + packed[slots[PER]]
        held[tiles[1], rows, :] = packed[slots[1]] + packed[slots[PER + 1]]
        held[tiles[2], rows, :] = packed[slots[2]]
        held[tiles[3], rows, :] = packed[slots[3]]
    tiles = WIDE // LANES
    values = [held[c, pl.ds(8 * a, 8), :] for c in range(tiles) for a in range(TILES)]
    exponent = exponent_of(largest_of(values))
    inverse = 1.0 / span_of(exponent)[:1]
    exponent = jnp.broadcast_to(exponent[:1], (TILES, LANES))
    lane = lax.broadcasted_iota(jnp.int32, (TILES, LANES), 1)
    for c in range(tiles):
        for r in range(4):
            high = code(held[c, pl.ds(r, TILES, stride=8), :], inverse)
            low = code(held[c, pl.ds(4 + r, TILES, stride=8), :], inverse)
            word = pair(high, low)
            if c == 0:
                word = jnp.where(lane == 0, exponent, word)
            rows = pl.ds((r >> 1) * BLOCK + c * 2 + (r & 1), TILES, stride=2 * BLOCK)
            out[rows, :] = word


def gather_shifted(pieces, q):
    vmem = pl.BlockSpec(memory_space=pltpu.VMEM)
    return pl.pallas_call(
        gather_kernel,
        in_specs=[pl.BlockSpec(memory_space=pltpu.SMEM)] + [vmem] * REACH,
        out_shape=jax.ShapeDtypeStruct((PARTS * BLOCK, LANES), jnp.int32),
        scratch_shapes=[
            pltpu.SMEM((REACH + 2,), jnp.int32),
            pltpu.VMEM((SPARE + 1, 8, LANES), jnp.float32),
            pltpu.VMEM((WIDE // LANES, 8 * TILES, LANES), jnp.float32),
        ],
        compiler_params=pltpu.CompilerParams(vmem_limit_bytes=24 << 20),
        name="gather_shifted",
    )(q, *pieces)


def final_groups(x_ref):
    beams = [[[] for _ in range(4)] for _ in range(BEAMS)]
    for g in range(4):
        for e in range(2):
            words = [
                x_ref[pl.ds(g * BLOCK + c * 2 + e, 8, stride=4 * BLOCK), :]
                for c in range(WIDE // LANES)
            ]
            step = jnp.broadcast_to(span_of(words[0][:, :1]) * (1.0 / TOP), (8, LANES))
            chunks = [unpair(word, step) for word in words]
            for b in range(BEAMS):
                row = jnp.concatenate([chunk[b] for chunk in chunks], axis=1)
                beams[b][g].append(row)
    return beams


def boxcar_bands(widths):
    u = lax.broadcasted_iota(jnp.int32, (2 * LANES, LANES), 0)
    t = lax.broadcasted_iota(jnp.int32, (2 * LANES, LANES), 1)
    ago = t + LANES - u
    bands = []
    for k in range(NBOX):
        inside = jnp.logical_and(ago >= 0, ago < widths[k])
        bands.append(jnp.where(inside, 1.0, 0.0).astype(jnp.bfloat16))
    return jnp.concatenate(bands, axis=1)


def boxcar_norms(widths):
    norms = []
    for k in range(NBOX):
        square = jnp.full((1, LANES), widths[k] * (CHANS * PARTS), jnp.int32)
        norms.append(lax.rsqrt(square.astype(jnp.float32)))
    return jnp.concatenate(norms, axis=1)


def boxcar_tile(before, here, bands, norms, held, c):
    window = jnp.concatenate([before, here], axis=1)
    sums = jnp.dot(window, bands, preferred_element_type=jnp.float32)
    rows = BEAMS * ROWS
    sums = (sums[:rows] + sums[rows:]) * norms
    for b in range(BEAMS):
        for k in range(NBOX):
            held[b, k, :, pl.ds(c * LANES, LANES)] = sums[
                b * ROWS : (b + 1) * ROWS, k * LANES : (k + 1) * LANES
            ]


def final_kernel(widths, x_ref, out, one, two, held, sems):
    merge_rows(final_groups(x_ref), one, two, WIDE // LANES)
    bands = boxcar_bands(widths)
    norms = boxcar_norms(widths)
    parts = []
    for c in range(WIDE // LANES):
        tile = jnp.concatenate([two[b, c] for b in range(BEAMS)], axis=0)
        parts.append(jnp.concatenate(split(tile), axis=0))
    copies = []
    for c in range(PER):
        boxcar_tile(parts[c], parts[c + 1], bands, norms, held, c)
        lanes = pl.ds(c * LANES, LANES)
        copies.append(
            pltpu.make_async_copy(
                held.at[:, :, :, lanes], out.at[:, :, :, lanes], sems.at[c]
            )
        )
        copies[-1].start()
    for copy in copies:
        copy.wait()


def final_boxcars(x, widths):
    return pl.pallas_call(
        final_kernel,
        in_specs=[
            pl.BlockSpec(memory_space=pltpu.SMEM),
            pl.BlockSpec(memory_space=pltpu.VMEM),
        ],
        out_specs=pl.BlockSpec(memory_space=pltpu.HBM),
        out_shape=jax.ShapeDtypeStruct((BEAMS, NBOX, ROWS, SPAN), jnp.float32),
        scratch_shapes=[
            pltpu.VMEM((BEAMS, WIDE // LANES, ROWS, LANES), jnp.float32),
            pltpu.VMEM((BEAMS, WIDE // LANES, ROWS, LANES), jnp.float32),
            pltpu.VMEM((BEAMS, NBOX, ROWS, SPAN), jnp.float32),
            pltpu.SemaphoreType.DMA((PER,)),
        ],
        compiler_params=pltpu.CompilerParams(vmem_limit_bytes=24 << 20),
        name="final_boxcars",
    )(widths, x)


def later(block, distances):
    route = []
    for part, distance in enumerate(distances):
        if distance:
            for i in range(SEGMENTS - distance):
                sender = part * SEGMENTS + i
                route.append((sender, sender + distance))
    return lax.ppermute(block, ("chan", "tm"), route)


def per_device(intensity, channel_scale, box_widths):
    q = (PARTS - 1 - lax.axis_index("chan")).astype(jnp.int32).reshape(1)
    pieces = list(local_plane(intensity, channel_scale.reshape(1, CHANS), q))
    for k in range(REACH - 1, 0, -1):
        pieces[k] = later(pieces[k], DISTANCES[::-1, k].tolist())
    lined = gather_shifted(pieces, q)
    lined = lined.reshape(PARTS, 1, BLOCK * LANES)
    lined = lax.all_to_all(lined, "chan", 0, 0, tiled=True)
    lined = lined.reshape(PARTS * BLOCK, LANES)
    return final_boxcars(lined, box_widths)


def solution(mesh):
    in_specs = (P(None, "chan", "tm"), P("chan"), P())
    out_specs = P(None, None, "chan", "tm")
    return jax.shard_map(
        per_device, mesh=mesh, in_specs=in_specs, out_specs=out_specs, check_vma=False
    )
```

```python
import jax
import jax.numpy as jnp
import numpy as np
from jax import lax
from jax.experimental import pallas as pl
from jax.experimental.pallas import tpu as pltpu
from jax.sharding import PartitionSpec as P

BEAMS = 2
CHANS = 512
SPAN = 512
PARTS = 32
SEGMENTS = 8
ROWS = 64
WIDE = SPAN + 128
NBOX = 6
LANES = 128
REACH = 6
TILES = 16
UNITS = 6
PER = SPAN // LANES
BLOCK = 10
TOP = 32000.0


def tails(a):
    reach = [sum((i >> level) + 1 >> 1 for level in range(6)) for i in range(4 * a, 4 * a + 4)]
    return max(reach[:2]), max(reach[2:])


def tile_span(q, a):
    delay = 4 * q * a
    first, second = tails(a)
    within = delay & (LANES - 1)
    end = within + SPAN + (max if isinstance(q, int) else jnp.maximum)(first, 2 * q + second)
    tile = delay >> 7
    far = (tile & (PER - 1)) * LANES + end > 2 * SPAN - (2 * q + 63)
    return tile, (end + LANES - 1) >> 7, far


def group_shares(q, a, least=min):
    tile, number, far = tile_span(q, a)
    at = tile & (PER - 1)
    here = PER - at
    then = least(number - here, PER)
    over = number - here - then
    return tile >> 2, at, number, far, (here, 1 + then, over + far)


def packing():
    counts = np.zeros((PARTS, REACH), np.int32)
    for q in range(PARTS):
        for a in range(TILES):
            k, _, _, _, shares = group_shares(q, a)
            for i, share in enumerate(shares):
                if share:
                    counts[q, k + i] += share
    sizes = [64, 60, 38, 30, 16, 2]
    buffers = np.zeros((PARTS, REACH), np.int32)
    distances = np.zeros((PARTS, REACH), np.int32)
    for q in range(PARTS):
        taken = {0}
        for k in range(REACH - 1, 0, -1):
            if counts[q, k]:
                allowed = (k,) if q >= 22 else (4, 2, 1)
                fits = [i for i in allowed if i not in taken and sizes[i] >= counts[q, k]]
                buffers[q, k] = fits[0]
                distances[q, fits[0]] = k
                taken.add(fits[0])
    starts = [sum(sizes[:k]) for k in range(REACH)]
    return sizes, starts, sum(sizes), buffers, distances


SIZES, STARTS, SPARE, BUFFERS, DISTANCES = packing()


def first_slots(q, free):
    for k in range(REACH):
        slot = STARTS[BUFFERS[0, k]]
        for band in range(1, PARTS):
            if BUFFERS[band, k] != BUFFERS[band - 1, k]:
                slot = jnp.where(q >= band, STARTS[BUFFERS[band, k]], slot)
        free[k] = slot


def unit_slots(q, a, free):
    k, at, number, far, shares = group_shares(q, a, jnp.minimum)
    here = shares[0]
    p0, p1, p2 = free[k], free[k + 1], free[k + 2]
    free[k] = p0 + here
    free[k + 1] = p1 + shares[1]
    free[k + 2] = p2 + shares[2]
    slots = [p0]
    for i in range(1, PER):
        slots.append(jnp.where(i < here, p0 + i, p1 + 1 + i - here))
    slots.append(p1 + 1 + PER - here)
    last = jnp.where(here > 1, p1 + PER + 2 - here, p2 + 1)
    slots.append(jnp.where(number > PER + 1, last, SPARE))
    again = (p1, p0 + here - 1), (jnp.where(far, p2, SPARE), jnp.where(far, p1 + PER, SPARE))
    return slots, at, again


def split(x):
    first = x.astype(jnp.bfloat16)
    second = (x - first.astype(jnp.float32)).astype(jnp.bfloat16)
    return first, second


def exponent_of(largest):
    return jnp.floor(64.0 * jnp.log2(jnp.maximum(largest, 1e-36))).astype(jnp.int32) + 2


def largest_of(tiles):
    top = jnp.abs(tiles[0])
    for tile in tiles[1:]:
        top = jnp.maximum(top, jnp.abs(tile))
    top = jnp.max(jnp.max(top, axis=1, keepdims=True), axis=0, keepdims=True)
    return jnp.broadcast_to(top, (8, LANES))


def span_of(exponent):
    return jnp.exp2(exponent.astype(jnp.float32) * (1.0 / 64.0))


def code(x, inverse):
    return jnp.round(x * inverse * TOP).astype(jnp.int32)


def pair(high, low):
    return (high << 16) | (low & 0xFFFF)


def unpair(word, step):
    high = (word >> 16).astype(jnp.float32) * step
    low = ((word << 16) >> 16).astype(jnp.float32) * step
    return high, low


def roll(x, shift):
    return x if isinstance(shift, int) and shift == 0 else pltpu.roll(x, shift, 1)


def merge_groups(groups):
    merged = []
    for upper, lower in zip(groups[0::2], groups[1::2]):
        trials = []
        for e in range(len(upper)):
            trials += [lower[e] + roll(upper[e], e), lower[e] + roll(upper[e], e + 1)]
        merged.append(trials)
    return merged


def put(ref, start, stride, rows):
    for c in range(rows.shape[1] // LANES):
        ref[c, pl.ds(start, 8, stride=stride), :] = rows[:, c * LANES : (c + 1) * LANES]


def take(ref, start, count, first, last):
    chunks = [ref[c, pl.ds(start, count), :] for c in range(first, last)]
    return jnp.concatenate(chunks, axis=1)


def merge_rows(groups, one, two, tiles):
    while len(groups[0]) > 1:
        groups = [merge_groups(beam) for beam in groups]
    for e in range(8):
        for b, beam in enumerate(groups):
            put(one.at[b], e, 8, beam[0][e])
    source, target = one, two
    trials = 8
    while trials < ROWS:
        for base in range(0, ROWS, 2 * trials):
            for a in range(0, trials, 8):
                for b in range(BEAMS):
                    upper = take(source.at[b], base + a, 8, 0, tiles)
                    lower = take(source.at[b], base + trials + a, 8, 0, tiles)
                    early = pltpu.roll(upper, a, 1, stride=1, stride_axis=0)
                    late = pltpu.roll(upper, a + 1, 1, stride=1, stride_axis=0)
                    put(target.at[b], base + 2 * a, 2, lower + early)
                    put(target.at[b], base + 2 * a + 1, 2, lower + late)
        source, target = target, source
        trials *= 2


def local_kernel(
    q_ref,
    scale_hbm,
    x_hbm,
    o0,
    o1,
    o2,
    o3,
    o4,
    o5,
    free,
    scale,
    x,
    one,
    two,
    packed,
    sems,
):
    half = CHANS // 2
    q = q_ref[0]
    fetch_scale = pltpu.make_async_copy(scale_hbm, scale, sems.at[2 * BEAMS])
    fetch_scale.start()
    fetches = []
    for b in range(BEAMS):
        for h in range(2):
            piece = pl.ds(h * half, half)
            fetches.append(
                pltpu.make_async_copy(
                    x_hbm.at[b, piece], x.at[b, piece], sems.at[2 * b + h]
                )
            )
            fetches[-1].start()
    row = lax.broadcasted_iota(jnp.int32, (ROWS, CHANS), 0)
    col = lax.broadcasted_iota(jnp.int32, (ROWS, CHANS), 1)
    member = (row & 7) * 8 + (row >> 3) == col >> 3
    fetch_scale.wait()
    weights = jnp.where(member, scale[...], 0.0)
    weights = jnp.concatenate(split(weights), axis=0)
    blank = jnp.zeros((8, LANES), jnp.float32)
    for fetch in fetches:
        fetch.wait()
    groups = []
    for b in range(BEAMS):
        base = jnp.dot(weights, x[b], preferred_element_type=jnp.float32)
        base = base[:ROWS] + base[ROWS:]
        groups.append(
            [
                [jnp.concatenate([base[8 * g : 8 * g + 8], blank], axis=1)]
                for g in range(8)
            ]
        )
    merge_rows(groups, one, two, WIDE // LANES)
    first_slots(q, free)
    odd = lax.broadcasted_iota(jnp.int32, (8, UNITS * LANES), 0) & 2 != 0
    for a in range(TILES):
        rows = [take(two.at[b], 4 * a, 4, 0, WIDE // LANES) for b in range(BEAMS)]
        rows = jnp.concatenate([jnp.concatenate(rows, axis=0), blank], axis=1)
        rows = jnp.where(odd, pltpu.roll(rows, 2 * q, 1), rows)
        rows = pltpu.roll(rows, (4 * q * a) & (LANES - 1), 1)
        slots, _, again = unit_slots(q, a, free)
        for i, slot in enumerate(slots):
            packed[slot] = rows[:, i * LANES : (i + 1) * LANES]
        for slot, origin in again:
            packed[slot] = packed[origin]
    o0[...] = packed[pl.ds(0, SIZES[0])]
    tiles = [
        two[b, c, pl.ds(8 * a, 8), :]
        for b in range(BEAMS)
        for c in range(WIDE // LANES)
        for a in range(8)
    ]
    exponent = exponent_of(largest_of(tiles))
    inverse = 1.0 / span_of(exponent)
    for k, out in enumerate((o1, o2, o3, o4, o5), 1):
        words = SIZES[k] // 2
        for t in range(words):
            slot = STARTS[k] + 2 * t
            high, low = code(packed[slot], inverse), code(packed[slot + 1], inverse)
            out[t] = pair(high, low)
        out[words] = exponent


def local_plane(x, scale, q):
    return pl.pallas_call(
        local_kernel,
        in_specs=[
            pl.BlockSpec(memory_space=pltpu.SMEM),
            pl.BlockSpec(memory_space=pltpu.HBM),
            pl.BlockSpec(memory_space=pltpu.HBM),
        ],
        out_shape=[jax.ShapeDtypeStruct((SIZES[0], 8, LANES), jnp.float32)]
        + [jax.ShapeDtypeStruct((n // 2 + 1, 8, LANES), jnp.int32) for n in SIZES[1:]],
        scratch_shapes=[
            pltpu.SMEM((REACH + 2,), jnp.int32),
            pltpu.VMEM((1, CHANS), jnp.float32),
            pltpu.VMEM((BEAMS, CHANS, SPAN), jnp.bfloat16),
            pltpu.VMEM((BEAMS, WIDE // LANES, ROWS, LANES), jnp.float32),
            pltpu.VMEM((BEAMS, WIDE // LANES, ROWS, LANES), jnp.float32),
            pltpu.VMEM((SPARE + 1, 8, LANES), jnp.float32),
            pltpu.SemaphoreType.DMA((2 * BEAMS + 1,)),
        ],
        compiler_params=pltpu.CompilerParams(vmem_limit_bytes=24 << 20),
        name="local_plane",
    )(
        q,
        pltpu.with_memory_space_constraint(scale, pltpu.HBM),
        pltpu.with_memory_space_constraint(x, pltpu.HBM),
    )


def gather_kernel(q_ref, o0, r1, r2, r3, r4, r5, out, free, packed, held):
    q = q_ref[0]
    first_slots(q, free)
    packed[pl.ds(0, SIZES[0])] = o0[...]
    for k, piece in enumerate((r1, r2, r3, r4, r5), 1):
        words = SIZES[k] // 2
        step = span_of(piece[words]) * (1.0 / TOP)
        for t in range(words):
            slot = STARTS[k] + 2 * t
            packed[slot], packed[slot + 1] = unpair(piece[t], step)
    packed[SPARE] = jnp.zeros((8, LANES), jnp.float32)
    for a in range(TILES):
        slots, at, again = unit_slots(q, a, free)
        rows = pl.ds(8 * a, 8)
        tiles = [1 + ((at + i) & (PER - 1)) for i in range(PER)]
        held[0, rows, :] = packed[again[0][0]] + packed[again[1][0]]
        held[tiles[0], rows, :] = packed[slots[0]] + packed[slots[PER]]
        held[tiles[1], rows, :] = packed[slots[1]] + packed[slots[PER + 1]]
        held[tiles[2], rows, :] = packed[slots[2]]
        held[tiles[3], rows, :] = packed[slots[3]]
    tiles = WIDE // LANES
    values = [held[c, pl.ds(8 * a, 8), :] for c in range(tiles) for a in range(TILES)]
    exponent = exponent_of(largest_of(values))
    inverse = 1.0 / span_of(exponent)[:1]
    exponent = jnp.broadcast_to(exponent[:1], (TILES, LANES))
    lane = lax.broadcasted_iota(jnp.int32, (TILES, LANES), 1)
    for c in range(tiles):
        for r in range(4):
            high = code(held[c, pl.ds(r, TILES, stride=8), :], inverse)
            low = code(held[c, pl.ds(4 + r, TILES, stride=8), :], inverse)
            word = pair(high, low)
            if c == 0:
                word = jnp.where(lane == 0, exponent, word)
            rows = pl.ds((r >> 1) * BLOCK + c * 2 + (r & 1), TILES, stride=2 * BLOCK)
            out[rows, :] = word


def gather_shifted(pieces, q):
    vmem = pl.BlockSpec(memory_space=pltpu.VMEM)
    return pl.pallas_call(
        gather_kernel,
        in_specs=[pl.BlockSpec(memory_space=pltpu.SMEM)] + [vmem] * REACH,
        out_shape=jax.ShapeDtypeStruct((PARTS * BLOCK, LANES), jnp.int32),
        scratch_shapes=[
            pltpu.SMEM((REACH + 2,), jnp.int32),
            pltpu.VMEM((SPARE + 1, 8, LANES), jnp.float32),
            pltpu.VMEM((WIDE // LANES, 8 * TILES, LANES), jnp.float32),
        ],
        compiler_params=pltpu.CompilerParams(vmem_limit_bytes=24 << 20),
        name="gather_shifted",
    )(q, *pieces)


def final_groups(x_ref):
    beams = [[[] for _ in range(4)] for _ in range(BEAMS)]
    for g in range(4):
        for e in range(2):
            words = [
                x_ref[pl.ds(g * BLOCK + c * 2 + e, 8, stride=4 * BLOCK), :]
                for c in range(WIDE // LANES)
            ]
            step = jnp.broadcast_to(span_of(words[0][:, :1]) * (1.0 / TOP), (8, LANES))
            chunks = [unpair(word, step) for word in words]
            for b in range(BEAMS):
                row = jnp.concatenate([chunk[b] for chunk in chunks], axis=1)
                beams[b][g].append(row)
    return beams


def boxcar_bands(widths):
    u = lax.broadcasted_iota(jnp.int32, (2 * LANES, LANES), 0)
    t = lax.broadcasted_iota(jnp.int32, (2 * LANES, LANES), 1)
    ago = t + LANES - u
    bands = []
    for k in range(NBOX):
        inside = jnp.logical_and(ago >= 0, ago < widths[k])
        bands.append(jnp.where(inside, 1.0, 0.0).astype(jnp.bfloat16))
    return jnp.concatenate(bands, axis=1)


def boxcar_norms(widths):
    norms = []
    for k in range(NBOX):
        square = jnp.full((1, LANES), widths[k] * (CHANS * PARTS), jnp.int32)
        norms.append(lax.rsqrt(square.astype(jnp.float32)))
    return jnp.concatenate(norms, axis=1)


def boxcar_tile(before, here, bands, norms, held, c):
    window = jnp.concatenate([before, here], axis=1)
    sums = jnp.dot(window, bands, preferred_element_type=jnp.float32)
    rows = BEAMS * ROWS
    sums = (sums[:rows] + sums[rows:]) * norms
    for b in range(BEAMS):
        for k in range(NBOX):
            held[b, k, :, pl.ds(c * LANES, LANES)] = sums[
                b * ROWS : (b + 1) * ROWS, k * LANES : (k + 1) * LANES
            ]


def final_kernel(widths, x_ref, out, one, two, held, sems):
    merge_rows(final_groups(x_ref), one, two, WIDE // LANES)
    bands = boxcar_bands(widths)
    norms = boxcar_norms(widths)
    parts = []
    for c in range(WIDE // LANES):
        tile = jnp.concatenate([two[b, c] for b in range(BEAMS)], axis=0)
        parts.append(jnp.concatenate(split(tile), axis=0))
    copies = []
    for c in range(PER):
        boxcar_tile(parts[c], parts[c + 1], bands, norms, held, c)
        lanes = pl.ds(c * LANES, LANES)
        copies.append(
            pltpu.make_async_copy(
                held.at[:, :, :, lanes], out.at[:, :, :, lanes], sems.at[c]
            )
        )
        copies[-1].start()
    for copy in copies:
        copy.wait()


def final_boxcars(x, widths):
    return pl.pallas_call(
        final_kernel,
        in_specs=[
            pl.BlockSpec(memory_space=pltpu.SMEM),
            pl.BlockSpec(memory_space=pltpu.VMEM),
        ],
        out_specs=pl.BlockSpec(memory_space=pltpu.HBM),
        out_shape=jax.ShapeDtypeStruct((BEAMS, NBOX, ROWS, SPAN), jnp.float32),
        scratch_shapes=[
            pltpu.VMEM((BEAMS, WIDE // LANES, ROWS, LANES), jnp.float32),
            pltpu.VMEM((BEAMS, WIDE // LANES, ROWS, LANES), jnp.float32),
            pltpu.VMEM((BEAMS, NBOX, ROWS, SPAN), jnp.float32),
            pltpu.SemaphoreType.DMA((PER,)),
        ],
        compiler_params=pltpu.CompilerParams(vmem_limit_bytes=24 << 20),
        name="final_boxcars",
    )(widths, x)


def later(block, distances):
    route = []
    for part, distance in enumerate(distances):
        if distance:
            for i in range(SEGMENTS - distance):
                sender = part * SEGMENTS + i
                route.append((sender, sender + distance))
    return lax.ppermute(block, ("chan", "tm"), route)


def per_device(intensity, channel_scale, box_widths):
    q = (PARTS - 1 - lax.axis_index("chan")).astype(jnp.int32).reshape(1)
    pieces = list(local_plane(intensity, channel_scale.reshape(1, CHANS), q))
    for k in range(REACH - 1, 0, -1):
        pieces[k] = later(pieces[k], DISTANCES[::-1, k].tolist())
    lined = gather_shifted(pieces, q)
    lined = lined.reshape(PARTS, 1, BLOCK * LANES)
    lined = lax.all_to_all(lined, "chan", 0, 0, tiled=True)
    lined = lined.reshape(PARTS * BLOCK, LANES)
    return final_boxcars(lined, box_widths)


def solution(mesh):
    in_specs = (P(None, "chan", "tm"), P("chan"), P())
    out_specs = P(None, None, "chan", "tm")
    return jax.shard_map(
        per_device, mesh=mesh, in_specs=in_specs, out_specs=out_specs, check_vma=False
    )
```

```python
import jax
import jax.numpy as jnp
import numpy as np
from jax import lax
from jax.experimental import pallas as pl
from jax.experimental.pallas import tpu as pltpu
from jax.sharding import PartitionSpec as P

BEAMS = 2
CHANS = 512
SPAN = 512
PARTS = 32
SEGMENTS = 8
ROWS = 64
WIDE = SPAN + 128
NBOX = 6
LANES = 128
REACH = 6
TILES = 16
UNITS = 6
PLACES = UNITS + 4
PER = SPAN // LANES
BLOCK = 10
TOP = 32000.0


def tails(a):
    reach = [sum((i >> level) + 1 >> 1 for level in range(6)) for i in range(4 * a, 4 * a + 4)]
    return max(reach[:2]), max(reach[2:])


def tile_span(q, a):
    delay = 4 * q * a
    first, second = tails(a)
    within = delay & (LANES - 1)
    end = within + SPAN + (max if isinstance(q, int) else jnp.maximum)(first, 2 * q + second)
    tile = delay >> 7
    far = (tile & (PER - 1)) * LANES + end > 2 * SPAN - (2 * q + 63)
    return tile, (end + LANES - 1) >> 7, far


def group_shares(q, a, least=min):
    tile, number, far = tile_span(q, a)
    at = tile & (PER - 1)
    here = PER - at
    then = least(number - here, PER)
    over = number - here - then
    return tile >> 2, at, number, far, (here, 1 + then, over + far)


def packing():
    counts = np.zeros((PARTS, REACH), np.int32)
    for q in range(PARTS):
        for a in range(TILES):
            k, _, _, _, shares = group_shares(q, a)
            for i, share in enumerate(shares):
                if share:
                    counts[q, k + i] += share
    sizes = [64, 60, 38, 30, 16, 2]
    buffers = np.zeros((PARTS, REACH), np.int32)
    distances = np.zeros((PARTS, REACH), np.int32)
    for q in range(PARTS):
        taken = {0}
        for k in range(REACH - 1, 0, -1):
            if counts[q, k]:
                allowed = (k,) if q >= 22 else (4, 2, 1)
                fits = [i for i in allowed if i not in taken and sizes[i] >= counts[q, k]]
                buffers[q, k] = fits[0]
                distances[q, fits[0]] = k
                taken.add(fits[0])
    starts = [sum(sizes[:k]) for k in range(REACH)]
    return sizes, starts, sum(sizes), buffers, distances


SIZES, STARTS, SPARE, BUFFERS, DISTANCES = packing()


def first_slots(q, free):
    for k in range(REACH):
        slot = STARTS[BUFFERS[0, k]]
        for band in range(1, PARTS):
            if BUFFERS[band, k] != BUFFERS[band - 1, k]:
                slot = jnp.where(q >= band, STARTS[BUFFERS[band, k]], slot)
        free[k] = slot


def unit_slots(q, a, free):
    k, at, number, far, shares = group_shares(q, a, jnp.minimum)
    here = shares[0]
    p0, p1, p2 = free[k], free[k + 1], free[k + 2]
    free[k] = p0 + here
    free[k + 1] = p1 + shares[1]
    free[k + 2] = p2 + shares[2]
    slots = [p0]
    for i in range(1, PER):
        slots.append(jnp.where(i < here, p0 + i, p1 + 1 + i - here))
    slots.append(p1 + 1 + PER - here)
    last = jnp.where(here > 1, p1 + PER + 2 - here, p2 + 1)
    slots.append(jnp.where(number > PER + 1, last, SPARE))
    again = (p1, p0 + here - 1), (jnp.where(far, p2, SPARE), jnp.where(far, p1 + PER, SPARE))
    return slots, at, again


def split(x):
    first = x.astype(jnp.bfloat16)
    second = (x - first.astype(jnp.float32)).astype(jnp.bfloat16)
    return first, second


def exponent_of(largest):
    return jnp.floor(64.0 * jnp.log2(jnp.maximum(largest, 1e-36))).astype(jnp.int32) + 2


def largest_of(tiles):
    top = jnp.abs(tiles[0])
    for tile in tiles[1:]:
        top = jnp.maximum(top, jnp.abs(tile))
    top = jnp.max(jnp.max(top, axis=1, keepdims=True), axis=0, keepdims=True)
    return jnp.broadcast_to(top, (8, LANES))


def span_of(exponent):
    return jnp.exp2(exponent.astype(jnp.float32) * (1.0 / 64.0))


def code(x, inverse):
    return jnp.round(x * inverse * TOP).astype(jnp.int32)


def pair(high, low):
    return (high << 16) | (low & 0xFFFF)


def unpair(word, step):
    high = (word >> 16).astype(jnp.float32) * step
    low = ((word << 16) >> 16).astype(jnp.float32) * step
    return high, low


def roll(x, shift):
    return x if isinstance(shift, int) and shift == 0 else pltpu.roll(x, shift, 1)


def merge_groups(groups):
    merged = []
    for upper, lower in zip(groups[0::2], groups[1::2]):
        trials = []
        for e in range(len(upper)):
            trials += [lower[e] + roll(upper[e], e), lower[e] + roll(upper[e], e + 1)]
        merged.append(trials)
    return merged


def put(ref, start, stride, rows):
    for c in range(rows.shape[1] // LANES):
        ref[c, pl.ds(start, 8, stride=stride), :] = rows[:, c * LANES : (c + 1) * LANES]


def take(ref, start, count, first, last):
    chunks = [ref[c, pl.ds(start, count), :] for c in range(first, last)]
    return jnp.concatenate(chunks, axis=1)


def merge_rows(groups, one, two, tiles):
    while len(groups[0]) > 1:
        groups = [merge_groups(beam) for beam in groups]
    for e in range(8):
        for b, beam in enumerate(groups):
            put(one.at[b], e, 8, beam[0][e])
    source, target = one, two
    trials = 8
    while trials < ROWS:
        for base in range(0, ROWS, 2 * trials):
            for a in range(0, trials, 8):
                for b in range(BEAMS):
                    upper = take(source.at[b], base + a, 8, 0, tiles)
                    lower = take(source.at[b], base + trials + a, 8, 0, tiles)
                    early = pltpu.roll(upper, a, 1, stride=1, stride_axis=0)
                    late = pltpu.roll(upper, a + 1, 1, stride=1, stride_axis=0)
                    put(target.at[b], base + 2 * a, 2, lower + early)
                    put(target.at[b], base + 2 * a + 1, 2, lower + late)
        source, target = target, source
        trials *= 2


def local_kernel(
    q_ref,
    scale_hbm,
    x_hbm,
    o0,
    o1,
    o2,
    o3,
    o4,
    o5,
    free,
    places,
    scale,
    x,
    one,
    two,
    packed,
    sems,
):
    half = CHANS // 2
    q = q_ref[0]
    fetch_scale = pltpu.make_async_copy(scale_hbm, scale, sems.at[2 * BEAMS])
    fetch_scale.start()
    fetches = []
    for b in range(BEAMS):
        for h in range(2):
            piece = pl.ds(h * half, half)
            fetches.append(
                pltpu.make_async_copy(
                    x_hbm.at[b, piece], x.at[b, piece], sems.at[2 * b + h]
                )
            )
            fetches[-1].start()
    row = lax.broadcasted_iota(jnp.int32, (ROWS, CHANS), 0)
    col = lax.broadcasted_iota(jnp.int32, (ROWS, CHANS), 1)
    member = (row & 7) * 8 + (row >> 3) == col >> 3
    first_slots(q, free)
    for a in range(TILES):
        slots, _, again = unit_slots(q, a, free)
        for i, slot in enumerate(slots + [*again[0], *again[1]]):
            places[a * PLACES + i] = slot
    fetch_scale.wait()
    weights = jnp.where(member, scale[...], 0.0)
    weights = jnp.concatenate(split(weights), axis=0)
    blank = jnp.zeros((8, LANES), jnp.float32)
    groups = []
    for b in range(BEAMS):
        fetches[2 * b].wait()
        fetches[2 * b + 1].wait()
        base = jnp.dot(weights, x[b], preferred_element_type=jnp.float32)
        base = base[:ROWS] + base[ROWS:]
        groups.append(
            [
                [jnp.concatenate([base[8 * g : 8 * g + 8], blank], axis=1)]
                for g in range(8)
            ]
        )
    merge_rows(groups, one, two, WIDE // LANES)
    odd = lax.broadcasted_iota(jnp.int32, (8, UNITS * LANES), 0) & 2 != 0
    for a in range(TILES):
        rows = [take(two.at[b], 4 * a, 4, 0, WIDE // LANES) for b in range(BEAMS)]
        rows = jnp.concatenate([jnp.concatenate(rows, axis=0), blank], axis=1)
        rows = jnp.where(odd, pltpu.roll(rows, 2 * q, 1), rows)
        rows = pltpu.roll(rows, (4 * q * a) & (LANES - 1), 1)
        place = a * PLACES
        for i in range(UNITS):
            packed[places[place + i]] = rows[:, i * LANES : (i + 1) * LANES]
        for i in (UNITS, UNITS + 2):
            packed[places[place + i]] = packed[places[place + i + 1]]
    o0[...] = packed[pl.ds(0, SIZES[0])]
    tiles = [
        two[b, c, pl.ds(8 * a, 8), :]
        for b in range(BEAMS)
        for c in range(WIDE // LANES)
        for a in range(8)
    ]
    exponent = exponent_of(largest_of(tiles))
    inverse = 1.0 / span_of(exponent)
    for k, out in enumerate((o1, o2, o3, o4, o5), 1):
        words = SIZES[k] // 2
        for t in range(words):
            slot = STARTS[k] + 2 * t
            high, low = code(packed[slot], inverse), code(packed[slot + 1], inverse)
            out[t] = pair(high, low)
        out[words] = exponent


def local_plane(x, scale, q):
    return pl.pallas_call(
        local_kernel,
        in_specs=[
            pl.BlockSpec(memory_space=pltpu.SMEM),
            pl.BlockSpec(memory_space=pltpu.HBM),
            pl.BlockSpec(memory_space=pltpu.HBM),
        ],
        out_shape=[jax.ShapeDtypeStruct((SIZES[0], 8, LANES), jnp.float32)]
        + [jax.ShapeDtypeStruct((n // 2 + 1, 8, LANES), jnp.int32) for n in SIZES[1:]],
        scratch_shapes=[
            pltpu.SMEM((REACH + 2,), jnp.int32),
            pltpu.SMEM((TILES * PLACES,), jnp.int32),
            pltpu.VMEM((1, CHANS), jnp.float32),
            pltpu.VMEM((BEAMS, CHANS, SPAN), jnp.bfloat16),
            pltpu.VMEM((BEAMS, WIDE // LANES, ROWS, LANES), jnp.float32),
            pltpu.VMEM((BEAMS, WIDE // LANES, ROWS, LANES), jnp.float32),
            pltpu.VMEM((SPARE + 1, 8, LANES), jnp.float32),
            pltpu.SemaphoreType.DMA((2 * BEAMS + 1,)),
        ],
        compiler_params=pltpu.CompilerParams(vmem_limit_bytes=24 << 20),
        name="local_plane",
    )(
        q,
        pltpu.with_memory_space_constraint(scale, pltpu.HBM),
        pltpu.with_memory_space_constraint(x, pltpu.HBM),
    )


def gather_kernel(q_ref, o0, r1, r2, r3, r4, r5, out, free, packed, held):
    q = q_ref[0]
    first_slots(q, free)
    packed[pl.ds(0, SIZES[0])] = o0[...]
    for k, piece in enumerate((r1, r2, r3, r4, r5), 1):
        words = SIZES[k] // 2
        step = span_of(piece[words]) * (1.0 / TOP)
        for t in range(words):
            slot = STARTS[k] + 2 * t
            packed[slot], packed[slot + 1] = unpair(piece[t], step)
    packed[SPARE] = jnp.zeros((8, LANES), jnp.float32)
    for a in range(TILES):
        slots, at, again = unit_slots(q, a, free)
        rows = pl.ds(8 * a, 8)
        tiles = [1 + ((at + i) & (PER - 1)) for i in range(PER)]
        held[0, rows, :] = packed[again[0][0]] + packed[again[1][0]]
        held[tiles[0], rows, :] = packed[slots[0]] + packed[slots[PER]]
        held[tiles[1], rows, :] = packed[slots[1]] + packed[slots[PER + 1]]
        held[tiles[2], rows, :] = packed[slots[2]]
        held[tiles[3], rows, :] = packed[slots[3]]
    tiles = WIDE // LANES
    values = [held[c, pl.ds(8 * a, 8), :] for c in range(tiles) for a in range(TILES)]
    exponent = exponent_of(largest_of(values))
    inverse = 1.0 / span_of(exponent)[:1]
    exponent = jnp.broadcast_to(exponent[:1], (TILES, LANES))
    lane = lax.broadcasted_iota(jnp.int32, (TILES, LANES), 1)
    for c in range(tiles):
        for r in range(4):
            high = code(held[c, pl.ds(r, TILES, stride=8), :], inverse)
            low = code(held[c, pl.ds(4 + r, TILES, stride=8), :], inverse)
            word = pair(high, low)
            if c == 0:
                word = jnp.where(lane == 0, exponent, word)
            rows = pl.ds((r >> 1) * BLOCK + c * 2 + (r & 1), TILES, stride=2 * BLOCK)
            out[rows, :] = word


def gather_shifted(pieces, q):
    vmem = pl.BlockSpec(memory_space=pltpu.VMEM)
    return pl.pallas_call(
        gather_kernel,
        in_specs=[pl.BlockSpec(memory_space=pltpu.SMEM)] + [vmem] * REACH,
        out_shape=jax.ShapeDtypeStruct((PARTS * BLOCK, LANES), jnp.int32),
        scratch_shapes=[
            pltpu.SMEM((REACH + 2,), jnp.int32),
            pltpu.VMEM((SPARE + 1, 8, LANES), jnp.float32),
            pltpu.VMEM((WIDE // LANES, 8 * TILES, LANES), jnp.float32),
        ],
        compiler_params=pltpu.CompilerParams(vmem_limit_bytes=24 << 20),
        name="gather_shifted",
    )(q, *pieces)


def final_groups(x_ref):
    beams = [[[] for _ in range(4)] for _ in range(BEAMS)]
    for g in range(4):
        for e in range(2):
            words = [
                x_ref[pl.ds(g * BLOCK + c * 2 + e, 8, stride=4 * BLOCK), :]
                for c in range(WIDE // LANES)
            ]
            step = jnp.broadcast_to(span_of(words[0][:, :1]) * (1.0 / TOP), (8, LANES))
            chunks = [unpair(word, step) for word in words]
            for b in range(BEAMS):
                row = jnp.concatenate([chunk[b] for chunk in chunks], axis=1)
                beams[b][g].append(row)
    return beams


def boxcar_bands(widths, places):
    u = lax.broadcasted_iota(jnp.int32, (2 * LANES, LANES), 0)
    t = lax.broadcasted_iota(jnp.int32, (2 * LANES, LANES), 1)
    ago = t + LANES - u
    bands = []
    for k in places:
        inside = jnp.logical_and(ago >= 0, ago < widths[k])
        bands.append(jnp.where(inside, 1.0, 0.0).astype(jnp.bfloat16))
    return jnp.concatenate(bands, axis=1)


def boxcar_norm(width):
    square = jnp.full((1, LANES), width * (CHANS * PARTS), jnp.int32)
    return lax.rsqrt(square.astype(jnp.float32))


def final_kernel(widths, x_ref, out, one, two, held, sems):
    merge_rows(final_groups(x_ref), one, two, WIDE // LANES)
    rows = BEAMS * ROWS
    copies = []

    def send(k):
        copies.append(pltpu.make_async_copy(held.at[:, k], out.at[:, k], sems.at[k]))
        copies[-1].start()

    norm = boxcar_norm(widths[0])
    for b in range(BEAMS):
        for c in range(PER):
            held[b, 0, :, pl.ds(c * LANES, LANES)] = two[b, c + 1] * norm
    send(0)
    parts = []
    for c in range(WIDE // LANES):
        tile = jnp.concatenate([two[b, c] for b in range(BEAMS)], axis=0)
        parts.append(split(tile))
    windows = [
        jnp.concatenate([before[0], here[0], before[1], here[1]], axis=1)
        for before, here in zip(parts, parts[1:])
    ]
    windows = jnp.concatenate(windows, axis=0)
    for places in ((1, 2), (3, 4), (5,)):
        bands = boxcar_bands(widths, places)
        bands = jnp.concatenate([bands, bands], axis=0)
        sums = jnp.dot(windows, bands, preferred_element_type=jnp.float32)
        for i, k in enumerate(places):
            norm = boxcar_norm(widths[k])
            for c in range(PER):
                term = sums[rows * c : rows * (c + 1), i * LANES : (i + 1) * LANES]
                term = term * norm
                for b in range(BEAMS):
                    held[b, k, :, pl.ds(c * LANES, LANES)] = term[
                        b * ROWS : (b + 1) * ROWS
                    ]
            send(k)
    for copy in copies:
        copy.wait()


def final_boxcars(x, widths):
    return pl.pallas_call(
        final_kernel,
        in_specs=[
            pl.BlockSpec(memory_space=pltpu.SMEM),
            pl.BlockSpec(memory_space=pltpu.VMEM),
        ],
        out_specs=pl.BlockSpec(memory_space=pltpu.HBM),
        out_shape=jax.ShapeDtypeStruct((BEAMS, NBOX, ROWS, SPAN), jnp.float32),
        scratch_shapes=[
            pltpu.VMEM((BEAMS, WIDE // LANES, ROWS, LANES), jnp.float32),
            pltpu.VMEM((BEAMS, WIDE // LANES, ROWS, LANES), jnp.float32),
            pltpu.VMEM((BEAMS, NBOX, ROWS, SPAN), jnp.float32),
            pltpu.SemaphoreType.DMA((NBOX,)),
        ],
        compiler_params=pltpu.CompilerParams(vmem_limit_bytes=24 << 20),
        name="final_boxcars",
    )(widths, x)


def later(block, distances):
    route = []
    for part, distance in enumerate(distances):
        if distance:
            for i in range(SEGMENTS - distance):
                sender = part * SEGMENTS + i
                route.append((sender, sender + distance))
    return lax.ppermute(block, ("chan", "tm"), route)


def per_device(intensity, channel_scale, box_widths):
    q = (PARTS - 1 - lax.axis_index("chan")).astype(jnp.int32).reshape(1)
    pieces = list(local_plane(intensity, channel_scale.reshape(1, CHANS), q))
    for k in range(REACH - 1, 0, -1):
        pieces[k] = later(pieces[k], DISTANCES[::-1, k].tolist())
    lined = gather_shifted(pieces, q)
    lined = lined.reshape(PARTS, 1, BLOCK * LANES)
    lined = lax.all_to_all(lined, "chan", 0, 0, tiled=True)
    lined = lined.reshape(PARTS * BLOCK, LANES)
    return final_boxcars(lined, box_widths)


def solution(mesh):
    in_specs = (P(None, "chan", "tm"), P("chan"), P())
    out_specs = P(None, None, "chan", "tm")
    return jax.shard_map(
        per_device, mesh=mesh, in_specs=in_specs, out_specs=out_specs, check_vma=False
    )
```

```python
import jax
import jax.numpy as jnp
import numpy as np
from jax import lax
from jax.experimental import pallas as pl
from jax.experimental.pallas import tpu as pltpu
from jax.sharding import PartitionSpec as P

BEAMS = 2
CHANS = 512
SPAN = 512
PARTS = 32
SEGMENTS = 8
ROWS = 64
WIDE = SPAN + 128
NBOX = 6
LANES = 128
REACH = 6
TILES = 16
UNITS = 6
PLACES = UNITS + 4
PER = SPAN // LANES
BLOCK = 10
TOP = 32000.0


def tails(a):
    reach = [sum((i >> level) + 1 >> 1 for level in range(6)) for i in range(4 * a, 4 * a + 4)]
    return max(reach[:2]), max(reach[2:])


def tile_span(q, a):
    delay = 4 * q * a
    first, second = tails(a)
    within = delay & (LANES - 1)
    end = within + SPAN + (max if isinstance(q, int) else jnp.maximum)(first, 2 * q + second)
    tile = delay >> 7
    far = (tile & (PER - 1)) * LANES + end > 2 * SPAN - (2 * q + 63)
    return tile, (end + LANES - 1) >> 7, far


def group_shares(q, a, least=min):
    tile, number, far = tile_span(q, a)
    at = tile & (PER - 1)
    here = PER - at
    then = least(number - here, PER)
    over = number - here - then
    return tile >> 2, at, number, far, (here, 1 + then, over + far)


def packing():
    counts = np.zeros((PARTS, REACH), np.int32)
    for q in range(PARTS):
        for a in range(TILES):
            k, _, _, _, shares = group_shares(q, a)
            for i, share in enumerate(shares):
                if share:
                    counts[q, k + i] += share
    sizes = [64, 60, 38, 30, 16, 2]
    buffers = np.zeros((PARTS, REACH), np.int32)
    distances = np.zeros((PARTS, REACH), np.int32)
    for q in range(PARTS):
        taken = {0}
        for k in range(REACH - 1, 0, -1):
            if counts[q, k]:
                allowed = (k,) if q >= 22 else (4, 2, 1)
                fits = [i for i in allowed if i not in taken and sizes[i] >= counts[q, k]]
                buffers[q, k] = fits[0]
                distances[q, fits[0]] = k
                taken.add(fits[0])
    starts = [sum(sizes[:k]) for k in range(REACH)]
    return sizes, starts, sum(sizes), buffers, distances


SIZES, STARTS, SPARE, BUFFERS, DISTANCES = packing()


def first_slots(q, free):
    for k in range(REACH):
        slot = STARTS[BUFFERS[0, k]]
        for band in range(1, PARTS):
            if BUFFERS[band, k] != BUFFERS[band - 1, k]:
                slot = jnp.where(q >= band, STARTS[BUFFERS[band, k]], slot)
        free[k] = slot


def unit_slots(q, a, free):
    k, at, number, far, shares = group_shares(q, a, jnp.minimum)
    here = shares[0]
    p0, p1, p2 = free[k], free[k + 1], free[k + 2]
    free[k] = p0 + here
    free[k + 1] = p1 + shares[1]
    free[k + 2] = p2 + shares[2]
    slots = [p0]
    for i in range(1, PER):
        slots.append(jnp.where(i < here, p0 + i, p1 + 1 + i - here))
    slots.append(p1 + 1 + PER - here)
    last = jnp.where(here > 1, p1 + PER + 2 - here, p2 + 1)
    slots.append(jnp.where(number > PER + 1, last, SPARE))
    again = (p1, p0 + here - 1), (jnp.where(far, p2, SPARE), jnp.where(far, p1 + PER, SPARE))
    return slots, at, again


def split(x):
    first = x.astype(jnp.bfloat16)
    second = (x - first.astype(jnp.float32)).astype(jnp.bfloat16)
    return first, second


def exponent_of(largest):
    return jnp.floor(64.0 * jnp.log2(jnp.maximum(largest, 1e-36))).astype(jnp.int32) + 2


def largest_of(tiles):
    top = jnp.abs(tiles[0])
    for tile in tiles[1:]:
        top = jnp.maximum(top, jnp.abs(tile))
    top = jnp.max(jnp.max(top, axis=1, keepdims=True), axis=0, keepdims=True)
    return jnp.broadcast_to(top, (8, LANES))


def span_of(exponent):
    return jnp.exp2(exponent.astype(jnp.float32) * (1.0 / 64.0))


def code(x, inverse):
    return jnp.round(x * inverse * TOP).astype(jnp.int32)


def pair(high, low):
    return (high << 16) | (low & 0xFFFF)


def unpair(word, step):
    high = (word >> 16).astype(jnp.float32) * step
    low = ((word << 16) >> 16).astype(jnp.float32) * step
    return high, low


def roll(x, shift):
    return x if isinstance(shift, int) and shift == 0 else pltpu.roll(x, shift, 1)


def merge_groups(groups):
    merged = []
    for upper, lower in zip(groups[0::2], groups[1::2]):
        trials = []
        for e in range(len(upper)):
            trials += [lower[e] + roll(upper[e], e), lower[e] + roll(upper[e], e + 1)]
        merged.append(trials)
    return merged


def put(ref, start, stride, rows):
    for c in range(rows.shape[1] // LANES):
        ref[c, pl.ds(start, 8, stride=stride), :] = rows[:, c * LANES : (c + 1) * LANES]


def take(ref, start, count, first, last):
    chunks = [ref[c, pl.ds(start, count), :] for c in range(first, last)]
    return jnp.concatenate(chunks, axis=1)


def merge_rows(groups, one, two, tiles):
    while len(groups[0]) > 1:
        groups = [merge_groups(beam) for beam in groups]
    for e in range(8):
        for b, beam in enumerate(groups):
            put(one.at[b], e, 8, beam[0][e])
    source, target = one, two
    trials = 8
    while trials < ROWS:
        for base in range(0, ROWS, 2 * trials):
            for a in range(0, trials, 8):
                for b in range(BEAMS):
                    upper = take(source.at[b], base + a, 8, 0, tiles)
                    lower = take(source.at[b], base + trials + a, 8, 0, tiles)
                    early = pltpu.roll(upper, a, 1, stride=1, stride_axis=0)
                    late = pltpu.roll(upper, a + 1, 1, stride=1, stride_axis=0)
                    put(target.at[b], base + 2 * a, 2, lower + early)
                    put(target.at[b], base + 2 * a + 1, 2, lower + late)
        source, target = target, source
        trials *= 2


def local_kernel(
    scale_hbm,
    x_hbm,
    o0,
    o1,
    o2,
    o3,
    o4,
    o5,
    free,
    places,
    scale,
    x,
    one,
    two,
    packed,
    sems,
):
    half = CHANS // 2
    q = PARTS - 1 - lax.axis_index("chan")
    fetch_scale = pltpu.make_async_copy(scale_hbm, scale, sems.at[2 * BEAMS])
    fetch_scale.start()
    fetches = []
    for b in range(BEAMS):
        for h in range(2):
            piece = pl.ds(h * half, half)
            fetches.append(
                pltpu.make_async_copy(
                    x_hbm.at[b, piece], x.at[b, piece], sems.at[2 * b + h]
                )
            )
            fetches[-1].start()
    row = lax.broadcasted_iota(jnp.int32, (ROWS, CHANS), 0)
    col = lax.broadcasted_iota(jnp.int32, (ROWS, CHANS), 1)
    member = (row & 7) * 8 + (row >> 3) == col >> 3
    first_slots(q, free)
    for a in range(TILES):
        slots, _, again = unit_slots(q, a, free)
        for i, slot in enumerate(slots + [*again[0], *again[1]]):
            places[a * PLACES + i] = slot
    fetch_scale.wait()
    weights = jnp.where(member, scale[...], 0.0)
    weights = jnp.concatenate(split(weights), axis=0)
    blank = jnp.zeros((8, LANES), jnp.float32)
    groups = []
    for b in range(BEAMS):
        fetches[2 * b].wait()
        fetches[2 * b + 1].wait()
        base = jnp.dot(weights, x[b], preferred_element_type=jnp.float32)
        base = base[:ROWS] + base[ROWS:]
        groups.append(
            [
                [jnp.concatenate([base[8 * g : 8 * g + 8], blank], axis=1)]
                for g in range(8)
            ]
        )
    merge_rows(groups, one, two, WIDE // LANES)
    odd = lax.broadcasted_iota(jnp.int32, (8, UNITS * LANES), 0) & 2 != 0
    for a in range(TILES):
        rows = [take(two.at[b], 4 * a, 4, 0, WIDE // LANES) for b in range(BEAMS)]
        rows = jnp.concatenate([jnp.concatenate(rows, axis=0), blank], axis=1)
        rows = jnp.where(odd, pltpu.roll(rows, 2 * q, 1), rows)
        rows = pltpu.roll(rows, (4 * q * a) & (LANES - 1), 1)
        place = a * PLACES
        for i in range(UNITS):
            packed[places[place + i]] = rows[:, i * LANES : (i + 1) * LANES]
        for i in (UNITS, UNITS + 2):
            packed[places[place + i]] = packed[places[place + i + 1]]
    o0[...] = packed[pl.ds(0, SIZES[0])]
    tiles = [
        two[b, c, pl.ds(8 * a, 8), :]
        for b in range(BEAMS)
        for c in range(WIDE // LANES)
        for a in range(8)
    ]
    exponent = exponent_of(largest_of(tiles))
    inverse = 1.0 / span_of(exponent)
    for k, out in enumerate((o1, o2, o3, o4, o5), 1):
        words = SIZES[k] // 2
        for t in range(words):
            slot = STARTS[k] + 2 * t
            high, low = code(packed[slot], inverse), code(packed[slot + 1], inverse)
            out[t] = pair(high, low)
        out[words] = exponent


def local_plane(x, scale):
    return pl.pallas_call(
        local_kernel,
        in_specs=[
            pl.BlockSpec(memory_space=pltpu.HBM),
            pl.BlockSpec(memory_space=pltpu.HBM),
        ],
        out_shape=[jax.ShapeDtypeStruct((SIZES[0], 8, LANES), jnp.float32)]
        + [jax.ShapeDtypeStruct((n // 2 + 1, 8, LANES), jnp.int32) for n in SIZES[1:]],
        scratch_shapes=[
            pltpu.SMEM((REACH + 2,), jnp.int32),
            pltpu.SMEM((TILES * PLACES,), jnp.int32),
            pltpu.VMEM((1, CHANS), jnp.float32),
            pltpu.VMEM((BEAMS, CHANS, SPAN), jnp.bfloat16),
            pltpu.VMEM((BEAMS, WIDE // LANES, ROWS, LANES), jnp.float32),
            pltpu.VMEM((BEAMS, WIDE // LANES, ROWS, LANES), jnp.float32),
            pltpu.VMEM((SPARE + 1, 8, LANES), jnp.float32),
            pltpu.SemaphoreType.DMA((2 * BEAMS + 1,)),
        ],
        compiler_params=pltpu.CompilerParams(vmem_limit_bytes=24 << 20),
        name="local_plane",
    )(
        pltpu.with_memory_space_constraint(scale, pltpu.HBM),
        pltpu.with_memory_space_constraint(x, pltpu.HBM),
    )


def gather_kernel(o0, r1, r2, r3, r4, r5, out, free, packed, held):
    q = PARTS - 1 - lax.axis_index("chan")
    first_slots(q, free)
    packed[pl.ds(0, SIZES[0])] = o0[...]
    for k, piece in enumerate((r1, r2, r3, r4, r5), 1):
        words = SIZES[k] // 2
        step = span_of(piece[words]) * (1.0 / TOP)
        for t in range(words):
            slot = STARTS[k] + 2 * t
            packed[slot], packed[slot + 1] = unpair(piece[t], step)
    packed[SPARE] = jnp.zeros((8, LANES), jnp.float32)
    for a in range(TILES):
        slots, at, again = unit_slots(q, a, free)
        rows = pl.ds(8 * a, 8)
        tiles = [1 + ((at + i) & (PER - 1)) for i in range(PER)]
        held[0, rows, :] = packed[again[0][0]] + packed[again[1][0]]
        held[tiles[0], rows, :] = packed[slots[0]] + packed[slots[PER]]
        held[tiles[1], rows, :] = packed[slots[1]] + packed[slots[PER + 1]]
        held[tiles[2], rows, :] = packed[slots[2]]
        held[tiles[3], rows, :] = packed[slots[3]]
    tiles = WIDE // LANES
    values = [held[c, pl.ds(8 * a, 8), :] for c in range(tiles) for a in range(TILES)]
    exponent = exponent_of(largest_of(values))
    inverse = 1.0 / span_of(exponent)[:1]
    exponent = jnp.broadcast_to(exponent[:1], (TILES, LANES))
    lane = lax.broadcasted_iota(jnp.int32, (TILES, LANES), 1)
    for c in range(tiles):
        for r in range(4):
            high = code(held[c, pl.ds(r, TILES, stride=8), :], inverse)
            low = code(held[c, pl.ds(4 + r, TILES, stride=8), :], inverse)
            word = pair(high, low)
            if c == 0:
                word = jnp.where(lane == 0, exponent, word)
            rows = pl.ds((r >> 1) * BLOCK + c * 2 + (r & 1), TILES, stride=2 * BLOCK)
            out[rows, :] = word


def gather_shifted(pieces):
    vmem = pl.BlockSpec(memory_space=pltpu.VMEM)
    return pl.pallas_call(
        gather_kernel,
        in_specs=[vmem] * REACH,
        out_shape=jax.ShapeDtypeStruct((PARTS * BLOCK, LANES), jnp.int32),
        scratch_shapes=[
            pltpu.SMEM((REACH + 2,), jnp.int32),
            pltpu.VMEM((SPARE + 1, 8, LANES), jnp.float32),
            pltpu.VMEM((WIDE // LANES, 8 * TILES, LANES), jnp.float32),
        ],
        compiler_params=pltpu.CompilerParams(vmem_limit_bytes=24 << 20),
        name="gather_shifted",
    )(*pieces)


def final_groups(x_ref):
    beams = [[[] for _ in range(4)] for _ in range(BEAMS)]
    for g in range(4):
        for e in range(2):
            words = [
                x_ref[pl.ds(g * BLOCK + c * 2 + e, 8, stride=4 * BLOCK), :]
                for c in range(WIDE // LANES)
            ]
            step = jnp.broadcast_to(span_of(words[0][:, :1]) * (1.0 / TOP), (8, LANES))
            chunks = [unpair(word, step) for word in words]
            for b in range(BEAMS):
                row = jnp.concatenate([chunk[b] for chunk in chunks], axis=1)
                beams[b][g].append(row)
    return beams


def boxcar_bands(widths, places):
    u = lax.broadcasted_iota(jnp.int32, (2 * LANES, LANES), 0)
    t = lax.broadcasted_iota(jnp.int32, (2 * LANES, LANES), 1)
    ago = t + LANES - u
    bands = []
    for k in places:
        inside = jnp.logical_and(ago >= 0, ago < widths[:, k : k + 1])
        bands.append(jnp.where(inside, 1.0, 0.0).astype(jnp.bfloat16))
    return jnp.concatenate(bands, axis=1)


def boxcar_norm(width):
    return lax.rsqrt((width * (CHANS * PARTS)).astype(jnp.float32))


def final_kernel(widths, x_ref, out, one, two, held, sems):
    merge_rows(final_groups(x_ref), one, two, WIDE // LANES)
    rows = BEAMS * ROWS
    copies = []

    def send(k):
        copies.append(pltpu.make_async_copy(held.at[:, k], out.at[:, k], sems.at[k]))
        copies[-1].start()

    norm = boxcar_norm(widths[:, :1])
    for b in range(BEAMS):
        for c in range(PER):
            held[b, 0, :, pl.ds(c * LANES, LANES)] = two[b, c + 1] * norm
    send(0)
    parts = []
    for c in range(WIDE // LANES):
        tile = jnp.concatenate([two[b, c] for b in range(BEAMS)], axis=0)
        parts.append(split(tile))
    windows = [
        jnp.concatenate([before[0], here[0], before[1], here[1]], axis=1)
        for before, here in zip(parts, parts[1:])
    ]
    windows = jnp.concatenate(windows, axis=0)
    for places in ((1, 2), (3, 4), (5,)):
        bands = boxcar_bands(widths, places)
        bands = jnp.concatenate([bands, bands], axis=0)
        sums = jnp.dot(windows, bands, preferred_element_type=jnp.float32)
        for i, k in enumerate(places):
            norm = boxcar_norm(widths[:, k : k + 1])
            for c in range(PER):
                term = sums[rows * c : rows * (c + 1), i * LANES : (i + 1) * LANES]
                term = term * norm
                for b in range(BEAMS):
                    held[b, k, :, pl.ds(c * LANES, LANES)] = term[
                        b * ROWS : (b + 1) * ROWS
                    ]
            send(k)
    for copy in copies:
        copy.wait()


def final_boxcars(x, widths):
    return pl.pallas_call(
        final_kernel,
        in_specs=[pl.BlockSpec(memory_space=pltpu.VMEM)] * 2,
        out_specs=pl.BlockSpec(memory_space=pltpu.HBM),
        out_shape=jax.ShapeDtypeStruct((BEAMS, NBOX, ROWS, SPAN), jnp.float32),
        scratch_shapes=[
            pltpu.VMEM((BEAMS, WIDE // LANES, ROWS, LANES), jnp.float32),
            pltpu.VMEM((BEAMS, WIDE // LANES, ROWS, LANES), jnp.float32),
            pltpu.VMEM((BEAMS, NBOX, ROWS, SPAN), jnp.float32),
            pltpu.SemaphoreType.DMA((NBOX,)),
        ],
        compiler_params=pltpu.CompilerParams(vmem_limit_bytes=24 << 20),
        name="final_boxcars",
    )(widths.reshape(1, NBOX), x)


def later(block, distances):
    route = []
    for part, distance in enumerate(distances):
        if distance:
            for i in range(SEGMENTS - distance):
                sender = part * SEGMENTS + i
                route.append((sender, sender + distance))
    return lax.ppermute(block, ("chan", "tm"), route)


def per_device(intensity, channel_scale, box_widths):
    pieces = list(local_plane(intensity, channel_scale.reshape(1, CHANS)))
    for k in range(REACH - 1, 0, -1):
        pieces[k] = later(pieces[k], DISTANCES[::-1, k].tolist())
    lined = gather_shifted(pieces)
    lined = lined.reshape(PARTS, 1, BLOCK * LANES)
    lined = lax.all_to_all(lined, "chan", 0, 0, tiled=True)
    lined = lined.reshape(PARTS * BLOCK, LANES)
    return final_boxcars(lined, box_widths)


def solution(mesh):
    in_specs = (P(None, "chan", "tm"), P("chan"), P())
    out_specs = P(None, None, "chan", "tm")
    return jax.shard_map(
        per_device, mesh=mesh, in_specs=in_specs, out_specs=out_specs, check_vma=False
    )
```

```python
import jax
import jax.numpy as jnp
import numpy as np
from jax import lax
from jax.experimental import pallas as pl
from jax.experimental.pallas import tpu as pltpu
from jax.sharding import PartitionSpec as P

BEAMS = 2
CHANS = 512
SPAN = 512
PARTS = 32
SEGMENTS = 8
ROWS = 64
WIDE = SPAN + 128
NBOX = 6
LANES = 128
REACH = 6
TILES = 16
UNITS = 6
PLACES = UNITS + 4
PER = SPAN // LANES
FRONT = PER
BLOCK = 10
TOP = 32000.0


def tails(a):
    reach = [sum((i >> level) + 1 >> 1 for level in range(6)) for i in range(4 * a, 4 * a + 4)]
    return max(reach[:2]), max(reach[2:])


def tile_span(q, a):
    delay = 4 * q * a
    first, second = tails(a)
    within = delay & (LANES - 1)
    end = within + SPAN + (max if isinstance(q, int) else jnp.maximum)(first, 2 * q + second)
    tile = delay >> 7
    far = (tile & (PER - 1)) * LANES + end > 2 * SPAN - (2 * q + 63)
    return tile, (end + LANES - 1) >> 7, far


def group_shares(q, a, least=min):
    tile, number, far = tile_span(q, a)
    at = tile & (PER - 1)
    here = PER - at
    then = least(number - here, PER)
    over = number - here - then
    return tile >> 2, at, number, far, (here, 1 + then, over + far)


def packing():
    counts = np.zeros((PARTS, REACH), np.int32)
    for q in range(PARTS):
        for a in range(TILES):
            k, _, _, _, shares = group_shares(q, a)
            for i, share in enumerate(shares):
                if share:
                    counts[q, k + i] += share
    sizes = [64, 60, 38, 30, 16, 2]
    buffers = np.zeros((PARTS, REACH), np.int32)
    distances = np.zeros((PARTS, REACH), np.int32)
    for q in range(PARTS):
        taken = {0}
        for k in range(REACH - 1, 0, -1):
            if counts[q, k]:
                allowed = (k,) if q >= 22 or k == 3 else (4, 2, 1)
                fits = [i for i in allowed if i not in taken and sizes[i] >= counts[q, k]]
                buffers[q, k] = fits[0]
                distances[q, fits[0]] = k
                taken.add(fits[0])
    starts = [sum(sizes[:k]) for k in range(REACH)]
    return sizes, starts, sum(sizes), buffers, distances


SIZES, STARTS, SPARE, BUFFERS, DISTANCES = packing()


def first_slots(q, free):
    for k in range(REACH):
        slot = STARTS[BUFFERS[0, k]]
        for band in range(1, PARTS):
            if BUFFERS[band, k] != BUFFERS[band - 1, k]:
                slot = jnp.where(q >= band, STARTS[BUFFERS[band, k]], slot)
        free[k] = slot


def unit_slots(q, a, free):
    k, at, number, far, shares = group_shares(q, a, jnp.minimum)
    here = shares[0]
    p0, p1, p2 = free[k], free[k + 1], free[k + 2]
    free[k] = p0 + here
    free[k + 1] = p1 + shares[1]
    free[k + 2] = p2 + shares[2]
    slots = [p0]
    for i in range(1, PER):
        slots.append(jnp.where(i < here, p0 + i, p1 + 1 + i - here))
    slots.append(p1 + 1 + PER - here)
    last = jnp.where(here > 1, p1 + PER + 2 - here, p2 + 1)
    slots.append(jnp.where(number > PER + 1, last, SPARE))
    again = (p1, p0 + here - 1), (jnp.where(far, p2, SPARE), jnp.where(far, p1 + PER, SPARE))
    return slots, at, again


def split(x):
    first = x.astype(jnp.bfloat16)
    second = (x - first.astype(jnp.float32)).astype(jnp.bfloat16)
    return first, second


def exponent_of(largest):
    return jnp.floor(64.0 * jnp.log2(jnp.maximum(largest, 1e-36))).astype(jnp.int32) + 2


def largest_of(tiles):
    top = jnp.abs(tiles[0])
    for tile in tiles[1:]:
        top = jnp.maximum(top, jnp.abs(tile))
    top = jnp.max(jnp.max(top, axis=1, keepdims=True), axis=0, keepdims=True)
    return jnp.broadcast_to(top, (8, LANES))


def span_of(exponent):
    return jnp.exp2(exponent.astype(jnp.float32) * (1.0 / 64.0))


def code(x, inverse):
    return jnp.round(x * inverse * TOP).astype(jnp.int32)


def pair(high, low):
    return (high << 16) | (low & 0xFFFF)


def unpair(word, step):
    high = (word >> 16).astype(jnp.float32) * step
    low = ((word << 16) >> 16).astype(jnp.float32) * step
    return high, low


def roll(x, shift):
    return x if isinstance(shift, int) and shift == 0 else pltpu.roll(x, shift, 1)


def merge_groups(groups):
    merged = []
    for upper, lower in zip(groups[0::2], groups[1::2]):
        trials = []
        for e in range(len(upper)):
            trials += [lower[e] + roll(upper[e], e), lower[e] + roll(upper[e], e + 1)]
        merged.append(trials)
    return merged


def put(ref, start, stride, rows):
    for c in range(rows.shape[1] // LANES):
        ref[c, pl.ds(start, 8, stride=stride), :] = rows[:, c * LANES : (c + 1) * LANES]


def take(ref, start, count, first, last):
    chunks = [ref[c, pl.ds(start, count), :] for c in range(first, last)]
    return jnp.concatenate(chunks, axis=1)


def merge_rows(groups, one, two, tiles):
    while len(groups[0]) > 1:
        groups = [merge_groups(beam) for beam in groups]
    for e in range(8):
        for b, beam in enumerate(groups):
            put(one.at[b], e, 8, beam[0][e])
    source, target = one, two
    trials = 8
    while trials < ROWS:
        for base in range(0, ROWS, 2 * trials):
            for a in range(0, trials, 8):
                for b in range(BEAMS):
                    upper = take(source.at[b], base + a, 8, 0, tiles)
                    lower = take(source.at[b], base + trials + a, 8, 0, tiles)
                    early = pltpu.roll(upper, a, 1, stride=1, stride_axis=0)
                    late = pltpu.roll(upper, a + 1, 1, stride=1, stride_axis=0)
                    put(target.at[b], base + 2 * a, 2, lower + early)
                    put(target.at[b], base + 2 * a + 1, 2, lower + late)
        source, target = target, source
        trials *= 2


def local_kernel(
    scale_hbm,
    x_hbm,
    o0,
    o1,
    o2,
    o3,
    o4,
    o5,
    free,
    places,
    scale,
    x,
    one,
    two,
    packed,
    sems,
):
    half = CHANS // 2
    q = PARTS - 1 - lax.axis_index("chan")
    fetch_scale = pltpu.make_async_copy(scale_hbm, scale, sems.at[2 * BEAMS])
    fetch_scale.start()
    fetches = []
    for b in range(BEAMS):
        for h in range(2):
            piece = pl.ds(h * half, half)
            fetches.append(
                pltpu.make_async_copy(
                    x_hbm.at[b, piece], x.at[b, piece], sems.at[2 * b + h]
                )
            )
            fetches[-1].start()
    row = lax.broadcasted_iota(jnp.int32, (ROWS, CHANS), 0)
    col = lax.broadcasted_iota(jnp.int32, (ROWS, CHANS), 1)
    member = (row & 7) * 8 + (row >> 3) == col >> 3
    first_slots(q, free)
    for a in range(TILES):
        slots, _, again = unit_slots(q, a, free)
        for i, slot in enumerate(slots + [*again[0], *again[1]]):
            places[a * PLACES + i] = slot
    fetch_scale.wait()
    weights = jnp.where(member, scale[...], 0.0)
    weights = jnp.concatenate(split(weights), axis=0)
    blank = jnp.zeros((8, LANES), jnp.float32)
    groups = []
    for b in range(BEAMS):
        fetches[2 * b].wait()
        fetches[2 * b + 1].wait()
        base = jnp.dot(weights, x[b], preferred_element_type=jnp.float32)
        base = base[:ROWS] + base[ROWS:]
        groups.append(
            [
                [jnp.concatenate([base[8 * g : 8 * g + 8], blank], axis=1)]
                for g in range(8)
            ]
        )
    merge_rows(groups, one, two, WIDE // LANES)
    odd = lax.broadcasted_iota(jnp.int32, (8, UNITS * LANES), 0) & 2 != 0
    for a in range(TILES):
        rows = [take(two.at[b], 4 * a, 4, 0, WIDE // LANES) for b in range(BEAMS)]
        rows = jnp.concatenate([jnp.concatenate(rows, axis=0), blank], axis=1)
        rows = jnp.where(odd, pltpu.roll(rows, 2 * q, 1), rows)
        rows = pltpu.roll(rows, (4 * q * a) & (LANES - 1), 1)
        place = a * PLACES
        for i in range(UNITS):
            packed[places[place + i]] = rows[:, i * LANES : (i + 1) * LANES]
        for i in (UNITS, UNITS + 2):
            packed[places[place + i]] = packed[places[place + i + 1]]
    o0[...] = packed[pl.ds(0, SIZES[0])]
    tiles = [
        two[b, c, pl.ds(8 * a, 8), :]
        for b in range(BEAMS)
        for c in range(WIDE // LANES)
        for a in range(8)
    ]
    exponent = exponent_of(largest_of(tiles))
    inverse = 1.0 / span_of(exponent)
    for k, out in enumerate((o1, o2, o3, o4, o5), 1):
        words = SIZES[k] // 2
        for t in range(words):
            slot = STARTS[k] + 2 * t
            high, low = code(packed[slot], inverse), code(packed[slot + 1], inverse)
            out[t] = pair(high, low)
        out[words] = exponent


def local_plane(x, scale):
    return pl.pallas_call(
        local_kernel,
        in_specs=[
            pl.BlockSpec(memory_space=pltpu.HBM),
            pl.BlockSpec(memory_space=pltpu.HBM),
        ],
        out_shape=[jax.ShapeDtypeStruct((SIZES[0], 8, LANES), jnp.float32)]
        + [jax.ShapeDtypeStruct((n // 2 + 1, 8, LANES), jnp.int32) for n in SIZES[1:]],
        scratch_shapes=[
            pltpu.SMEM((REACH + 2,), jnp.int32),
            pltpu.SMEM((TILES * PLACES,), jnp.int32),
            pltpu.VMEM((1, CHANS), jnp.float32),
            pltpu.VMEM((BEAMS, CHANS, SPAN), jnp.bfloat16),
            pltpu.VMEM((BEAMS, WIDE // LANES, ROWS, LANES), jnp.float32),
            pltpu.VMEM((BEAMS, WIDE // LANES, ROWS, LANES), jnp.float32),
            pltpu.VMEM((SPARE + 1, 8, LANES), jnp.float32),
            pltpu.SemaphoreType.DMA((2 * BEAMS + 1,)),
        ],
        compiler_params=pltpu.CompilerParams(vmem_limit_bytes=24 << 20),
        name="local_plane",
    )(
        pltpu.with_memory_space_constraint(scale, pltpu.HBM),
        pltpu.with_memory_space_constraint(x, pltpu.HBM),
    )


def gather_kernel(o0, r1, r2, r3, r4, r5, out, free, packed, held):
    q = PARTS - 1 - lax.axis_index("chan")
    tiles = WIDE // LANES
    first_slots(q, free)
    packed[pl.ds(FRONT, SIZES[0])] = o0[...]
    for k, piece in enumerate((r1, r2, r3, r4, r5), 1):
        words = SIZES[k] // 2
        step = span_of(piece[words]) * (1.0 / TOP)
        for t in range(words):
            slot = FRONT + STARTS[k] + 2 * t
            packed[slot], packed[slot + 1] = unpair(piece[t], step)
    top = jnp.zeros((8, LANES), jnp.float32)
    for a in range(TILES):
        k, at, _, _, (here, then, over) = group_shares(q, a, jnp.minimum)
        p0, p1, p2 = free[k], free[k + 1], free[k + 2]
        free[k] = p0 + here
        free[k + 1] = p1 + then
        free[k + 2] = p2 + over
        end = packed[pl.ds(FRONT + p0 - at, PER)]
        begin = packed[pl.ds(FRONT + p1, tiles)]
        more = packed[pl.ds(FRONT + p2, 2)]
        for c in range(tiles):
            tile = jnp.where(c < then, begin[c], 0.0)
            if c > 0:
                tile = tile + jnp.where(c > at, end[c - 1], 0.0)
            if c < 2:
                tile = tile + jnp.where(c < over, more[c], 0.0)
            held[c, pl.ds(8 * a, 8), :] = tile
            top = jnp.maximum(top, jnp.abs(tile))
    exponent = exponent_of(largest_of([top]))
    inverse = 1.0 / span_of(exponent)[:1]
    exponent = jnp.broadcast_to(exponent[:1], (TILES, LANES))
    lane = lax.broadcasted_iota(jnp.int32, (TILES, LANES), 1)
    for c in range(tiles):
        for r in range(4):
            high = code(held[c, pl.ds(r, TILES, stride=8), :], inverse)
            low = code(held[c, pl.ds(4 + r, TILES, stride=8), :], inverse)
            word = pair(high, low)
            if c == 0:
                word = jnp.where(lane == 0, exponent, word)
            rows = pl.ds((r >> 1) * BLOCK + c * 2 + (r & 1), TILES, stride=2 * BLOCK)
            out[rows, :] = word


def gather_shifted(pieces):
    vmem = pl.BlockSpec(memory_space=pltpu.VMEM)
    return pl.pallas_call(
        gather_kernel,
        in_specs=[vmem] * REACH,
        out_shape=jax.ShapeDtypeStruct((PARTS * BLOCK, LANES), jnp.int32),
        scratch_shapes=[
            pltpu.SMEM((REACH + 2,), jnp.int32),
            pltpu.VMEM((FRONT + SPARE + WIDE // LANES, 8, LANES), jnp.float32),
            pltpu.VMEM((WIDE // LANES, 8 * TILES, LANES), jnp.float32),
        ],
        compiler_params=pltpu.CompilerParams(vmem_limit_bytes=24 << 20),
        name="gather_shifted",
    )(*pieces)


def final_groups(x_ref):
    beams = [[[] for _ in range(4)] for _ in range(BEAMS)]
    for g in range(4):
        for e in range(2):
            words = [
                x_ref[pl.ds(g * BLOCK + c * 2 + e, 8, stride=4 * BLOCK), :]
                for c in range(WIDE // LANES)
            ]
            step = jnp.broadcast_to(span_of(words[0][:, :1]) * (1.0 / TOP), (8, LANES))
            chunks = [unpair(word, step) for word in words]
            for b in range(BEAMS):
                row = jnp.concatenate([chunk[b] for chunk in chunks], axis=1)
                beams[b][g].append(row)
    return beams


def boxcar_bands(widths, places):
    u = lax.broadcasted_iota(jnp.int32, (2 * LANES, LANES), 0)
    t = lax.broadcasted_iota(jnp.int32, (2 * LANES, LANES), 1)
    ago = t + LANES - u
    bands = []
    for k in places:
        inside = jnp.logical_and(ago >= 0, ago < widths[:, k : k + 1])
        bands.append(jnp.where(inside, 1.0, 0.0).astype(jnp.bfloat16))
    return jnp.concatenate(bands, axis=1)


def boxcar_norm(width):
    return lax.rsqrt((width * (CHANS * PARTS)).astype(jnp.float32))


def final_kernel(widths, x_ref, out, one, two, held, sems):
    merge_rows(final_groups(x_ref), one, two, WIDE // LANES)
    rows = BEAMS * ROWS
    copies = []

    def send(k):
        copies.append(pltpu.make_async_copy(held.at[:, k], out.at[:, k], sems.at[k]))
        copies[-1].start()

    norm = boxcar_norm(widths[:, :1])
    for b in range(BEAMS):
        for c in range(PER):
            held[b, 0, :, pl.ds(c * LANES, LANES)] = two[b, c + 1] * norm
    send(0)
    parts = []
    for c in range(WIDE // LANES):
        tile = jnp.concatenate([two[b, c] for b in range(BEAMS)], axis=0)
        parts.append(split(tile))
    windows = [
        jnp.concatenate([before[0], here[0], before[1], here[1]], axis=1)
        for before, here in zip(parts, parts[1:])
    ]
    windows = jnp.concatenate(windows, axis=0)
    for places in ((1, 2), (3, 4), (5,)):
        bands = boxcar_bands(widths, places)
        bands = jnp.concatenate([bands, bands], axis=0)
        sums = jnp.dot(windows, bands, preferred_element_type=jnp.float32)
        for i, k in enumerate(places):
            norm = boxcar_norm(widths[:, k : k + 1])
            for c in range(PER):
                term = sums[rows * c : rows * (c + 1), i * LANES : (i + 1) * LANES]
                term = term * norm
                for b in range(BEAMS):
                    held[b, k, :, pl.ds(c * LANES, LANES)] = term[
                        b * ROWS : (b + 1) * ROWS
                    ]
            send(k)
    for copy in copies:
        copy.wait()


def final_boxcars(x, widths):
    return pl.pallas_call(
        final_kernel,
        in_specs=[pl.BlockSpec(memory_space=pltpu.VMEM)] * 2,
        out_specs=pl.BlockSpec(memory_space=pltpu.HBM),
        out_shape=jax.ShapeDtypeStruct((BEAMS, NBOX, ROWS, SPAN), jnp.float32),
        scratch_shapes=[
            pltpu.VMEM((BEAMS, WIDE // LANES, ROWS, LANES), jnp.float32),
            pltpu.VMEM((BEAMS, WIDE // LANES, ROWS, LANES), jnp.float32),
            pltpu.VMEM((BEAMS, NBOX, ROWS, SPAN), jnp.float32),
            pltpu.SemaphoreType.DMA((NBOX,)),
        ],
        compiler_params=pltpu.CompilerParams(vmem_limit_bytes=24 << 20),
        name="final_boxcars",
    )(widths.reshape(1, NBOX), x)


def later(block, distances):
    route = []
    for part, distance in enumerate(distances):
        if distance:
            for i in range(SEGMENTS - distance):
                sender = part * SEGMENTS + i
                route.append((sender, sender + distance))
    return lax.ppermute(block, ("chan", "tm"), route)


def per_device(intensity, channel_scale, box_widths):
    pieces = list(local_plane(intensity, channel_scale.reshape(1, CHANS)))
    for k in range(REACH - 1, 0, -1):
        pieces[k] = later(pieces[k], DISTANCES[::-1, k].tolist())
    lined = gather_shifted(pieces)
    lined = lined.reshape(PARTS, 1, BLOCK * LANES)
    lined = lax.all_to_all(lined, "chan", 0, 0, tiled=True)
    lined = lined.reshape(PARTS * BLOCK, LANES)
    return final_boxcars(lined, box_widths)


def solution(mesh):
    in_specs = (P(None, "chan", "tm"), P("chan"), P())
    out_specs = P(None, None, "chan", "tm")
    return jax.shard_map(
        per_device, mesh=mesh, in_specs=in_specs, out_specs=out_specs, check_vma=False
    )
```

```python
import jax
import jax.numpy as jnp
import numpy as np
from jax import lax
from jax.experimental import pallas as pl
from jax.experimental.pallas import tpu as pltpu
from jax.sharding import PartitionSpec as P

BEAMS = 2
CHANS = 512
SPAN = 512
PARTS = 32
SEGMENTS = 8
ROWS = 64
WIDE = SPAN + 128
NBOX = 6
LANES = 128
REACH = 6
TILES = 16
UNITS = 6
PLACES = UNITS + 4
PER = SPAN // LANES
FRONT = PER
BLOCK = 10
TOP = 32000.0


def tails(a):
    reach = [sum((i >> level) + 1 >> 1 for level in range(6)) for i in range(4 * a, 4 * a + 4)]
    return max(reach[:2]), max(reach[2:])


def tile_span(q, a):
    delay = 4 * q * a
    first, second = tails(a)
    within = delay & (LANES - 1)
    end = within + SPAN + (max if isinstance(q, int) else jnp.maximum)(first, 2 * q + second)
    tile = delay >> 7
    far = (tile & (PER - 1)) * LANES + end > 2 * SPAN - (2 * q + 63)
    return tile, (end + LANES - 1) >> 7, far


def group_shares(q, a, least=min):
    tile, number, far = tile_span(q, a)
    at = tile & (PER - 1)
    here = PER - at
    then = least(number - here, PER)
    over = number - here - then
    return tile >> 2, at, number, far, (here, 1 + then, over + far)


def packing():
    counts = np.zeros((PARTS, REACH), np.int32)
    for q in range(PARTS):
        for a in range(TILES):
            k, _, _, _, shares = group_shares(q, a)
            for i, share in enumerate(shares):
                if share:
                    counts[q, k + i] += share
    sizes = [64, 60, 38, 30, 16, 2]
    buffers = np.zeros((PARTS, REACH), np.int32)
    distances = np.zeros((PARTS, REACH), np.int32)
    for q in range(PARTS):
        taken = {0}
        for k in range(REACH - 1, 0, -1):
            if counts[q, k]:
                allowed = (k,) if q >= 22 or k == 3 else (4, 2, 1)
                fits = [i for i in allowed if i not in taken and sizes[i] >= counts[q, k]]
                buffers[q, k] = fits[0]
                distances[q, fits[0]] = k
                taken.add(fits[0])
    starts = [sum(sizes[:k]) for k in range(REACH)]
    return sizes, starts, sum(sizes), buffers, distances


SIZES, STARTS, SPARE, BUFFERS, DISTANCES = packing()


def first_slots(q, free):
    for k in range(REACH):
        slot = STARTS[BUFFERS[0, k]]
        for band in range(1, PARTS):
            if BUFFERS[band, k] != BUFFERS[band - 1, k]:
                slot = jnp.where(q >= band, STARTS[BUFFERS[band, k]], slot)
        free[k] = slot


def unit_slots(q, a, free):
    k, at, number, far, shares = group_shares(q, a, jnp.minimum)
    here = shares[0]
    p0, p1, p2 = free[k], free[k + 1], free[k + 2]
    free[k] = p0 + here
    free[k + 1] = p1 + shares[1]
    free[k + 2] = p2 + shares[2]
    slots = [p0]
    for i in range(1, PER):
        slots.append(jnp.where(i < here, p0 + i, p1 + 1 + i - here))
    slots.append(p1 + 1 + PER - here)
    last = jnp.where(here > 1, p1 + PER + 2 - here, p2 + 1)
    slots.append(jnp.where(number > PER + 1, last, SPARE))
    again = (p1, p0 + here - 1), (jnp.where(far, p2, SPARE), jnp.where(far, p1 + PER, SPARE))
    return slots, at, again


def split(x):
    first = x.astype(jnp.bfloat16)
    second = (x - first.astype(jnp.float32)).astype(jnp.bfloat16)
    return first, second


def exponent_of(largest):
    return jnp.floor(64.0 * jnp.log2(jnp.maximum(largest, 1e-36))).astype(jnp.int32) + 2


def largest_of(tiles):
    top = jnp.abs(tiles[0])
    for tile in tiles[1:]:
        top = jnp.maximum(top, jnp.abs(tile))
    top = jnp.max(jnp.max(top, axis=1, keepdims=True), axis=0, keepdims=True)
    return jnp.broadcast_to(top, (8, LANES))


def span_of(exponent):
    return jnp.exp2(exponent.astype(jnp.float32) * (1.0 / 64.0))


def code(x, inverse):
    return jnp.round(x * inverse * TOP).astype(jnp.int32)


def pair(high, low):
    return (high << 16) | (low & 0xFFFF)


def unpair(word, span):
    high = (word >> 16).astype(jnp.float32) * (1.0 / TOP) * span
    low = ((word << 16) >> 16).astype(jnp.float32) * (1.0 / TOP) * span
    return high, low


def roll(x, shift):
    return x if isinstance(shift, int) and shift == 0 else pltpu.roll(x, shift, 1)


def merge_groups(groups):
    merged = []
    for upper, lower in zip(groups[0::2], groups[1::2]):
        trials = []
        for e in range(len(upper)):
            trials += [lower[e] + roll(upper[e], e), lower[e] + roll(upper[e], e + 1)]
        merged.append(trials)
    return merged


def put(ref, start, stride, rows):
    for c in range(rows.shape[1] // LANES):
        ref[c, pl.ds(start, 8, stride=stride), :] = rows[:, c * LANES : (c + 1) * LANES]


def take(ref, start, count, first, last):
    chunks = [ref[c, pl.ds(start, count), :] for c in range(first, last)]
    return jnp.concatenate(chunks, axis=1)


def merge_rows(groups, one, two, tiles):
    while len(groups[0]) > 1:
        groups = [merge_groups(beam) for beam in groups]
    for e in range(8):
        for b, beam in enumerate(groups):
            put(one.at[b], e, 8, beam[0][e])
    source, target = one, two
    trials = 8
    while trials < ROWS:
        for base in range(0, ROWS, 2 * trials):
            for a in range(0, trials, 8):
                for b in range(BEAMS):
                    upper = take(source.at[b], base + a, 8, 0, tiles)
                    lower = take(source.at[b], base + trials + a, 8, 0, tiles)
                    early = pltpu.roll(upper, a, 1, stride=1, stride_axis=0)
                    late = pltpu.roll(upper, a + 1, 1, stride=1, stride_axis=0)
                    put(target.at[b], base + 2 * a, 2, lower + early)
                    put(target.at[b], base + 2 * a + 1, 2, lower + late)
        source, target = target, source
        trials *= 2


def local_kernel(
    scale_hbm,
    x_hbm,
    o0,
    o1,
    o2,
    o3,
    o4,
    o5,
    free,
    places,
    scale,
    x,
    one,
    two,
    packed,
    sems,
):
    half = CHANS // 2
    q = PARTS - 1 - lax.axis_index("chan")
    fetch_scale = pltpu.make_async_copy(scale_hbm, scale, sems.at[2 * BEAMS])
    fetch_scale.start()
    fetches = []
    for b in range(BEAMS):
        for h in range(2):
            piece = pl.ds(h * half, half)
            fetches.append(
                pltpu.make_async_copy(
                    x_hbm.at[b, piece], x.at[b, piece], sems.at[2 * b + h]
                )
            )
            fetches[-1].start()
    row = lax.broadcasted_iota(jnp.int32, (ROWS, CHANS), 0)
    col = lax.broadcasted_iota(jnp.int32, (ROWS, CHANS), 1)
    member = (row & 7) * 8 + (row >> 3) == col >> 3
    first_slots(q, free)
    for a in range(TILES):
        slots, _, again = unit_slots(q, a, free)
        for i, slot in enumerate(slots + [*again[0], *again[1]]):
            places[a * PLACES + i] = slot
    fetch_scale.wait()
    weights = jnp.where(member, scale[...], 0.0)
    weights = jnp.concatenate(split(weights), axis=0)
    blank = jnp.zeros((8, LANES), jnp.float32)
    groups = []
    for b in range(BEAMS):
        fetches[2 * b].wait()
        fetches[2 * b + 1].wait()
        base = jnp.dot(weights, x[b], preferred_element_type=jnp.float32)
        base = base[:ROWS] + base[ROWS:]
        groups.append(
            [
                [jnp.concatenate([base[8 * g : 8 * g + 8], blank], axis=1)]
                for g in range(8)
            ]
        )
    merge_rows(groups, one, two, WIDE // LANES)
    odd = lax.broadcasted_iota(jnp.int32, (8, UNITS * LANES), 0) & 2 != 0
    top = jnp.zeros((8, LANES), jnp.float32)
    for a in range(TILES):
        rows = [take(two.at[b], 4 * a, 4, 0, WIDE // LANES) for b in range(BEAMS)]
        rows = jnp.concatenate([jnp.concatenate(rows, axis=0), blank], axis=1)
        for c in range(WIDE // LANES):
            top = jnp.maximum(top, jnp.abs(rows[:, c * LANES : (c + 1) * LANES]))
        rows = jnp.where(odd, pltpu.roll(rows, 2 * q, 1), rows)
        rows = pltpu.roll(rows, (4 * q * a) & (LANES - 1), 1)
        place = a * PLACES
        for i in range(UNITS):
            packed[places[place + i]] = rows[:, i * LANES : (i + 1) * LANES]
        for i in (UNITS, UNITS + 2):
            packed[places[place + i]] = packed[places[place + i + 1]]
    o0[...] = packed[pl.ds(0, SIZES[0])]
    exponent = exponent_of(largest_of([top]))
    inverse = 1.0 / span_of(exponent)
    for k, out in enumerate((o1, o2, o3, o4, o5), 1):
        words = SIZES[k] // 2
        for t in range(words):
            slot = STARTS[k] + 2 * t
            high, low = code(packed[slot], inverse), code(packed[slot + 1], inverse)
            out[t] = pair(high, low)
        out[words] = exponent


def local_plane(x, scale):
    return pl.pallas_call(
        local_kernel,
        in_specs=[
            pl.BlockSpec(memory_space=pltpu.HBM),
            pl.BlockSpec(memory_space=pltpu.HBM),
        ],
        out_shape=[jax.ShapeDtypeStruct((SIZES[0], 8, LANES), jnp.float32)]
        + [jax.ShapeDtypeStruct((n // 2 + 1, 8, LANES), jnp.int32) for n in SIZES[1:]],
        scratch_shapes=[
            pltpu.SMEM((REACH + 2,), jnp.int32),
            pltpu.SMEM((TILES * PLACES,), jnp.int32),
            pltpu.VMEM((1, CHANS), jnp.float32),
            pltpu.VMEM((BEAMS, CHANS, SPAN), jnp.bfloat16),
            pltpu.VMEM((BEAMS, WIDE // LANES, ROWS, LANES), jnp.float32),
            pltpu.VMEM((BEAMS, WIDE // LANES, ROWS, LANES), jnp.float32),
            pltpu.VMEM((SPARE + 1, 8, LANES), jnp.float32),
            pltpu.SemaphoreType.DMA((2 * BEAMS + 1,)),
        ],
        compiler_params=pltpu.CompilerParams(vmem_limit_bytes=24 << 20),
        name="local_plane",
    )(
        pltpu.with_memory_space_constraint(scale, pltpu.HBM),
        pltpu.with_memory_space_constraint(x, pltpu.HBM),
    )


def gather_kernel(o0, r1, r2, r3, r4, r5, out, free, packed, held):
    q = PARTS - 1 - lax.axis_index("chan")
    tiles = WIDE // LANES
    first_slots(q, free)
    packed[pl.ds(FRONT, SIZES[0])] = o0[...]
    for k, piece in enumerate((r1, r2, r3, r4, r5), 1):
        words = SIZES[k] // 2
        span = span_of(piece[words])
        for t in range(words):
            slot = FRONT + STARTS[k] + 2 * t
            packed[slot], packed[slot + 1] = unpair(piece[t], span)
    top = jnp.zeros((8, LANES), jnp.float32)
    for a in range(TILES):
        k, at, _, _, (here, then, over) = group_shares(q, a, jnp.minimum)
        p0, p1, p2 = free[k], free[k + 1], free[k + 2]
        free[k] = p0 + here
        free[k + 1] = p1 + then
        free[k + 2] = p2 + over
        end = packed[pl.ds(FRONT + p0 - at, PER)]
        begin = packed[pl.ds(FRONT + p1, tiles)]
        more = packed[pl.ds(FRONT + p2, 2)]
        for c in range(tiles):
            tile = jnp.where(c < then, begin[c], 0.0)
            if c > 0:
                tile = tile + jnp.where(c > at, end[c - 1], 0.0)
            if c < 2:
                tile = tile + jnp.where(c < over, more[c], 0.0)
            held[c, pl.ds(8 * a, 8), :] = tile
            top = jnp.maximum(top, jnp.abs(tile))
    exponent = exponent_of(largest_of([top]))
    inverse = 1.0 / span_of(exponent)[:1]
    exponent = jnp.broadcast_to(exponent[:1], (TILES, LANES))
    lane = lax.broadcasted_iota(jnp.int32, (TILES, LANES), 1)
    for c in range(tiles):
        for r in range(4):
            high = code(held[c, pl.ds(r, TILES, stride=8), :], inverse)
            low = code(held[c, pl.ds(4 + r, TILES, stride=8), :], inverse)
            word = pair(high, low)
            if c == 0:
                word = jnp.where(lane == 0, exponent, word)
            rows = pl.ds((r >> 1) * BLOCK + c * 2 + (r & 1), TILES, stride=2 * BLOCK)
            out[rows, :] = word


def gather_shifted(pieces):
    vmem = pl.BlockSpec(memory_space=pltpu.VMEM)
    return pl.pallas_call(
        gather_kernel,
        in_specs=[vmem] * REACH,
        out_shape=jax.ShapeDtypeStruct((PARTS * BLOCK, LANES), jnp.int32),
        scratch_shapes=[
            pltpu.SMEM((REACH + 2,), jnp.int32),
            pltpu.VMEM((FRONT + SPARE + WIDE // LANES, 8, LANES), jnp.float32),
            pltpu.VMEM((WIDE // LANES, 8 * TILES, LANES), jnp.float32),
        ],
        compiler_params=pltpu.CompilerParams(vmem_limit_bytes=24 << 20),
        name="gather_shifted",
    )(*pieces)


def final_groups(x_ref):
    beams = [[[] for _ in range(4)] for _ in range(BEAMS)]
    for g in range(4):
        for e in range(2):
            words = [
                x_ref[pl.ds(g * BLOCK + c * 2 + e, 8, stride=4 * BLOCK), :]
                for c in range(WIDE // LANES)
            ]
            span = jnp.broadcast_to(span_of(words[0][:, :1]), (8, LANES))
            chunks = [unpair(word, span) for word in words]
            for b in range(BEAMS):
                row = jnp.concatenate([chunk[b] for chunk in chunks], axis=1)
                beams[b][g].append(row)
    return beams


def boxcar_bands(widths, places):
    u = lax.broadcasted_iota(jnp.int32, (2 * LANES, LANES), 0)
    t = lax.broadcasted_iota(jnp.int32, (2 * LANES, LANES), 1)
    ago = t + LANES - u
    bands = []
    for k in places:
        inside = jnp.logical_and(ago >= 0, ago < widths[:, k : k + 1])
        bands.append(jnp.where(inside, 1.0, 0.0).astype(jnp.bfloat16))
    return jnp.concatenate(bands, axis=1)


def boxcar_norm(width):
    return lax.rsqrt((width * (CHANS * PARTS)).astype(jnp.float32))


def final_kernel(widths, x_ref, out, one, two, held, sems):
    merge_rows(final_groups(x_ref), one, two, WIDE // LANES)
    rows = BEAMS * ROWS
    copies = []

    def send(k):
        copies.append(pltpu.make_async_copy(held.at[:, k], out.at[:, k], sems.at[k]))
        copies[-1].start()

    norm = boxcar_norm(widths[:, :1])
    for b in range(BEAMS):
        for c in range(PER):
            held[b, 0, :, pl.ds(c * LANES, LANES)] = two[b, c + 1] * norm
    send(0)
    parts = []
    for c in range(WIDE // LANES):
        tile = jnp.concatenate([two[b, c] for b in range(BEAMS)], axis=0)
        parts.append(split(tile))
    windows = [
        jnp.concatenate([before[0], here[0], before[1], here[1]], axis=1)
        for before, here in zip(parts, parts[1:])
    ]
    for places in ((1, 2), (3, 4), (5,)):
        bands = boxcar_bands(widths, places)
        bands = jnp.concatenate([bands, bands], axis=0)
        sums = [
            jnp.dot(window, bands, preferred_element_type=jnp.float32)
            for window in windows
        ]
        for i, k in enumerate(places):
            norm = boxcar_norm(widths[:, k : k + 1])
            for c in range(PER):
                term = sums[c][:, i * LANES : (i + 1) * LANES] * norm
                for b in range(BEAMS):
                    held[b, k, :, pl.ds(c * LANES, LANES)] = term[
                        b * ROWS : (b + 1) * ROWS
                    ]
            send(k)
    for copy in copies:
        copy.wait()


def final_boxcars(x, widths):
    return pl.pallas_call(
        final_kernel,
        in_specs=[pl.BlockSpec(memory_space=pltpu.VMEM)] * 2,
        out_specs=pl.BlockSpec(memory_space=pltpu.HBM),
        out_shape=jax.ShapeDtypeStruct((BEAMS, NBOX, ROWS, SPAN), jnp.float32),
        scratch_shapes=[
            pltpu.VMEM((BEAMS, WIDE // LANES, ROWS, LANES), jnp.float32),
            pltpu.VMEM((BEAMS, WIDE // LANES, ROWS, LANES), jnp.float32),
            pltpu.VMEM((BEAMS, NBOX, ROWS, SPAN), jnp.float32),
            pltpu.SemaphoreType.DMA((NBOX,)),
        ],
        compiler_params=pltpu.CompilerParams(vmem_limit_bytes=24 << 20),
        name="final_boxcars",
    )(widths.reshape(1, NBOX), x)


def later(block, distances):
    route = []
    for part, distance in enumerate(distances):
        if distance:
            for i in range(SEGMENTS - distance):
                sender = part * SEGMENTS + i
                route.append((sender, sender + distance))
    return lax.ppermute(block, ("chan", "tm"), route)


def per_device(intensity, channel_scale, box_widths):
    pieces = list(local_plane(intensity, channel_scale.reshape(1, CHANS)))
    for k in range(REACH - 1, 0, -1):
        pieces[k] = later(pieces[k], DISTANCES[::-1, k].tolist())
    lined = gather_shifted(pieces)
    lined = lined.reshape(PARTS, 1, BLOCK * LANES)
    lined = lax.all_to_all(lined, "chan", 0, 0, tiled=True)
    lined = lined.reshape(PARTS * BLOCK, LANES)
    return final_boxcars(lined, box_widths)


def solution(mesh):
    in_specs = (P(None, "chan", "tm"), P("chan"), P())
    out_specs = P(None, None, "chan", "tm")
    return jax.shard_map(
        per_device, mesh=mesh, in_specs=in_specs, out_specs=out_specs, check_vma=False
    )
```

```python
import jax
import jax.numpy as jnp
import numpy as np
from jax import lax
from jax.experimental import pallas as pl
from jax.experimental.pallas import tpu as pltpu
from jax.sharding import PartitionSpec as P

BEAMS = 2
CHANS = 512
SPAN = 512
PARTS = 32
SEGMENTS = 8
ROWS = 64
WIDE = SPAN + 128
NBOX = 6
LANES = 128
REACH = 6
TILES = 16
UNITS = 6
PLACES = UNITS + 4
PER = SPAN // LANES
FAR = 3
FRONT = PER
BLOCK = 10
TOP = 32000.0


def tails(a):
    reach = [sum((i >> level) + 1 >> 1 for level in range(6)) for i in range(4 * a, 4 * a + 4)]
    return max(reach[:2]), max(reach[2:])


def tile_span(q, a):
    delay = 4 * q * a
    first, second = tails(a)
    within = delay & (LANES - 1)
    end = within + SPAN + (max if isinstance(q, int) else jnp.maximum)(first, 2 * q + second)
    tile = delay >> 7
    far = (tile & (PER - 1)) * LANES + end > 2 * SPAN - (2 * q + 63)
    return tile, (end + LANES - 1) >> 7, far


def group_shares(q, a, least=min):
    tile, number, far = tile_span(q, a)
    at = tile & (PER - 1)
    here = PER - at
    then = least(number - here, PER)
    over = number - here - then
    return tile >> 2, at, number, far, (here, 1 + then, over + far)


def packing():
    counts = np.zeros((PARTS, REACH), np.int32)
    for q in range(PARTS):
        for a in range(TILES):
            k, _, _, _, shares = group_shares(q, a)
            for i, share in enumerate(shares):
                if share:
                    counts[q, k + i] += share
    sizes = [64, 60, 38, 30, 16, 2]
    buffers = np.zeros((PARTS, REACH), np.int32)
    distances = np.zeros((PARTS, REACH), np.int32)
    for q in range(PARTS):
        taken = {0}
        for k in range(REACH - 1, 0, -1):
            if counts[q, k]:
                allowed = (k,) if q >= 22 or k == 3 else (2, 1)
                fits = [i for i in allowed if i not in taken and sizes[i] >= counts[q, k]]
                buffers[q, k] = fits[0]
                distances[q, fits[0]] = k
                taken.add(fits[0])
    starts = [sum(sizes[:k]) for k in range(REACH)]
    return sizes, starts, sum(sizes), buffers, distances


SIZES, STARTS, SPARE, BUFFERS, DISTANCES = packing()


def first_slots(q, free):
    for k in range(REACH):
        slot = STARTS[BUFFERS[0, k]]
        for band in range(1, PARTS):
            if BUFFERS[band, k] != BUFFERS[band - 1, k]:
                slot = jnp.where(q >= band, STARTS[BUFFERS[band, k]], slot)
        free[k] = slot


def unit_slots(q, a, free):
    k, at, number, far, shares = group_shares(q, a, jnp.minimum)
    here = shares[0]
    p0, p1, p2 = free[k], free[k + 1], free[k + 2]
    free[k] = p0 + here
    free[k + 1] = p1 + shares[1]
    free[k + 2] = p2 + shares[2]
    slots = [p0]
    for i in range(1, PER):
        slots.append(jnp.where(i < here, p0 + i, p1 + 1 + i - here))
    slots.append(p1 + 1 + PER - here)
    last = jnp.where(here > 1, p1 + PER + 2 - here, p2 + 1)
    slots.append(jnp.where(number > PER + 1, last, SPARE))
    again = (p1, p0 + here - 1), (jnp.where(far, p2, SPARE), jnp.where(far, p1 + PER, SPARE))
    return slots, at, again


def split(x):
    first = x.astype(jnp.bfloat16)
    second = (x - first.astype(jnp.float32)).astype(jnp.bfloat16)
    return first, second


def exponent_of(largest):
    return jnp.floor(64.0 * jnp.log2(jnp.maximum(largest, 1e-36))).astype(jnp.int32) + 2


def largest_of(tiles):
    top = jnp.abs(tiles[0])
    for tile in tiles[1:]:
        top = jnp.maximum(top, jnp.abs(tile))
    top = jnp.max(jnp.max(top, axis=1, keepdims=True), axis=0, keepdims=True)
    return jnp.broadcast_to(top, (8, LANES))


def span_of(exponent):
    return jnp.exp2(exponent.astype(jnp.float32) * (1.0 / 64.0))


def code(x, inverse):
    return jnp.round(x * inverse * TOP).astype(jnp.int32)


def pair(high, low):
    return (high << 16) | (low & 0xFFFF)


def unpair(word, span):
    high = (word >> 16).astype(jnp.float32) * (1.0 / TOP) * span
    low = ((word << 16) >> 16).astype(jnp.float32) * (1.0 / TOP) * span
    return high, low


def roll(x, shift):
    return x if isinstance(shift, int) and shift == 0 else pltpu.roll(x, shift, 1)


def merge_groups(groups):
    merged = []
    for upper, lower in zip(groups[0::2], groups[1::2]):
        trials = []
        for e in range(len(upper)):
            trials += [lower[e] + roll(upper[e], e), lower[e] + roll(upper[e], e + 1)]
        merged.append(trials)
    return merged


def put(ref, start, stride, rows):
    for c in range(rows.shape[1] // LANES):
        ref[c, pl.ds(start, 8, stride=stride), :] = rows[:, c * LANES : (c + 1) * LANES]


def take(ref, start, count, first, last):
    chunks = [ref[c, pl.ds(start, count), :] for c in range(first, last)]
    return jnp.concatenate(chunks, axis=1)


def merge_rows(groups, one, two, tiles):
    while len(groups[0]) > 1:
        groups = [merge_groups(beam) for beam in groups]
    for e in range(8):
        for b, beam in enumerate(groups):
            put(one.at[b], e, 8, beam[0][e])
    source, target = one, two
    trials = 8
    while trials < ROWS:
        for base in range(0, ROWS, 2 * trials):
            for a in range(0, trials, 8):
                for b in range(BEAMS):
                    upper = take(source.at[b], base + a, 8, 0, tiles)
                    lower = take(source.at[b], base + trials + a, 8, 0, tiles)
                    early = pltpu.roll(upper, a, 1, stride=1, stride_axis=0)
                    late = pltpu.roll(upper, a + 1, 1, stride=1, stride_axis=0)
                    put(target.at[b], base + 2 * a, 2, lower + early)
                    put(target.at[b], base + 2 * a + 1, 2, lower + late)
        source, target = target, source
        trials *= 2


def local_kernel(
    scale_hbm,
    x_hbm,
    o0,
    o1,
    o2,
    o3,
    o4,
    o5,
    free,
    places,
    scale,
    x,
    one,
    two,
    packed,
    sems,
):
    half = CHANS // 2
    q = PARTS - 1 - lax.axis_index("chan")
    fetch_scale = pltpu.make_async_copy(scale_hbm, scale, sems.at[2 * BEAMS])
    fetch_scale.start()
    fetches = []
    for b in range(BEAMS):
        for h in range(2):
            piece = pl.ds(h * half, half)
            fetches.append(
                pltpu.make_async_copy(
                    x_hbm.at[b, piece], x.at[b, piece], sems.at[2 * b + h]
                )
            )
            fetches[-1].start()
    row = lax.broadcasted_iota(jnp.int32, (ROWS, CHANS), 0)
    col = lax.broadcasted_iota(jnp.int32, (ROWS, CHANS), 1)
    member = (row & 7) * 8 + (row >> 3) == col >> 3
    first_slots(q, free)
    for a in range(TILES):
        slots, _, again = unit_slots(q, a, free)
        for i, slot in enumerate(slots + [*again[0], *again[1]]):
            places[a * PLACES + i] = slot
    fetch_scale.wait()
    weights = jnp.where(member, scale[...], 0.0)
    weights = jnp.concatenate(split(weights), axis=0)
    blank = jnp.zeros((8, LANES), jnp.float32)
    groups = []
    for b in range(BEAMS):
        fetches[2 * b].wait()
        fetches[2 * b + 1].wait()
        base = jnp.dot(weights, x[b], preferred_element_type=jnp.float32)
        base = base[:ROWS] + base[ROWS:]
        groups.append(
            [
                [jnp.concatenate([base[8 * g : 8 * g + 8], blank], axis=1)]
                for g in range(8)
            ]
        )
    merge_rows(groups, one, two, WIDE // LANES)
    odd = lax.broadcasted_iota(jnp.int32, (8, UNITS * LANES), 0) & 2 != 0
    top = jnp.zeros((8, LANES), jnp.float32)
    for a in range(TILES):
        rows = [take(two.at[b], 4 * a, 4, 0, WIDE // LANES) for b in range(BEAMS)]
        rows = jnp.concatenate([jnp.concatenate(rows, axis=0), blank], axis=1)
        for c in range(WIDE // LANES):
            top = jnp.maximum(top, jnp.abs(rows[:, c * LANES : (c + 1) * LANES]))
        rows = jnp.where(odd, pltpu.roll(rows, 2 * q, 1), rows)
        rows = pltpu.roll(rows, (4 * q * a) & (LANES - 1), 1)
        place = a * PLACES
        for i in range(UNITS):
            packed[places[place + i]] = rows[:, i * LANES : (i + 1) * LANES]
        for i in (UNITS, UNITS + 2):
            packed[places[place + i]] = packed[places[place + i + 1]]
    o0[...] = packed[pl.ds(0, SIZES[0])]
    exponent = exponent_of(largest_of([top]))
    inverse = 1.0 / span_of(exponent)
    for k, out in enumerate((o1, o2, o3, o4, o5), 1):
        words = SIZES[k] // 2
        for t in range(words):
            slot = STARTS[k] + 2 * t
            high, low = code(packed[slot], inverse), code(packed[slot + 1], inverse)
            out[t] = pair(high, low)
        out[words] = exponent


def local_plane(x, scale):
    return pl.pallas_call(
        local_kernel,
        in_specs=[
            pl.BlockSpec(memory_space=pltpu.HBM),
            pl.BlockSpec(memory_space=pltpu.HBM),
        ],
        out_shape=[jax.ShapeDtypeStruct((SIZES[0], 8, LANES), jnp.float32)]
        + [jax.ShapeDtypeStruct((n // 2 + 1, 8, LANES), jnp.int32) for n in SIZES[1:]],
        scratch_shapes=[
            pltpu.SMEM((REACH + 2,), jnp.int32),
            pltpu.SMEM((TILES * PLACES,), jnp.int32),
            pltpu.VMEM((1, CHANS), jnp.float32),
            pltpu.VMEM((BEAMS, CHANS, SPAN), jnp.bfloat16),
            pltpu.VMEM((BEAMS, WIDE // LANES, ROWS, LANES), jnp.float32),
            pltpu.VMEM((BEAMS, WIDE // LANES, ROWS, LANES), jnp.float32),
            pltpu.VMEM((SPARE + 1, 8, LANES), jnp.float32),
            pltpu.SemaphoreType.DMA((2 * BEAMS + 1,)),
        ],
        compiler_params=pltpu.CompilerParams(vmem_limit_bytes=24 << 20),
        name="local_plane",
    )(
        pltpu.with_memory_space_constraint(scale, pltpu.HBM),
        pltpu.with_memory_space_constraint(x, pltpu.HBM),
    )


def unpack(pieces, first, packed):
    for k, piece in enumerate(pieces, first):
        words = SIZES[k] // 2
        span = span_of(piece[words])
        for t in range(words):
            slot = FRONT + STARTS[k] + 2 * t
            packed[slot], packed[slot + 1] = unpair(piece[t], span)


def window_tiles(q, a, free, packed, used):
    k, at, _, _, (here, then, over) = group_shares(q, a, jnp.minimum)
    p0, p1, p2 = free[k], free[k + 1], free[k + 2]
    free[k] = p0 + here
    free[k + 1] = p1 + then
    free[k + 2] = p2 + over
    end = packed[pl.ds(FRONT + p0 - at, PER)]
    begin = packed[pl.ds(FRONT + p1, WIDE // LANES)]
    more = packed[pl.ds(FRONT + p2, 2)]
    at = jnp.where(used(p0), at, PER)
    then = jnp.where(used(p1), then, 0)
    over = jnp.where(used(p2), over, 0)
    window = []
    for c in range(WIDE // LANES):
        tile = jnp.where(c < then, begin[c], 0.0)
        if c > 0:
            tile = tile + jnp.where(c > at, end[c - 1], 0.0)
        if c < 2:
            tile = tile + jnp.where(c < over, more[c], 0.0)
        window.append(tile)
    return window


def near_kernel(o0, r1, r2, held, free, packed):
    q = PARTS - 1 - lax.axis_index("chan")
    first_slots(q, free)
    packed[pl.ds(FRONT, SIZES[0])] = o0[...]
    unpack((r1, r2), 1, packed)
    for a in range(TILES):
        window = window_tiles(q, a, free, packed, lambda p: p < STARTS[FAR])
        for c, tile in enumerate(window):
            held[c, pl.ds(8 * a, 8), :] = tile


def far_kernel(near, r3, r4, r5, out, free, packed, held):
    q = PARTS - 1 - lax.axis_index("chan")
    tiles = WIDE // LANES
    first_slots(q, free)
    unpack((r3, r4, r5), FAR, packed)
    top = jnp.zeros((8, LANES), jnp.float32)
    for a in range(TILES):
        rows = pl.ds(8 * a, 8)
        window = [near[c, rows, :] for c in range(tiles)]
        if 4 * (PARTS - 1) * a >= SPAN:
            more = window_tiles(q, a, free, packed, lambda p: p >= STARTS[FAR])
            window = [tile + part for tile, part in zip(window, more)]
        for c, tile in enumerate(window):
            held[c, rows, :] = tile
            top = jnp.maximum(top, jnp.abs(tile))
    exponent = exponent_of(largest_of([top]))
    inverse = 1.0 / span_of(exponent)[:1]
    exponent = jnp.broadcast_to(exponent[:1], (TILES, LANES))
    lane = lax.broadcasted_iota(jnp.int32, (TILES, LANES), 1)
    for c in range(tiles):
        for r in range(4):
            high = code(held[c, pl.ds(r, TILES, stride=8), :], inverse)
            low = code(held[c, pl.ds(4 + r, TILES, stride=8), :], inverse)
            word = pair(high, low)
            if c == 0:
                word = jnp.where(lane == 0, exponent, word)
            rows = pl.ds((r >> 1) * BLOCK + c * 2 + (r & 1), TILES, stride=2 * BLOCK)
            out[rows, :] = word


def gather_shifted(pieces):
    vmem = pl.BlockSpec(memory_space=pltpu.VMEM)
    windows = (WIDE // LANES, 8 * TILES, LANES)
    slots = [
        pltpu.SMEM((REACH + 2,), jnp.int32),
        pltpu.VMEM((FRONT + SPARE + WIDE // LANES, 8, LANES), jnp.float32),
    ]
    params = pltpu.CompilerParams(vmem_limit_bytes=24 << 20)
    near = pl.pallas_call(
        near_kernel,
        in_specs=[vmem] * FAR,
        out_shape=jax.ShapeDtypeStruct(windows, jnp.float32),
        scratch_shapes=slots,
        compiler_params=params,
        cost_estimate=pl.CostEstimate(
            flops=1 << 22, bytes_accessed=4 << 20, transcendentals=0
        ),
        name="gather_near",
    )(*pieces[:FAR])
    return pl.pallas_call(
        far_kernel,
        in_specs=[vmem] * (1 + REACH - FAR),
        out_shape=jax.ShapeDtypeStruct((PARTS * BLOCK, LANES), jnp.int32),
        scratch_shapes=slots + [pltpu.VMEM(windows, jnp.float32)],
        compiler_params=params,
        name="gather_far",
    )(near, *pieces[FAR:])


def final_groups(x_ref):
    beams = [[[] for _ in range(4)] for _ in range(BEAMS)]
    for g in range(4):
        for e in range(2):
            words = [
                x_ref[pl.ds(g * BLOCK + c * 2 + e, 8, stride=4 * BLOCK), :]
                for c in range(WIDE // LANES)
            ]
            span = jnp.broadcast_to(span_of(words[0][:, :1]), (8, LANES))
            chunks = [unpair(word, span) for word in words]
            for b in range(BEAMS):
                row = jnp.concatenate([chunk[b] for chunk in chunks], axis=1)
                beams[b][g].append(row)
    return beams


def boxcar_bands(widths, places):
    u = lax.broadcasted_iota(jnp.int32, (2 * LANES, LANES), 0)
    t = lax.broadcasted_iota(jnp.int32, (2 * LANES, LANES), 1)
    ago = t + LANES - u
    bands = []
    for k in places:
        inside = jnp.logical_and(ago >= 0, ago < widths[:, k : k + 1])
        bands.append(jnp.where(inside, 1.0, 0.0).astype(jnp.bfloat16))
    return jnp.concatenate(bands, axis=1)


def boxcar_norm(width):
    return lax.rsqrt((width * (CHANS * PARTS)).astype(jnp.float32))


def final_kernel(widths, x_ref, out, one, two, held, sems):
    merge_rows(final_groups(x_ref), one, two, WIDE // LANES)
    rows = BEAMS * ROWS
    copies = []

    def send(k):
        copies.append(pltpu.make_async_copy(held.at[:, k], out.at[:, k], sems.at[k]))
        copies[-1].start()

    norm = boxcar_norm(widths[:, :1])
    for b in range(BEAMS):
        for c in range(PER):
            held[b, 0, :, pl.ds(c * LANES, LANES)] = two[b, c + 1] * norm
    send(0)
    parts = []
    for c in range(WIDE // LANES):
        tile = jnp.concatenate([two[b, c] for b in range(BEAMS)], axis=0)
        parts.append(split(tile))
    windows = [
        jnp.concatenate([before[0], here[0], before[1], here[1]], axis=1)
        for before, here in zip(parts, parts[1:])
    ]
    for places in ((1, 2), (3, 4), (5,)):
        bands = boxcar_bands(widths, places)
        bands = jnp.concatenate([bands, bands], axis=0)
        sums = [
            jnp.dot(window, bands, preferred_element_type=jnp.float32)
            for window in windows
        ]
        for i, k in enumerate(places):
            norm = boxcar_norm(widths[:, k : k + 1])
            for c in range(PER):
                term = sums[c][:, i * LANES : (i + 1) * LANES] * norm
                for b in range(BEAMS):
                    held[b, k, :, pl.ds(c * LANES, LANES)] = term[
                        b * ROWS : (b + 1) * ROWS
                    ]
            send(k)
    for copy in copies:
        copy.wait()


def final_boxcars(x, widths):
    return pl.pallas_call(
        final_kernel,
        in_specs=[pl.BlockSpec(memory_space=pltpu.VMEM)] * 2,
        out_specs=pl.BlockSpec(memory_space=pltpu.HBM),
        out_shape=jax.ShapeDtypeStruct((BEAMS, NBOX, ROWS, SPAN), jnp.float32),
        scratch_shapes=[
            pltpu.VMEM((BEAMS, WIDE // LANES, ROWS, LANES), jnp.float32),
            pltpu.VMEM((BEAMS, WIDE // LANES, ROWS, LANES), jnp.float32),
            pltpu.VMEM((BEAMS, NBOX, ROWS, SPAN), jnp.float32),
            pltpu.SemaphoreType.DMA((NBOX,)),
        ],
        compiler_params=pltpu.CompilerParams(vmem_limit_bytes=24 << 20),
        name="final_boxcars",
    )(widths.reshape(1, NBOX), x)


def later(block, distances):
    route = []
    for part, distance in enumerate(distances):
        if distance:
            for i in range(SEGMENTS - distance):
                sender = part * SEGMENTS + i
                route.append((sender, sender + distance))
    return lax.ppermute(block, ("chan", "tm"), route)


def per_device(intensity, channel_scale, box_widths):
    pieces = list(local_plane(intensity, channel_scale.reshape(1, CHANS)))
    for k in range(REACH - 1, 0, -1):
        pieces[k] = later(pieces[k], DISTANCES[::-1, k].tolist())
    lined = gather_shifted(pieces)
    lined = lined.reshape(PARTS, 1, BLOCK * LANES)
    lined = lax.all_to_all(lined, "chan", 0, 0, tiled=True)
    lined = lined.reshape(PARTS * BLOCK, LANES)
    return final_boxcars(lined, box_widths)


def solution(mesh):
    in_specs = (P(None, "chan", "tm"), P("chan"), P())
    out_specs = P(None, None, "chan", "tm")
    return jax.shard_map(
        per_device, mesh=mesh, in_specs=in_specs, out_specs=out_specs, check_vma=False
    )
```

```python
import jax
import jax.numpy as jnp
import numpy as np
from jax import lax
from jax.experimental import pallas as pl
from jax.experimental.pallas import tpu as pltpu
from jax.sharding import PartitionSpec as P

BEAMS = 2
CHANS = 512
SPAN = 512
PARTS = 32
SEGMENTS = 8
ROWS = 64
WIDE = SPAN + 128
NBOX = 6
LANES = 128
REACH = 6
TILES = 16
UNITS = 6
PLACES = UNITS + 4
PER = SPAN // LANES
FAR = 3
FRONT = PER
BLOCK = 10
TOP = 32000.0


def tails(a):
    reach = [sum((i >> level) + 1 >> 1 for level in range(6)) for i in range(4 * a, 4 * a + 4)]
    return max(reach[:2]), max(reach[2:])


def tile_span(q, a):
    delay = 4 * q * a
    first, second = tails(a)
    within = delay & (LANES - 1)
    end = within + SPAN + (max if isinstance(q, int) else jnp.maximum)(first, 2 * q + second)
    tile = delay >> 7
    far = (tile & (PER - 1)) * LANES + end > 2 * SPAN - (2 * q + 63)
    return tile, (end + LANES - 1) >> 7, far


def group_shares(q, a, least=min):
    tile, number, far = tile_span(q, a)
    at = tile & (PER - 1)
    here = PER - at
    then = least(number - here, PER)
    over = number - here - then
    return tile >> 2, at, number, far, (here, 1 + then, over + far)


def packing():
    counts = np.zeros((PARTS, REACH), np.int32)
    for q in range(PARTS):
        for a in range(TILES):
            k, _, _, _, shares = group_shares(q, a)
            for i, share in enumerate(shares):
                if share:
                    counts[q, k + i] += share
    sizes = [64, 60, 38, 30, 16, 2]
    buffers = np.zeros((PARTS, REACH), np.int32)
    distances = np.zeros((PARTS, REACH), np.int32)
    for q in range(PARTS):
        taken = {0}
        for k in range(REACH - 1, 0, -1):
            if counts[q, k]:
                allowed = (k,) if q >= 22 or k == 3 else (2, 1)
                fits = [i for i in allowed if i not in taken and sizes[i] >= counts[q, k]]
                buffers[q, k] = fits[0]
                distances[q, fits[0]] = k
                taken.add(fits[0])
    starts = [sum(sizes[:k]) for k in range(REACH)]
    return sizes, starts, sum(sizes), buffers, distances


SIZES, STARTS, SPARE, BUFFERS, DISTANCES = packing()


def first_slots(q, free):
    for k in range(REACH):
        slot = STARTS[BUFFERS[0, k]]
        for band in range(1, PARTS):
            if BUFFERS[band, k] != BUFFERS[band - 1, k]:
                slot = jnp.where(q >= band, STARTS[BUFFERS[band, k]], slot)
        free[k] = slot


def unit_slots(q, a, free):
    k, at, number, far, shares = group_shares(q, a, jnp.minimum)
    here = shares[0]
    p0, p1, p2 = free[k], free[k + 1], free[k + 2]
    free[k] = p0 + here
    free[k + 1] = p1 + shares[1]
    free[k + 2] = p2 + shares[2]
    slots = [p0]
    for i in range(1, PER):
        slots.append(jnp.where(i < here, p0 + i, p1 + 1 + i - here))
    slots.append(p1 + 1 + PER - here)
    last = jnp.where(here > 1, p1 + PER + 2 - here, p2 + 1)
    slots.append(jnp.where(number > PER + 1, last, SPARE))
    again = (p1, p0 + here - 1), (jnp.where(far, p2, SPARE), jnp.where(far, p1 + PER, SPARE))
    return slots, at, again


def split(x):
    first = x.astype(jnp.bfloat16)
    second = (x - first.astype(jnp.float32)).astype(jnp.bfloat16)
    return first, second


def exponent_of(largest):
    return jnp.floor(64.0 * jnp.log2(jnp.maximum(largest, 1e-36))).astype(jnp.int32) + 2


def largest_of(tiles):
    top = jnp.abs(tiles[0])
    for tile in tiles[1:]:
        top = jnp.maximum(top, jnp.abs(tile))
    top = jnp.max(jnp.max(top, axis=1, keepdims=True), axis=0, keepdims=True)
    return jnp.broadcast_to(top, (8, LANES))


def span_of(exponent):
    return jnp.exp2(exponent.astype(jnp.float32) * (1.0 / 64.0))


def code(x, inverse):
    return jnp.round(x * inverse * TOP).astype(jnp.int32)


def pair(high, low):
    return (high << 16) | (low & 0xFFFF)


def unpair(word, span):
    high = (word >> 16).astype(jnp.float32) * (1.0 / TOP) * span
    low = ((word << 16) >> 16).astype(jnp.float32) * (1.0 / TOP) * span
    return high, low


def roll(x, shift):
    return x if isinstance(shift, int) and shift == 0 else pltpu.roll(x, shift, 1)


def merge_groups(groups):
    merged = []
    for upper, lower in zip(groups[0::2], groups[1::2]):
        trials = []
        for e in range(len(upper)):
            trials += [lower[e] + roll(upper[e], e), lower[e] + roll(upper[e], e + 1)]
        merged.append(trials)
    return merged


def put(ref, start, stride, rows):
    for c in range(rows.shape[1] // LANES):
        ref[c, pl.ds(start, 8, stride=stride), :] = rows[:, c * LANES : (c + 1) * LANES]


def take(ref, start, count, first, last):
    chunks = [ref[c, pl.ds(start, count), :] for c in range(first, last)]
    return jnp.concatenate(chunks, axis=1)


def merge_rows(groups, one, two, tiles):
    while len(groups[0]) > 1:
        groups = [merge_groups(beam) for beam in groups]
    for e in range(8):
        for b, beam in enumerate(groups):
            put(one.at[b], e, 8, beam[0][e])
    source, target = one, two
    trials = 8
    while trials < ROWS:
        for base in range(0, ROWS, 2 * trials):
            for a in range(0, trials, 8):
                for b in range(BEAMS):
                    upper = take(source.at[b], base + a, 8, 0, tiles)
                    lower = take(source.at[b], base + trials + a, 8, 0, tiles)
                    early = pltpu.roll(upper, a, 1, stride=1, stride_axis=0)
                    late = pltpu.roll(upper, a + 1, 1, stride=1, stride_axis=0)
                    put(target.at[b], base + 2 * a, 2, lower + early)
                    put(target.at[b], base + 2 * a + 1, 2, lower + late)
        source, target = target, source
        trials *= 2


def local_kernel(
    scale_hbm,
    x_hbm,
    o0,
    o1,
    o2,
    o3,
    o4,
    o5,
    free,
    places,
    scale,
    x,
    one,
    two,
    packed,
    sems,
):
    half = CHANS // 2
    q = PARTS - 1 - lax.axis_index("chan")
    fetch_scale = pltpu.make_async_copy(scale_hbm, scale, sems.at[2 * BEAMS])
    fetch_scale.start()
    fetches = []
    for b in range(BEAMS):
        for h in range(2):
            piece = pl.ds(h * half, half)
            fetches.append(
                pltpu.make_async_copy(
                    x_hbm.at[b, piece], x.at[b, piece], sems.at[2 * b + h]
                )
            )
            fetches[-1].start()
    row = lax.broadcasted_iota(jnp.int32, (ROWS, CHANS), 0)
    col = lax.broadcasted_iota(jnp.int32, (ROWS, CHANS), 1)
    member = (row & 7) * 8 + (row >> 3) == col >> 3
    first_slots(q, free)
    for a in range(TILES):
        slots, _, again = unit_slots(q, a, free)
        for i, slot in enumerate(slots + [*again[0], *again[1]]):
            places[a * PLACES + i] = slot
    fetch_scale.wait()
    weights = jnp.where(member, scale[...], 0.0)
    weights = jnp.concatenate(split(weights), axis=0)
    blank = jnp.zeros((8, LANES), jnp.float32)
    groups = []
    for b in range(BEAMS):
        fetches[2 * b].wait()
        fetches[2 * b + 1].wait()
        base = jnp.dot(weights, x[b], preferred_element_type=jnp.float32)
        base = base[:ROWS] + base[ROWS:]
        groups.append(
            [
                [jnp.concatenate([base[8 * g : 8 * g + 8], blank], axis=1)]
                for g in range(8)
            ]
        )
    merge_rows(groups, one, two, WIDE // LANES)
    odd = lax.broadcasted_iota(jnp.int32, (8, UNITS * LANES), 0) & 2 != 0
    top = jnp.zeros((8, LANES), jnp.float32)
    for a in range(TILES):
        rows = [take(two.at[b], 4 * a, 4, 0, WIDE // LANES) for b in range(BEAMS)]
        rows = jnp.concatenate([jnp.concatenate(rows, axis=0), blank], axis=1)
        for c in range(WIDE // LANES):
            top = jnp.maximum(top, jnp.abs(rows[:, c * LANES : (c + 1) * LANES]))
        rows = jnp.where(odd, pltpu.roll(rows, 2 * q, 1), rows)
        rows = pltpu.roll(rows, (4 * q * a) & (LANES - 1), 1)
        place = a * PLACES
        for i in range(UNITS):
            packed[places[place + i]] = rows[:, i * LANES : (i + 1) * LANES]
        for i in (UNITS, UNITS + 2):
            packed[places[place + i]] = packed[places[place + i + 1]]
    o0[...] = packed[pl.ds(0, SIZES[0])]
    exponent = exponent_of(largest_of([top]))
    inverse = 1.0 / span_of(exponent)
    for k, out in enumerate((o1, o2, o3, o4, o5), 1):
        words = SIZES[k] // 2
        for t in range(words):
            slot = STARTS[k] + 2 * t
            high, low = code(packed[slot], inverse), code(packed[slot + 1], inverse)
            out[t] = pair(high, low)
        out[words] = exponent


def local_plane(x, scale):
    return pl.pallas_call(
        local_kernel,
        in_specs=[
            pl.BlockSpec(memory_space=pltpu.HBM),
            pl.BlockSpec(memory_space=pltpu.HBM),
        ],
        out_shape=[jax.ShapeDtypeStruct((SIZES[0], 8, LANES), jnp.float32)]
        + [jax.ShapeDtypeStruct((n // 2 + 1, 8, LANES), jnp.int32) for n in SIZES[1:]],
        scratch_shapes=[
            pltpu.SMEM((REACH + 2,), jnp.int32),
            pltpu.SMEM((TILES * PLACES,), jnp.int32),
            pltpu.VMEM((1, CHANS), jnp.float32),
            pltpu.VMEM((BEAMS, CHANS, SPAN), jnp.bfloat16),
            pltpu.VMEM((BEAMS, WIDE // LANES, ROWS, LANES), jnp.float32),
            pltpu.VMEM((BEAMS, WIDE // LANES, ROWS, LANES), jnp.float32),
            pltpu.VMEM((SPARE + 1, 8, LANES), jnp.float32),
            pltpu.SemaphoreType.DMA((2 * BEAMS + 1,)),
        ],
        compiler_params=pltpu.CompilerParams(vmem_limit_bytes=24 << 20),
        name="local_plane",
    )(
        pltpu.with_memory_space_constraint(scale, pltpu.HBM),
        pltpu.with_memory_space_constraint(x, pltpu.HBM),
    )


def unpack(pieces, first, packed):
    for k, piece in enumerate(pieces, first):
        words = SIZES[k] // 2
        span = span_of(piece[words])
        for t in range(words):
            slot = FRONT + STARTS[k] + 2 * t
            packed[slot], packed[slot + 1] = unpair(piece[t], span)


def window_tiles(q, a, free, packed, used, least=0):
    k, at, _, _, shares = group_shares(q, a, jnp.minimum)
    most = 4 * (PARTS - 1) * a // SPAN
    window = [None] * (WIDE // LANES)
    for i, (first, count) in enumerate(((1, PER), (0, WIDE // LANES), (0, 2))):
        if most + i < least:
            continue
        p = free[k + i]
        free[k + i] = p + shares[i]
        if i == 0:
            block = packed[pl.ds(FRONT + p - at, count)]
            after = jnp.where(used(p), at, PER)
        else:
            block = packed[pl.ds(FRONT + p, count)]
            before = jnp.where(used(p), shares[i], 0)
        for c in range(first, first + count):
            inside = c > after if i == 0 else c < before
            tile = jnp.where(inside, block[c - first], 0.0)
            window[c] = tile if window[c] is None else window[c] + tile
    return window


def near_kernel(o0, r1, r2, held, free, packed):
    q = PARTS - 1 - lax.axis_index("chan")
    first_slots(q, free)
    packed[pl.ds(FRONT, SIZES[0])] = o0[...]
    unpack((r1, r2), 1, packed)
    for a in range(TILES):
        window = window_tiles(q, a, free, packed, lambda p: p < STARTS[FAR])
        for c, tile in enumerate(window):
            held[c, pl.ds(8 * a, 8), :] = tile


def far_kernel(near, r3, r4, r5, out, free, packed, held):
    q = PARTS - 1 - lax.axis_index("chan")
    tiles = WIDE // LANES
    first_slots(q, free)
    unpack((r3, r4, r5), FAR, packed)
    top = jnp.zeros((8, LANES), jnp.float32)
    for a in range(TILES):
        rows = pl.ds(8 * a, 8)
        window = [near[c, rows, :] for c in range(tiles)]
        if 4 * (PARTS - 1) * a >= SPAN:
            more = window_tiles(q, a, free, packed, lambda p: p >= STARTS[FAR], FAR)
            window = [
                tile if part is None else tile + part
                for tile, part in zip(window, more)
            ]
        for c, tile in enumerate(window):
            held[c, rows, :] = tile
            top = jnp.maximum(top, jnp.abs(tile))
    exponent = exponent_of(largest_of([top]))
    inverse = 1.0 / span_of(exponent)[:1]
    exponent = jnp.broadcast_to(exponent[:1], (TILES, LANES))
    lane = lax.broadcasted_iota(jnp.int32, (TILES, LANES), 1)
    for c in range(tiles):
        for r in range(4):
            high = code(held[c, pl.ds(r, TILES, stride=8), :], inverse)
            low = code(held[c, pl.ds(4 + r, TILES, stride=8), :], inverse)
            word = pair(high, low)
            if c == 0:
                word = jnp.where(lane == 0, exponent, word)
            rows = pl.ds((r >> 1) * BLOCK + c * 2 + (r & 1), TILES, stride=2 * BLOCK)
            out[rows, :] = word


def gather_shifted(pieces):
    vmem = pl.BlockSpec(memory_space=pltpu.VMEM)
    windows = (WIDE // LANES, 8 * TILES, LANES)
    slots = [
        pltpu.SMEM((REACH + 2,), jnp.int32),
        pltpu.VMEM((FRONT + SPARE + WIDE // LANES, 8, LANES), jnp.float32),
    ]
    params = pltpu.CompilerParams(vmem_limit_bytes=24 << 20)
    near = pl.pallas_call(
        near_kernel,
        in_specs=[vmem] * FAR,
        out_shape=jax.ShapeDtypeStruct(windows, jnp.float32),
        scratch_shapes=slots,
        compiler_params=params,
        cost_estimate=pl.CostEstimate(
            flops=1 << 22, bytes_accessed=4 << 20, transcendentals=0
        ),
        name="gather_near",
    )(*pieces[:FAR])
    return pl.pallas_call(
        far_kernel,
        in_specs=[vmem] * (1 + REACH - FAR),
        out_shape=jax.ShapeDtypeStruct((PARTS * BLOCK, LANES), jnp.int32),
        scratch_shapes=slots + [pltpu.VMEM(windows, jnp.float32)],
        compiler_params=params,
        name="gather_far",
    )(near, *pieces[FAR:])


def final_groups(x_ref):
    beams = [[[] for _ in range(4)] for _ in range(BEAMS)]
    for g in range(4):
        for e in range(2):
            words = [
                x_ref[pl.ds(g * BLOCK + c * 2 + e, 8, stride=4 * BLOCK), :]
                for c in range(WIDE // LANES)
            ]
            span = jnp.broadcast_to(span_of(words[0][:, :1]), (8, LANES))
            chunks = [unpair(word, span) for word in words]
            for b in range(BEAMS):
                row = jnp.concatenate([chunk[b] for chunk in chunks], axis=1)
                beams[b][g].append(row)
    return beams


def boxcar_bands(widths, places):
    u = lax.broadcasted_iota(jnp.int32, (2 * LANES, LANES), 0)
    t = lax.broadcasted_iota(jnp.int32, (2 * LANES, LANES), 1)
    ago = t + LANES - u
    bands = []
    for k in places:
        inside = jnp.logical_and(ago >= 0, ago < widths[:, k : k + 1])
        bands.append(jnp.where(inside, 1.0, 0.0).astype(jnp.bfloat16))
    return jnp.concatenate(bands, axis=1)


def boxcar_norm(width):
    return lax.rsqrt((width * (CHANS * PARTS)).astype(jnp.float32))


def final_kernel(widths, x_ref, out, one, two, held, sems):
    merge_rows(final_groups(x_ref), one, two, WIDE // LANES)
    rows = BEAMS * ROWS
    copies = []

    def send(k):
        copies.append(pltpu.make_async_copy(held.at[:, k], out.at[:, k], sems.at[k]))
        copies[-1].start()

    norm = boxcar_norm(widths[:, :1])
    for b in range(BEAMS):
        for c in range(PER):
            held[b, 0, :, pl.ds(c * LANES, LANES)] = two[b, c + 1] * norm
    send(0)
    parts = []
    for c in range(WIDE // LANES):
        tile = jnp.concatenate([two[b, c] for b in range(BEAMS)], axis=0)
        parts.append(split(tile))
    windows = [
        jnp.concatenate([before[0], here[0], before[1], here[1]], axis=1)
        for before, here in zip(parts, parts[1:])
    ]
    for places in ((1, 2), (3, 4), (5,)):
        bands = boxcar_bands(widths, places)
        bands = jnp.concatenate([bands, bands], axis=0)
        sums = [
            jnp.dot(window, bands, preferred_element_type=jnp.float32)
            for window in windows
        ]
        for i, k in enumerate(places):
            norm = boxcar_norm(widths[:, k : k + 1])
            for c in range(PER):
                term = sums[c][:, i * LANES : (i + 1) * LANES] * norm
                for b in range(BEAMS):
                    held[b, k, :, pl.ds(c * LANES, LANES)] = term[
                        b * ROWS : (b + 1) * ROWS
                    ]
            send(k)
    for copy in copies:
        copy.wait()


def final_boxcars(x, widths):
    return pl.pallas_call(
        final_kernel,
        in_specs=[pl.BlockSpec(memory_space=pltpu.VMEM)] * 2,
        out_specs=pl.BlockSpec(memory_space=pltpu.HBM),
        out_shape=jax.ShapeDtypeStruct((BEAMS, NBOX, ROWS, SPAN), jnp.float32),
        scratch_shapes=[
            pltpu.VMEM((BEAMS, WIDE // LANES, ROWS, LANES), jnp.float32),
            pltpu.VMEM((BEAMS, WIDE // LANES, ROWS, LANES), jnp.float32),
            pltpu.VMEM((BEAMS, NBOX, ROWS, SPAN), jnp.float32),
            pltpu.SemaphoreType.DMA((NBOX,)),
        ],
        compiler_params=pltpu.CompilerParams(vmem_limit_bytes=24 << 20),
        name="final_boxcars",
    )(widths.reshape(1, NBOX), x)


def later(block, distances):
    route = []
    for part, distance in enumerate(distances):
        if distance:
            for i in range(SEGMENTS - distance):
                sender = part * SEGMENTS + i
                route.append((sender, sender + distance))
    return lax.ppermute(block, ("chan", "tm"), route)


def per_device(intensity, channel_scale, box_widths):
    pieces = list(local_plane(intensity, channel_scale.reshape(1, CHANS)))
    for k in range(REACH - 1, 0, -1):
        pieces[k] = later(pieces[k], DISTANCES[::-1, k].tolist())
    lined = gather_shifted(pieces)
    lined = lined.reshape(PARTS, 1, BLOCK * LANES)
    lined = lax.all_to_all(lined, "chan", 0, 0, tiled=True)
    lined = lined.reshape(PARTS * BLOCK, LANES)
    return final_boxcars(lined, box_widths)


def solution(mesh):
    in_specs = (P(None, "chan", "tm"), P("chan"), P())
    out_specs = P(None, None, "chan", "tm")
    return jax.shard_map(
        per_device, mesh=mesh, in_specs=in_specs, out_specs=out_specs, check_vma=False
    )
```
